32 devices in a mesh: wide: 16 (over z, y, x), narrow: 2 (over core).
Axes of the slice: x: 2, y: 2, z: 4, core: 2. Of those that a mesh axis runs over, the one named last changes fastest.
Arguments:
- tokens: bfloat16 [32, 1024, 576], P('wide', 'narrow'), may hold values from -6 to 6
- doc_starts: int32 [32, 8], P('wide'), may hold values from 0 to 1023, as said below
- skip_flags: int32 [32], P('wide'), may hold values 0 or 1
- cotangent: bfloat16 [32, 1024, 576], P('wide', 'narrow'), may hold values from -6 to 6
- attn_gain: bfloat16 [576], replicated, may hold values from 0.25 to 1.75
- w_query: bfloat16 [576, 576], replicated, may hold values from -0.25 to 0.25
- w_key: bfloat16 [576, 192], replicated, may hold values from -0.25 to 0.25
- w_value: bfloat16 [576, 192], replicated, may hold values from -0.25 to 0.25
- w_out: bfloat16 [576, 576], replicated, may hold values from -1.5 to 1.5
- mlp_gain: bfloat16 [576], replicated, may hold values from 0.25 to 1.75
- w_gate: bfloat16 [576, 1536], replicated, may hold values from -0.25 to 0.25
- w_up: bfloat16 [576, 1536], replicated, may hold values from -0.25 to 0.25
- w_down: bfloat16 [1536, 576], replicated, may hold values from -0.15625 to 0.15625
Outputs:
- mixed_out: bfloat16 [32, 1024, 576], P('wide', 'narrow')
- grad_tokens: bfloat16 [32, 1024, 576], P('wide', 'narrow')
- grad_attn_gain: float32 [576], replicated
- grad_w_query: float32 [576, 576], replicated
- grad_w_key: float32 [576, 192], replicated
- grad_w_value: float32 [576, 192], replicated
- grad_w_out: float32 [576, 576], replicated
- grad_mlp_gain: float32 [576], replicated
- grad_w_gate: float32 [576, 1536], replicated
- grad_w_up: float32 [576, 1536], replicated
- grad_w_down: float32 [1536, 576], replicated
The draws below stay inside these ranges and needn't reach their ends.
Inputs may be any that keep to these rules, and one draw needn't show every extreme that they name: `doc_starts`: each row starts with 0, rises strictly and ends with 1023; no document begins at a position from 384 to 639.
All inputs are finite; a program needn't handle non-finite values. No bound on the sum of `skip_flags` on one device may be relied on, other than what follows from the above.
Results may differ from the reference program's by a relative error of at most 0.014.
Values may be sent and summed in bfloat16 or wider, within the bound.
No kernel may reach another device: no remote copies, remote signals or barrier semaphores. Data moves between devices by JAX's collectives and lax.ppermute only.
A program may use at most 192 MiB of HBM per device.

```python
import jax
import jax.numpy as jnp
from jax import lax

D = 576
HQ = 9
KVH = 3
HD = 64
FF = 1536
SEQ = 1024
NDOC = 8
SAMPLES = 32


def draw_doc_starts(key, part):
    key = jax.random.fold_in(key, 7)
    spots = jnp.arange(1, SEQ, dtype=jnp.int32)
    barred = (spots >= 3 * SEQ // 8) & (spots < 5 * SEQ // 8) | (spots == SEQ - 1)
    scores = jax.random.randint(key, (SAMPLES, SEQ - 1), 0, 128, dtype=jnp.int32) * spots[None, :]
    scores = jnp.where(barred[None, :], jnp.int32(2147483647), scores)
    chosen = jnp.argsort(scores, axis=1, stable=True)[:, :NDOC - 2]
    picked = jnp.sort(spots[chosen], axis=1)
    first = jnp.zeros((SAMPLES, 1), jnp.int32)
    final = jnp.full((SAMPLES, 1), SEQ - 1, jnp.int32)
    return jnp.concatenate([first, picked, final], 1)


def place_ends(array, own_key, least, top_value):
    index_at = [jax.random.randint(jax.random.fold_in(own_key, axis), (), 0, length) for axis, length in enumerate(array.shape)]
    longest = array.shape.index(max(array.shape))
    next_to = index_at[:longest] + [(index_at[longest] + 1) % array.shape[longest]] + index_at[longest + 1:]
    return array.at[tuple(index_at)].set(least).at[tuple(next_to)].set(top_value)


def block_levels(stream_key, dims, pieces, low, high):
    def one(position, parts):
        heights = jax.random.uniform(jax.random.fold_in(jax.random.fold_in(stream_key, 6), position), (parts,), jnp.float32, low / len(pieces), high / len(pieces))
        return jnp.repeat(jnp.exp(heights), dims[position] // parts).reshape((-1,) + (1,) * (len(dims) - position - 1))

    gain = one(*pieces[0])
    for cut in pieces[1:]:
        gain = gain * one(*cut)
    return gain


def gaussian(key, shape, spread, most, pieces=(), held_as=jnp.bfloat16):
    loudness = block_levels(key, shape, pieces, -0.22, 0.18) if pieces else 1.0
    entries = jax.random.normal(key, shape, jnp.float32) * spread * loudness
    return jnp.minimum(jnp.maximum(entries, -most), most).astype(held_as)


def setup_inputs(seed: int = 0) -> dict:
    key_list = jax.random.split(jax.random.key(seed), 14)
    return {
        "tokens": gaussian(key_list[0], (SAMPLES, SEQ, D), 1.0, 6.0, ((0, 16), (1, 2))),
        "doc_starts": draw_doc_starts(jax.random.fold_in(key_list[13], 71), 0),
        "skip_flags": place_ends((jax.random.randint(key_list[2], (SAMPLES,), 0, 2) < 1).astype(jnp.int32), jax.random.fold_in(key_list[2], 1), 0, 1),
        "cotangent": gaussian(key_list[3], (SAMPLES, SEQ, D), 1.0, 6.0, ((0, 16), (1, 2))),
        "attn_gain": jnp.clip(1.0 + 0.15 * jax.random.normal(key_list[4], (D,), jnp.float32), 0.25, 1.75).astype(jnp.bfloat16),
        "w_query": gaussian(key_list[5], (D, HQ * HD), D ** -0.5, 0.25),
        "w_key": gaussian(key_list[6], (D, KVH * HD), D ** -0.5, 0.25),
        "w_value": gaussian(key_list[7], (D, KVH * HD), D ** -0.5, 0.25),
        "w_out": gaussian(key_list[8], (HQ * HD, D), (HQ * HD // 32) ** -0.5, 1.5),
        "mlp_gain": jnp.clip(1.0 + 0.15 * jax.random.normal(key_list[9], (D,), jnp.float32), 0.25, 1.75).astype(jnp.bfloat16),
        "w_gate": gaussian(key_list[10], (D, FF), D ** -0.5, 0.25),
        "w_up": gaussian(key_list[11], (D, FF), D ** -0.5, 0.25),
        "w_down": gaussian(key_list[12], (FF, D), FF ** -0.5, 0.15625),
    }


@jax.custom_vjp
def low(v):
    return lax.optimization_barrier(v.astype(jnp.bfloat16)).astype(jnp.float32)

@jax.custom_vjp
def low_back(v):
    return v

def low_keep(v):
    return (low(v), None)

def low_pass(kept, grad):
    return (grad,)

def back_keep(v):
    return (v, None)

def back_low(kept, grad):
    return (low(grad),)
low.defvjp(low_keep, low_pass)
low_back.defvjp(back_keep, back_low)
theta_base = 100000.0
eps_norm = 1e-05
masked_score = -1e+30
highest = lax.Precision.HIGHEST

def rms_scale(inputs, gain_vec):
    return inputs * lax.rsqrt(lax.optimization_barrier(jnp.mean(inputs * inputs, -1, keepdims=True)) + eps_norm) * gain_vec

def rotary(field, positions):
    half_width = field.shape[-1] // 2
    frequency = theta_base ** (-2.0 * jnp.arange(half_width, dtype=jnp.float32) / field.shape[-1])
    angles = positions.astype(jnp.float32)[:, None] * frequency[None, :]
    cosine = jnp.concatenate([jnp.cos(angles), jnp.cos(angles)], -1)[:, None, :]
    sine_tab = jnp.concatenate([jnp.sin(angles), jnp.sin(angles)], -1)[:, None, :]
    turned = jnp.concatenate([-field[..., half_width:], field[..., :half_width]], -1)
    return field * cosine + turned * sine_tab

def sample_layer(params, sample_rows, starts, flag):
    gain_one, w_query, w_key, w_value, w_out, gain_two, w_gate, w_up, w_down = params
    length = sample_rows.shape[0]
    positions = jnp.arange(length, dtype=jnp.int32)
    documents = lax.optimization_barrier(jnp.sum((starts[None, :] <= positions[:, None]).astype(jnp.int32), -1))
    allowed = (positions[None, :] <= positions[:, None]) & (documents[None, :] == documents[:, None])
    normed = low(rms_scale(sample_rows, gain_one))
    queries = low_back(jnp.dot(normed, w_query, precision=highest))
    keyset = low_back(jnp.dot(normed, w_key, precision=highest))
    valueset = low(low_back(jnp.dot(normed, w_value, precision=highest)))
    queries = low(rotary(queries.reshape(length, HQ, HD), positions)).reshape(length, KVH, HQ // KVH, HD)
    keyset = low(rotary(keyset.reshape(length, KVH, HD), positions))
    valueset = valueset.reshape(length, KVH, HD)
    scores = low_back(jnp.einsum('skgd,tkd->kgst', queries, keyset, precision=highest)) * HD ** (-0.5)
    scores = jnp.where(allowed[None, None], scores, masked_score)
    peak_score = lax.optimization_barrier(jnp.max(scores, -1, keepdims=True))
    exponent = jnp.exp(scores - peak_score)
    soft_weights = low(exponent / lax.optimization_barrier(jnp.sum(exponent, -1, keepdims=True)))
    mixed_heads = jnp.einsum('kgst,tkd->skgd', soft_weights, valueset, precision=highest).reshape(length, HQ * HD)
    mixed_heads = low(low_back(mixed_heads))
    hidden_state = sample_rows + low_back(jnp.dot(mixed_heads, w_out, precision=highest))
    normed_two = low(rms_scale(hidden_state, gain_two))
    gate_proj = low_back(jnp.dot(normed_two, w_gate, precision=highest))
    up_proj = low_back(jnp.dot(normed_two, w_up, precision=highest))
    inner_act = low(gate_proj * jax.nn.sigmoid(gate_proj) * up_proj)
    result = hidden_state + low_back(jnp.dot(inner_act, w_down, precision=highest))
    return jnp.where(flag == 1, sample_rows, result)

def reference(tokens, doc_starts, skip_flags, cotangent, attn_gain, w_query, w_key, w_value, w_out, mlp_gain, w_gate, w_up, w_down):
    weights = tuple((parameter.astype(jnp.float32) for parameter in (attn_gain, w_query, w_key, w_value, w_out, mlp_gain, w_gate, w_up, w_down)))
    layer_step = jax.checkpoint(sample_layer)

    def forward(inputs, params):

        def scan_step(carried, element):
            return (carried, layer_step(params, element[0], element[1], element[2]))
        return lax.scan(scan_step, jnp.float32(0.0), (inputs, doc_starts, skip_flags))[1]
    outputs, pullback = jax.vjp(forward, tokens.astype(jnp.float32), weights)
    grad_inputs, grad_params = pullback(cotangent.astype(jnp.float32))
    return (outputs.astype(jnp.bfloat16), grad_inputs.astype(jnp.bfloat16), grad_params[0], grad_params[1], grad_params[2], grad_params[3], grad_params[4], grad_params[5], grad_params[6], grad_params[7], grad_params[8])
```

```python
import jax
import jax.numpy as jnp
from jax import lax
from jax.sharding import PartitionSpec as P

HQ = 9
KVH = 3
HD = 64


theta_base = 100000.0
eps_norm = 1e-05
masked_score = -1e30


def normalize(inputs, gain_vec):
    inverse = lax.rsqrt(jnp.mean(inputs * inputs, -1, keepdims=True) + eps_norm)
    return (inputs * inverse * gain_vec, inverse)


def norm_back(gradient, inputs, inverse, gain_vec):
    scaled = gradient * gain_vec
    gain_grad = jnp.sum(gradient * inputs * inverse, 0)
    input_grad = inverse * scaled - inputs * inverse * inverse * inverse * jnp.mean(
        scaled * inputs, -1, keepdims=True
    )
    return (input_grad, gain_grad)


def rotary_tables(positions):
    half_width = HD // 2
    frequency = theta_base ** (-2.0 * jnp.arange(half_width, dtype=jnp.float32) / HD)
    angles = positions.astype(jnp.float32)[:, None] * frequency[None, :]
    cosine = jnp.concatenate([jnp.cos(angles), jnp.cos(angles)], -1)[:, None, :]
    sine_tab = jnp.concatenate([jnp.sin(angles), jnp.sin(angles)], -1)[:, None, :]
    return (cosine, sine_tab)


def rotate_forward(field, cosine, sine_tab):
    half_width = field.shape[-1] // 2
    turned = jnp.concatenate([-field[..., half_width:], field[..., :half_width]], -1)
    return field * cosine + turned * sine_tab


def rotate_back(gradient, cosine, sine_tab):
    half_width = gradient.shape[-1] // 2
    scaled = gradient * sine_tab
    return gradient * cosine + jnp.concatenate(
        [scaled[..., half_width:], -scaled[..., :half_width]], -1
    )


def doc_index(positions, starts):
    return jnp.sum((starts[None, :] <= positions[:, None]).astype(jnp.int32), -1)


def block_scores(query_block, keys_three, allowed_block, score_scale):
    scores = (
        jnp.einsum("bkgd,tkd->kgbt", query_block, keys_three, preferred_element_type=jnp.float32)
        * score_scale
    )
    return jnp.where(allowed_block[None, None], scores, masked_score)


def axis_orders(bits):
    if bits == 4:
        return ((0, 1, 2, 3), (1, 2, 3, 0), (2, 0, 1, 3))
    base = tuple(range(bits))
    return tuple((base[turn:] + base[:turn] for turn in range(0, bits, max(1, bits // 3))))[:3]


def swap_bit(array, bit, count):
    return lax.ppermute(array, "wide", [(i, i ^ (1 << bit)) for i in range(count)])


def sum_over_chips(pieces, count):
    bits = count.bit_length() - 1
    orders = axis_orders(bits)
    place = lax.axis_index("wide")
    current = list(pieces)
    for step in range(bits):
        arrived = []
        kept = []
        for piece, order in zip(current, orders):
            mine = (place >> order[step]) & 1
            half = piece.shape[0] // 2
            kept.append(lax.dynamic_slice_in_dim(piece, mine * half, half, 0))
            out = lax.dynamic_slice_in_dim(piece, (1 - mine) * half, half, 0)
            arrived.append(swap_bit(out, order[step], count))
        current = [
            (a.astype(jnp.float32) + b.astype(jnp.float32)).astype(jnp.bfloat16)
            for a, b in zip(kept, arrived)
        ]
    for step in reversed(range(bits)):
        arrived = [swap_bit(p, order[step], count) for p, order in zip(current, orders)]
        following = []
        for piece, other, order in zip(current, arrived, orders):
            mine = (place >> order[step]) & 1
            following.append(
                jnp.where(
                    mine == 0,
                    jnp.concatenate([piece, other], 0),
                    jnp.concatenate([other, piece], 0),
                )
            )
        current = following
    return current


def swap_core(array):
    return lax.ppermute(array, "narrow", [(0, 1), (1, 0)])


def sum_everywhere(flat, count):
    core = lax.axis_index("narrow")
    half = flat.shape[0] // 2
    kept = lax.dynamic_slice_in_dim(flat, core * half, half, 0)
    out = lax.dynamic_slice_in_dim(flat, (1 - core) * half, half, 0)
    own = (kept.astype(jnp.float32) + swap_core(out).astype(jnp.float32)).astype(jnp.bfloat16)
    third = half // 3
    own = jnp.concatenate(
        sum_over_chips([own[:third], own[third : 2 * third], own[2 * third :]], count), 0
    )
    other = swap_core(own)
    return jnp.where(
        core == 0, jnp.concatenate([own, other], 0), jnp.concatenate([other, own], 0)
    )


def whole_sample(halves):
    core = lax.axis_index("narrow")
    own = lax.dynamic_index_in_dim(halves, core, 0, keepdims=False)
    other = swap_core(lax.dynamic_index_in_dim(halves, 1 - core, 0, keepdims=False))
    return jnp.where(core == 0, jnp.concatenate([own, other], 0), jnp.concatenate([other, own], 0))


def back_to_halves(sample):
    core = lax.axis_index("narrow")
    rows = sample.shape[0] // 2
    own = lax.dynamic_slice_in_dim(sample, core * rows, rows, 0)
    other = swap_core(lax.dynamic_slice_in_dim(sample, (1 - core) * rows, rows, 0))
    return jnp.where(core == 0, jnp.stack([own, other]), jnp.stack([other, own]))


def per_device(
    tokens,
    doc_starts,
    skip_flags,
    cotangent,
    attn_gain,
    w_query,
    w_key,
    w_value,
    w_out,
    mlp_gain,
    w_gate,
    w_up,
    w_down,
):
    core = lax.axis_index("narrow")
    tokens = whole_sample(tokens)[None]
    cotangent = whole_sample(cotangent)[None]
    doc_starts = lax.dynamic_slice_in_dim(doc_starts, core, 1, 0)
    skip_flags = lax.dynamic_slice_in_dim(skip_flags, core, 1, 0)
    micro_count = tokens.shape[0]
    rows_dev = tokens.shape[1]
    groups = HQ // KVH
    score_scale = HD ** (-0.5)
    block_rows = rows_dev
    query_pos = jnp.arange(rows_dev, dtype=jnp.int32)
    query_cos, query_sin = rotary_tables(query_pos)
    gain_one = attn_gain.astype(jnp.float32)
    gain_two = mlp_gain.astype(jnp.float32)
    shapes = (attn_gain, w_query, w_key, w_value, w_out, mlp_gain, w_gate, w_up, w_down)
    totals = tuple((jnp.zeros(parameter.shape, jnp.float32) for parameter in shapes))
    outputs = []
    grad_inputs = []
    for sample in range(micro_count):
        starts = doc_starts[sample]
        flag_skip = skip_flags[sample] == 1
        active = (1 - skip_flags[sample]).astype(jnp.float32)
        inputs = tokens[sample].astype(jnp.float32)
        normed_one, inverse_one = normalize(inputs, gain_one)
        normed_one = normed_one.astype(jnp.bfloat16)
        queries = jnp.dot(normed_one, w_query, preferred_element_type=jnp.float32)
        keyset = jnp.dot(normed_one, w_key, preferred_element_type=jnp.float32)
        valueset = jnp.dot(normed_one, w_value, preferred_element_type=jnp.float32).astype(
            jnp.bfloat16
        )
        queries = rotate_forward(queries.reshape(rows_dev, HQ, HD), query_cos, query_sin).astype(
            jnp.bfloat16
        )
        queries = queries.reshape(rows_dev, KVH, groups, HD)
        keyset = rotate_forward(keyset.reshape(rows_dev, KVH, HD), query_cos, query_sin).astype(
            jnp.bfloat16
        )
        keyset = keyset.reshape(rows_dev, KVH * HD)
        key_all, value_all = keyset, valueset
        key_pos = jnp.arange(key_all.shape[0], dtype=jnp.int32)
        key_count = key_all.shape[0]
        keys_three = key_all.reshape(key_count, KVH, HD)
        values_three = value_all.reshape(key_count, KVH, HD)
        query_docs = doc_index(query_pos, starts)
        key_docs = doc_index(key_pos, starts)
        allowed = (
            (key_pos[None, :] <= query_pos[:, None])
            & (key_docs[None, :] == query_docs[:, None])
            & (key_pos[None, :] >= 0)
        )
        query_block = queries
        scores = block_scores(query_block, keys_three, allowed, score_scale)
        peak_score = jnp.max(scores, -1, keepdims=True)
        exponent = jnp.exp(scores - peak_score)
        summed = jnp.sum(exponent, -1, keepdims=True)
        soft_weights = (exponent / summed).astype(jnp.bfloat16)
        log_totals = peak_score + jnp.log(summed)
        mixed_block = jnp.einsum(
            "kgbt,tkd->bkgd", soft_weights, values_three, preferred_element_type=jnp.float32
        )
        mixed_parts = mixed_block.reshape(block_rows, HQ * HD)
        mixed_heads = mixed_parts.astype(jnp.bfloat16)
        hidden_state = inputs + jnp.dot(mixed_heads, w_out, preferred_element_type=jnp.float32)
        normed_two, inverse_two = normalize(hidden_state, gain_two)
        normed_two = normed_two.astype(jnp.bfloat16)
        gate_proj = jnp.dot(normed_two, w_gate, preferred_element_type=jnp.float32)
        up_proj = jnp.dot(normed_two, w_up, preferred_element_type=jnp.float32)
        sigmoid_gate = jax.nn.sigmoid(gate_proj)
        inner_act = (gate_proj * sigmoid_gate * up_proj).astype(jnp.bfloat16)
        result = hidden_state + jnp.dot(inner_act, w_down, preferred_element_type=jnp.float32)
        outputs.append(jnp.where(flag_skip, inputs, result).astype(jnp.bfloat16))
        upstream = cotangent[sample].astype(jnp.float32)
        grad_out = upstream * active
        grad_low = grad_out.astype(jnp.bfloat16)
        grad_down = jnp.einsum("rf,rd->fd", inner_act, grad_low, preferred_element_type=jnp.float32)
        grad_inner = jnp.einsum("rd,fd->rf", grad_low, w_down, preferred_element_type=jnp.float32)
        grad_up = (grad_inner * gate_proj * sigmoid_gate).astype(jnp.bfloat16)
        grad_gate = (
            grad_inner * up_proj * sigmoid_gate * (1.0 + gate_proj * (1.0 - sigmoid_gate))
        ).astype(jnp.bfloat16)
        grad_gate_w = jnp.einsum(
            "rd,rf->df", normed_two, grad_gate, preferred_element_type=jnp.float32
        )
        grad_up_w = jnp.einsum("rd,rf->df", normed_two, grad_up, preferred_element_type=jnp.float32)
        grad_normed_two = jnp.einsum(
            "rf,df->rd", grad_gate, w_gate, preferred_element_type=jnp.float32
        ) + jnp.einsum("rf,df->rd", grad_up, w_up, preferred_element_type=jnp.float32)
        grad_hidden_norm, grad_gain_two = norm_back(
            grad_normed_two, hidden_state, inverse_two, gain_two
        )
        grad_hidden = grad_out + grad_hidden_norm
        grad_attn = grad_hidden.astype(jnp.bfloat16)
        grad_out_w = jnp.einsum(
            "rh,rd->hd", mixed_heads, grad_attn, preferred_element_type=jnp.float32
        )
        grad_mixed = jnp.einsum(
            "rd,hd->rh", grad_attn, w_out, preferred_element_type=jnp.float32
        ).astype(jnp.bfloat16)
        grad_mixed = grad_mixed.reshape(rows_dev, KVH, groups, HD)
        query_block = queries
        scores = block_scores(query_block, keys_three, allowed, score_scale)
        soft_full = jnp.exp(scores - log_totals)
        soft_low = soft_full.astype(jnp.bfloat16)
        grad_soft = jnp.einsum(
            "bkgd,tkd->kgbt", grad_mixed, values_three, preferred_element_type=jnp.float32
        )
        delta_sum = jnp.sum(soft_full * grad_soft, -1, keepdims=True)
        grad_scores = (soft_full * (grad_soft - delta_sum) * score_scale).astype(jnp.bfloat16)
        grad_query_parts = jnp.einsum(
            "kgbt,tkd->bkgd", grad_scores, keys_three, preferred_element_type=jnp.float32
        )
        grad_keys = jnp.einsum(
            "kgbt,bkgd->tkd", grad_scores, query_block, preferred_element_type=jnp.float32
        )
        grad_values = jnp.einsum(
            "kgbt,bkgd->tkd", soft_low, grad_mixed, preferred_element_type=jnp.float32
        )
        grad_keys = grad_keys.reshape(key_count, KVH * HD)
        grad_values = grad_values.reshape(key_count, KVH * HD)
        own_keys, own_values = grad_keys, grad_values
        grad_key_low = (
            rotate_back(own_keys.reshape(rows_dev, KVH, HD), query_cos, query_sin)
            .reshape(rows_dev, KVH * HD)
            .astype(jnp.bfloat16)
        )
        grad_queries = grad_query_parts.reshape(rows_dev, HQ, HD)
        grad_query_low = (
            rotate_back(grad_queries, query_cos, query_sin)
            .reshape(rows_dev, HQ * HD)
            .astype(jnp.bfloat16)
        )
        grad_value_low = own_values.astype(jnp.bfloat16)
        grad_query_w = jnp.einsum(
            "rd,rh->dh", normed_one, grad_query_low, preferred_element_type=jnp.float32
        )
        grad_key_w = jnp.einsum(
            "rd,rh->dh", normed_one, grad_key_low, preferred_element_type=jnp.float32
        )
        grad_value_w = jnp.einsum(
            "rd,rh->dh", normed_one, grad_value_low, preferred_element_type=jnp.float32
        )
        grad_normed_one = jnp.einsum(
            "rh,dh->rd", grad_query_low, w_query, preferred_element_type=jnp.float32
        )
        grad_normed_one = grad_normed_one + jnp.einsum(
            "rh,dh->rd", grad_key_low, w_key, preferred_element_type=jnp.float32
        )
        grad_normed_one = grad_normed_one + jnp.einsum(
            "rh,dh->rd", grad_value_low, w_value, preferred_element_type=jnp.float32
        )
        grad_input_norm, grad_gain_one = norm_back(grad_normed_one, inputs, inverse_one, gain_one)
        grad_total = grad_hidden + grad_input_norm
        grad_inputs.append(jnp.where(flag_skip, upstream, grad_total).astype(jnp.bfloat16))
        micro_grads = (
            grad_gain_one,
            grad_query_w,
            grad_key_w,
            grad_value_w,
            grad_out_w,
            grad_gain_two,
            grad_gate_w,
            grad_up_w,
            grad_down,
        )
        totals = tuple((running + fresh for running, fresh in zip(totals, micro_grads)))
    chips = lax.axis_size("wide")
    order = (6, 7, 8, 1, 2, 3, 4, 0, 5)
    flat = jnp.concatenate([totals[i].astype(jnp.bfloat16).reshape(-1) for i in order])
    unit = 128 * 16 * 2 * 3 * chips
    size = flat.shape[0]
    flat = jnp.pad(flat, (0, -size % unit)).reshape(-1, 128)
    summed = sum_everywhere(flat, chips).reshape(-1)
    results = [None] * 9
    offset = 0
    for i in order:
        length = totals[i].size
        results[i] = summed[offset : offset + length].reshape(totals[i].shape).astype(jnp.float32)
        offset += length
    return (
        back_to_halves(outputs[0]),
        back_to_halves(grad_inputs[0]),
        *results,
    )


def solution(mesh):
    in_specs = (
        P("wide", "narrow", None),
        P("wide", None),
        P("wide"),
        P("wide", "narrow", None),
        P(),
        P(),
        P(),
        P(),
        P(),
        P(),
        P(),
        P(),
        P(),
    )
    out_specs = (
        P("wide", "narrow", None),
        P("wide", "narrow", None),
        P(),
        P(),
        P(),
        P(),
        P(),
        P(),
        P(),
        P(),
        P(),
    )
    return jax.shard_map(
        per_device, mesh=mesh, in_specs=in_specs, out_specs=out_specs, check_vma=False
    )
```

```python
import functools

import jax
import jax.numpy as jnp
import numpy as np
from jax import lax
from jax.experimental import pallas as pl
from jax.experimental.pallas import tpu as pltpu
from jax.sharding import PartitionSpec as P

HQ = 9
KVH = 3
HD = 64
GROUPS = HQ // KVH
theta_base = 100000.0
eps_norm = 1e-05
masked_score = -1e30
BLOCK = 256
PARTS = 2
GAIN_ROWS = 16
f32 = jnp.float32
bf16 = jnp.bfloat16


def dot(a, b, ca=1, cb=0):
    return lax.dot_general(a, b, (((ca,), (cb,)), ((), ())), preferred_element_type=f32)


def turn(rows, cosine, sine, sign):
    half = HD // 2
    first, second = rows[:half], rows[half:]
    if sign > 0:
        return first * cosine - second * sine, second * cosine + first * sine
    return first * cosine + second * sine, second * cosine - first * sine


def forward_kernel(
    place_ref, skip_ref, own_ref, other_ref, cot_own_ref, cot_other_ref,
    gain_one_ref, wqkv_ref, w_out_ref, gain_two_ref, cos_ref, sin_ref, start_ref,
    qn_ref, kt_ref, vn_ref, soft_ref, mixed_ref, hidden_ref, n2_ref, n2t_ref, g_ref, gt_ref,
    kn_all, vt_all, qt_ref,
):
    step = pl.program_id(0)
    blocks = 4
    mine = (step >= blocks // 2).astype(jnp.int32) == place_ref[0]
    x = jnp.where(mine, own_ref[0], other_ref[...]).astype(f32)
    cot = jnp.where(mine, cot_own_ref[0], cot_other_ref[...])
    g = jnp.where(skip_ref[0] == 1, jnp.zeros_like(cot), cot)
    width = x.shape[1]
    blank = jnp.zeros((BLOCK, g_ref.shape[1] - width), bf16)
    g_ref[...] = jnp.concatenate([g, blank], 1)
    gt_ref[...] = g.T
    inverse = lax.rsqrt(jnp.mean(x * x, -1, keepdims=True) + eps_norm)
    n1 = (x * inverse * gain_one_ref[...]).astype(bf16)
    qkv = dot(wqkv_ref[...], n1, 1, 1)
    cosine, sine = cos_ref[...], sin_ref[...]
    per = (GROUPS + 2) * HD
    zero = jnp.zeros((HD, BLOCK), bf16)
    here = pl.ds(pl.multiple_of(step * BLOCK, BLOCK), BLOCK)
    for g in range(KVH):
        for r in range(GROUPS):
            head = g * GROUPS + r
            base = g * per + r * HD
            rows = jnp.concatenate(turn(qkv[base : base + HD], cosine, sine, 1), 0)
            rows = (rows * (HD**-0.5)).astype(bf16)
            qt_ref[head * HD : (head + 1) * HD] = rows
            qn_ref[head] = jnp.concatenate([rows, zero], 0).T
        base = g * per + GROUPS * HD
        rows = jnp.concatenate(turn(qkv[base : base + HD], cosine, sine, 1), 0).astype(bf16)
        kt_ref[g * HD : (g + 1) * HD] = rows
        kn_all[g, here] = rows.T
        rows = qkv[base + HD : base + 2 * HD].astype(bf16)
        vt_all[step, g * HD : (g + 1) * HD] = rows
        vn_ref[g] = rows.T

    start_row = start_ref[...]

    def attend(count):
        t = lax.broadcasted_iota(jnp.int32, (BLOCK, BLOCK), 0)
        s_pos = lax.broadcasted_iota(jnp.int32, (BLOCK, BLOCK), 1)

        def one_group(g, carry):
            for r in range(GROUPS):
                head = g * GROUPS + r
                rows = pl.ds(pl.multiple_of(head * HD, HD), HD)
                q = qt_ref[rows]
                scores = []
                for kb in range(count):
                    s = dot(kn_all[g, kb * BLOCK : (kb + 1) * BLOCK], q)
                    ok = t + kb * BLOCK >= start_row
                    if kb == count - 1:
                        ok = ok & (t <= s_pos)
                    scores.append(jnp.where(ok, s, masked_score))
                peak = scores[0].max(0, keepdims=True)
                for s in scores[1:]:
                    peak = jnp.maximum(peak, s.max(0, keepdims=True))
                exps = [jnp.exp(s - peak) for s in scores]
                total = exps[0].sum(0, keepdims=True)
                for e in exps[1:]:
                    total = total + e.sum(0, keepdims=True)
                scale = 1.0 / total
                out = None
                for kb in range(count):
                    p = (exps[kb] * scale).astype(bf16)
                    soft_ref[0, head, kb * BLOCK : (kb + 1) * BLOCK] = p
                    v = vt_all[kb, pl.ds(pl.multiple_of(g * HD, HD), HD)]
                    term = dot(v, p)
                    out = term if out is None else out + term
                mixed_ref[rows] = out.astype(bf16)
            return carry

        lax.fori_loop(0, KVH, one_group, 0)

    for count in range(1, 5):
        pl.when(step == count - 1)(lambda count=count: attend(count))

    hidden = x + dot(mixed_ref[...], w_out_ref[...], 0, 0)
    hidden_ref[...] = hidden
    inverse = lax.rsqrt(jnp.mean(hidden * hidden, -1, keepdims=True) + eps_norm)
    n2 = (hidden * inverse * gain_two_ref[...]).astype(bf16)
    n2_ref[...] = jnp.concatenate([n2, blank], 1)
    n2t_ref[...] = n2.T


def full(shape):
    return pl.BlockSpec(shape, lambda *_: (0,) * len(shape))


def forward(place, skip, tokens, other, cot, cot_other, gain_one, wqkv_t, w_out, gain_two, cos_t, sin_t, start_row):
    rows = 2 * tokens.shape[1]
    width = tokens.shape[2]
    blocks = rows // BLOCK
    near = blocks // 2
    own = pl.BlockSpec((1, BLOCK, width), lambda i, c, s: (c[0], jnp.where(i >= near, i - near, i), 0))
    oth = pl.BlockSpec((BLOCK, width), lambda i, c, s: (jnp.where(i >= near, i - near, i), 0))
    return pl.pallas_call(
        forward_kernel,
        grid_spec=pltpu.PrefetchScalarGridSpec(
            num_scalar_prefetch=2,
            grid=(blocks,),
            in_specs=[
                own, oth, own, oth,
                full((1, width)),
                full(wqkv_t.shape),
                full(w_out.shape),
                full((1, width)),
                pl.BlockSpec((HD // 2, BLOCK), lambda i, c, s: (0, i)),
                pl.BlockSpec((HD // 2, BLOCK), lambda i, c, s: (0, i)),
                pl.BlockSpec((1, BLOCK), lambda i, c, s: (0, i)),
            ],
            out_specs=[
                pl.BlockSpec((HQ, BLOCK, 2 * HD), lambda i, c, s: (0, i, 0)),
                pl.BlockSpec((KVH * HD, BLOCK), lambda i, c, s: (0, i)),
                pl.BlockSpec((KVH, BLOCK, HD), lambda i, c, s: (0, i, 0)),
                pl.BlockSpec((1, HQ, rows, BLOCK), lambda i, c, s: (i, 0, 0, 0)),
                pl.BlockSpec((HQ * HD, BLOCK), lambda i, c, s: (0, i)),
                pl.BlockSpec((BLOCK, width), lambda i, c, s: (i, 0)),
                pl.BlockSpec((BLOCK, lanes_up(width)), lambda i, c, s: (i, 0)),
                pl.BlockSpec((width, BLOCK), lambda i, c, s: (0, i)),
                pl.BlockSpec((BLOCK, lanes_up(width)), lambda i, c, s: (i, 0)),
                pl.BlockSpec((width, BLOCK), lambda i, c, s: (0, i)),
            ],
            scratch_shapes=[
                pltpu.VMEM((KVH, rows, HD), bf16),
                pltpu.VMEM((blocks, KVH * HD, BLOCK), bf16),
                pltpu.VMEM((HQ * HD, BLOCK), bf16),
            ],
        ),
        out_shape=[
            jax.ShapeDtypeStruct((HQ, rows, 2 * HD), bf16),
            jax.ShapeDtypeStruct((KVH * HD, rows), bf16),
            jax.ShapeDtypeStruct((KVH, rows, HD), bf16),
            jax.ShapeDtypeStruct((blocks, HQ, rows, BLOCK), bf16),
            jax.ShapeDtypeStruct((HQ * HD, rows), bf16),
            jax.ShapeDtypeStruct((rows, width), f32),
            jax.ShapeDtypeStruct((rows, lanes_up(width)), bf16),
            jax.ShapeDtypeStruct((width, rows), bf16),
            jax.ShapeDtypeStruct((rows, lanes_up(width)), bf16),
            jax.ShapeDtypeStruct((width, rows), bf16),
        ],
        compiler_params=pltpu.CompilerParams(vmem_limit_bytes=56 * 2**20),
        name="attention_forward",
    )(place, skip, tokens, other, cot, cot_other, gain_one, wqkv_t, w_out, gain_two, cos_t, sin_t, start_row)


def lanes_up(count):
    return -(-count // 128) * 128


def pack_blocks(target, spot, matrix):
    for k in range(matrix.shape[1] // 128):
        target[spot : spot + matrix.shape[0]] = matrix[:, k * 128 : (k + 1) * 128]
        spot += matrix.shape[0]
    return spot


def mlp_kernel(
    final, place_ref, skip_ref, n2_ref, n2t_ref, g_ref, gt_ref, w_gate_ref, w_up_ref, w_down_ref,
    sum_ref, gn2_in_ref, *refs,
):
    if final:
        (
            own_ref, other_ref, hidden_ref, gain_two_ref, w_out_ref, mixed_ref,
            mixed_out_ref, gh_ref, dot_ref, dop_ref, delta_ref, dw_out_ref, dgain_ref, keep_ref, send_ref,
            inner_sc, grads_sc, in_sc, in_t_sc, down_sc, down_t_sc, dw_out_sc,
        ) = refs
    else:
        (out_ref, gn2_ref, keep_ref, send_ref, inner_sc, grads_sc, in_sc, in_t_sc, down_sc, down_t_sc) = refs
    step = pl.program_id(0)
    width = n2t_ref.shape[0]
    wide = lanes_up(width)
    cols = w_gate_ref.shape[1]
    half = cols // 2

    @pl.when(step == 0)
    def _():
        in_sc[...] = jnp.zeros_like(in_sc)
        in_t_sc[...] = jnp.zeros_like(in_t_sc)
        down_sc[...] = jnp.zeros_like(down_sc)
        down_t_sc[...] = jnp.zeros_like(down_t_sc)
        for k, ref in enumerate((w_gate_ref, w_up_ref)):
            in_sc[:width, k * cols : (k + 1) * cols] = ref[...]
            in_t_sc[k * cols : (k + 1) * cols, :width] = ref[...].T
        down_sc[:, :width] = w_down_ref[...]
        down_t_sc[:width] = w_down_ref[...].T
        if final:
            dw_out_sc[...] = jnp.zeros_like(dw_out_sc)
            dgain_ref[...] = jnp.zeros_like(dgain_ref)

    here = pl.ds(pl.multiple_of(step * BLOCK, BLOCK), BLOCK)
    n2 = n2_ref[...]
    g = g_ref[...]
    for c in range(0, cols, BLOCK):
        gate = dot(n2, in_sc[:, c : c + BLOCK])
        up = dot(n2, in_sc[:, cols + c : cols + c + BLOCK])
        sig = jax.nn.sigmoid(gate)
        act = gate * sig
        inner_sc[here, c : c + BLOCK] = (act * up).astype(bf16)
        grad_inner = dot(g, down_t_sc[:, c : c + BLOCK])
        grads_sc[here, c : c + BLOCK] = (grad_inner * up * (sig + act * (1.0 - sig))).astype(bf16)
        grads_sc[here, cols + c : cols + c + BLOCK] = (grad_inner * act).astype(bf16)
    out = sum_ref[...] + dot(inner_sc[here], down_sc[...])[:, :width]
    gn2 = dot(grads_sc[here], in_t_sc[...])[:, :width]
    if final:
        gn2 = gn2 + gn2_in_ref[...]
        mine = (step >= 2).astype(jnp.int32) == place_ref[0]
        x = jnp.where(mine, own_ref[0], other_ref[...])
        skipped = skip_ref[0] == 1
        hidden = hidden_ref[...]
        mixed_out_ref[...] = jnp.where(skipped, x, out.astype(bf16))
        inverse = lax.rsqrt(jnp.mean(hidden * hidden, -1, keepdims=True) + eps_norm)
        c = gn2 * gain_two_ref[...]
        normed = hidden * inverse
        dgain_ref[0:1] += jnp.sum(gn2 * normed, 0, keepdims=True)
        gh = g[:, :width].astype(f32) + inverse * (c - normed * jnp.mean(c * normed, -1, keepdims=True))
        gh_ref[...] = gh
        ga = gh.astype(bf16)
        mixed = mixed_ref[...]
        dw_out_sc[...] += dot(mixed, ga)
        back = dot(w_out_ref[...], ga, 1, 1).astype(bf16)
        dot_ref[...] = back
        zero = jnp.zeros((HD, BLOCK), bf16)
        for head in range(HQ):
            rows = back[head * HD : (head + 1) * HD]
            dop_ref[head] = jnp.concatenate([zero, rows], 0).T
            delta_ref[head // GROUPS, head % GROUPS : head % GROUPS + 1] = jnp.sum(
                rows.astype(f32) * mixed[head * HD : (head + 1) * HD].astype(f32), 0, keepdims=True
            )
    else:
        out_ref[...] = out
        gn2_ref[...] = gn2

    @pl.when(step == pl.num_programs(0) - 1)
    def _():
        if final:
            dw_out_ref[...] = dw_out_sc[...].astype(bf16)
        for h in range(2):
            def emit(target):
                spot = 0
                for left, right, at in (
                    (n2t_ref, grads_sc, h * half),
                    (n2t_ref, grads_sc, cols + h * half),
                    (gt_ref, inner_sc, h * half),
                ):
                    spot = pack_blocks(target, spot, dot(left[...], right[:, at : at + half]).astype(bf16))
                target[spot:] = jnp.zeros((target.shape[0] - spot, 128), bf16)

            pl.when(place_ref[0] == h)(lambda: emit(keep_ref))
            pl.when(place_ref[0] != h)(lambda: emit(send_ref))


def mlp_part(part, parts, half_rows, place, skip, n2, n2t, g, gt, wg, wu, wd, sums, gn2, extra=()):
    final = part == parts - 1
    width, rows = n2t.shape
    wide = n2.shape[1]
    blocks = rows // BLOCK
    near = blocks // 2
    cols = wg.shape[1] // parts
    row = pl.BlockSpec((BLOCK, width), lambda i, c, s: (i, 0))
    row_wide = pl.BlockSpec((BLOCK, wide), lambda i, c, s: (i, 0))
    col = pl.BlockSpec((HQ * HD, BLOCK), lambda i, c, s: (0, i))
    own = pl.BlockSpec((1, BLOCK, width), lambda i, c, s: (c[0], jnp.where(i >= near, i - near, i), 0))
    oth = pl.BlockSpec((BLOCK, width), lambda i, c, s: (jnp.where(i >= near, i - near, i), 0))
    in_specs = [
        row_wide, full((width, rows)), row_wide, full((width, rows)),
        pl.BlockSpec((width, cols), lambda i, c, s: (0, part)),
        pl.BlockSpec((width, cols), lambda i, c, s: (0, part)),
        pl.BlockSpec((cols, width), lambda i, c, s: (part, 0)),
        row, row,
    ]
    halves = [full((half_rows, 128))] * 2
    half_shapes = [jax.ShapeDtypeStruct((half_rows, 128), bf16)] * 2
    if final:
        in_specs += [own, oth, row, full((1, width)), full((HQ * HD, width)), col]
        out_specs = [
            row, row, col,
            pl.BlockSpec((HQ, BLOCK, 2 * HD), lambda i, c, s: (0, i, 0)),
            pl.BlockSpec((KVH, GROUPS, BLOCK), lambda i, c, s: (0, 0, i)),
            full((HQ * HD, width)), full((8, width)),
        ] + halves
        out_shape = [
            jax.ShapeDtypeStruct((rows, width), bf16),
            jax.ShapeDtypeStruct((rows, width), f32),
            jax.ShapeDtypeStruct((HQ * HD, rows), bf16),
            jax.ShapeDtypeStruct((HQ, rows, 2 * HD), bf16),
            jax.ShapeDtypeStruct((KVH, GROUPS, rows), f32),
            jax.ShapeDtypeStruct((HQ * HD, width), bf16),
            jax.ShapeDtypeStruct((8, width), f32),
        ] + half_shapes
    else:
        out_specs = [row, row] + halves
        out_shape = [jax.ShapeDtypeStruct((rows, width), f32)] * 2 + half_shapes
    scratch = [
        pltpu.VMEM((rows, cols), bf16),
        pltpu.VMEM((rows, 2 * cols), bf16),
        pltpu.VMEM((wide, 2 * cols), bf16),
        pltpu.VMEM((2 * cols, wide), bf16),
        pltpu.VMEM((cols, wide), bf16),
        pltpu.VMEM((wide, cols), bf16),
    ]
    if final:
        scratch.append(pltpu.VMEM((HQ * HD, width), f32))
    return pl.pallas_call(
        functools.partial(mlp_kernel, final),
        grid_spec=pltpu.PrefetchScalarGridSpec(
            num_scalar_prefetch=2, grid=(blocks,), in_specs=in_specs, out_specs=out_specs, scratch_shapes=scratch
        ),
        out_shape=out_shape,
        compiler_params=pltpu.CompilerParams(vmem_limit_bytes=56 * 2**20),
        name="mlp_both_ways",
    )(place, skip, n2, n2t, g, gt, wg, wu, wd, sums, gn2, *extra)


def back_kernel(
    soft_ref, qn_ref, kt_ref, vn_ref, dot_ref, dop_ref, delta_ref, cos_ref, sin_ref,
    dqkv_ref,
    acc,
):
    step = pl.program_id(1)
    cosine, sine = cos_ref[...], sin_ref[...]

    def attend(count):
        last = count - 1
        terms = [None] * count
        for r in range(GROUPS):
            up = dot_ref[r * HD : (r + 1) * HD]
            delta = delta_ref[0, r : r + 1]
            dq = None
            pads = jnp.concatenate([qn_ref[r], dop_ref[r]], 0)
            for kb in range(count):
                span = slice(kb * BLOCK, (kb + 1) * BLOCK)
                p = soft_ref[0, r, span]
                ds = (p.astype(f32) * (dot(vn_ref[0, span], up) - delta)).astype(bf16)
                term = dot(kt_ref[:, span], ds)
                dq = term if dq is None else dq + term
                kv = dot(jnp.concatenate([ds, p], 1), pads)
                terms[kb] = kv if terms[kb] is None else terms[kb] + kv
            dq = dq * (HD**-0.5)
            a, b = turn(dq, cosine, sine, -1)
            dqkv_ref[0, r * HD : r * HD + HD // 2] = a.astype(bf16)
            dqkv_ref[0, r * HD + HD // 2 : (r + 1) * HD] = b.astype(bf16)
        for kb in range(count):
            span = slice(kb * BLOCK, (kb + 1) * BLOCK)
            total = terms[kb] if count == 4 else acc[span] + terms[kb]
            if kb < last:
                acc[span] = total
            else:
                done = total.T
                a, b = turn(done[:HD], cosine, sine, -1)
                base = GROUPS * HD
                dqkv_ref[0, base : base + HD // 2] = a.astype(bf16)
                dqkv_ref[0, base + HD // 2 : base + HD] = b.astype(bf16)
                dqkv_ref[0, base + HD : base + 2 * HD] = done[HD:].astype(bf16)

    for count in range(1, 5):
        pl.when(step == 4 - count)(lambda count=count: attend(count))


def back(first, groups, soft, qn, kt, vn, dot_t, dop, delta, cos_t, sin_t):
    blocks, _, rows, _ = soft.shape
    last = blocks - 1
    return pl.pallas_call(
        back_kernel,
        grid=(groups, blocks),
        in_specs=[
            pl.BlockSpec((1, GROUPS, rows, BLOCK), lambda g, i: (last - i, first + g, 0, 0)),
            pl.BlockSpec((GROUPS, BLOCK, 2 * HD), lambda g, i: (first + g, last - i, 0)),
            pl.BlockSpec((HD, rows), lambda g, i: (first + g, 0)),
            pl.BlockSpec((1, rows, HD), lambda g, i: (first + g, 0, 0)),
            pl.BlockSpec((GROUPS * HD, BLOCK), lambda g, i: (first + g, last - i)),
            pl.BlockSpec((GROUPS, BLOCK, 2 * HD), lambda g, i: (first + g, last - i, 0)),
            pl.BlockSpec((1, GROUPS, BLOCK), lambda g, i: (first + g, 0, last - i)),
            pl.BlockSpec((HD // 2, BLOCK), lambda g, i: (0, last - i)),
            pl.BlockSpec((HD // 2, BLOCK), lambda g, i: (0, last - i)),
        ],
        out_specs=pl.BlockSpec((1, (GROUPS + 2) * HD, BLOCK), lambda g, i: (g, 0, last - i)),
        out_shape=jax.ShapeDtypeStruct((groups, (GROUPS + 2) * HD, rows), bf16),
        scratch_shapes=[pltpu.VMEM((rows, 2 * HD), f32)],
        compiler_params=pltpu.CompilerParams(vmem_limit_bytes=56 * 2**20),
        name="attention_backward",
    )(soft, qn, kt, vn, dot_t, dop, delta, cos_t, sin_t)


def pack_gain(target, spot, gain):
    width = gain.shape[1]
    wide = jnp.concatenate([gain, jnp.zeros((1, lanes_up(width) - width), gain.dtype)], 1)
    rows = [wide[:, k * 128 : (k + 1) * 128] for k in range(wide.shape[1] // 128)]
    rows.append(jnp.zeros((GAIN_ROWS - len(rows), 128), gain.dtype))
    target[spot : spot + GAIN_ROWS] = jnp.concatenate(rows, 0).astype(bf16)


def last_kernel(
    place_ref, skip_ref, own_ref, other_ref, cot_own_ref, cot_other_ref, gh_ref, dqkv_ref, wqkv_ref, gain_one_ref,
    dw_out_ref, dgain_two_ref,
    grad_ref, keep_ref, send_ref,
    dw_sc, dgain_sc,
):
    step = pl.program_id(0)
    mine = (step >= 2).astype(jnp.int32) == place_ref[0]
    x = jnp.where(mine, own_ref[0], other_ref[...]).astype(f32)
    cot = jnp.where(mine, cot_own_ref[0], cot_other_ref[...])
    skipped = skip_ref[0] == 1
    inverse = lax.rsqrt(jnp.mean(x * x, -1, keepdims=True) + eps_norm)
    normed = x * inverse
    gain = gain_one_ref[...]
    n1 = (normed * gain).astype(bf16)
    dqkv = dqkv_ref[...].reshape(wqkv_ref.shape[0], BLOCK)
    dw = dot(n1.T, dqkv, 1, 1)
    gn1 = dot(dqkv, wqkv_ref[...], 0, 0)
    c = gn1 * gain
    gain_term = jnp.sum(gn1 * normed, 0, keepdims=True)

    @pl.when(step == 0)
    def _():
        dgain_sc[...] = jnp.zeros_like(dgain_sc)
        dw_sc[...] = jnp.zeros_like(dw_sc)

    dgain_sc[0:1] += gain_term
    dw_sc[...] += dw
    gx = gh_ref[...] + inverse * (c - normed * jnp.mean(c * normed, -1, keepdims=True))
    grad_ref[...] = jnp.where(skipped, cot, gx.astype(bf16))

    @pl.when(step == pl.num_programs(0) - 1)
    def _():
        both = jnp.concatenate([dw_sc[...].astype(bf16), dw_out_ref[...]], 1)
        half = both.shape[1] // 2

        def emit(h, target):
            spot = pack_blocks(target, 0, both[:, h * half : (h + 1) * half])
            target[spot:] = jnp.zeros((target.shape[0] - spot, 128), bf16)
            if h == 0:
                pack_gain(target, spot, dgain_sc[0:1])
                pack_gain(target, spot + GAIN_ROWS, dgain_two_ref[0:1])

        for h in range(2):
            pl.when(place_ref[0] == h)(lambda h=h: emit(h, keep_ref))
            pl.when(place_ref[0] != h)(lambda h=h: emit(h, send_ref))


def last(half_rows, place, skip, tokens, other, cot, cot_other, gh, dqkv, wqkv_g, gain_one, dw_out, dgain_two):
    rows, width = gh.shape
    blocks = rows // BLOCK
    near = blocks // 2
    own = pl.BlockSpec((1, BLOCK, width), lambda i, c, s: (c[0], jnp.where(i >= near, i - near, i), 0))
    oth = pl.BlockSpec((BLOCK, width), lambda i, c, s: (jnp.where(i >= near, i - near, i), 0))
    row = pl.BlockSpec((BLOCK, width), lambda i, c, s: (i, 0))
    return pl.pallas_call(
        last_kernel,
        grid_spec=pltpu.PrefetchScalarGridSpec(
            num_scalar_prefetch=2,
            grid=(blocks,),
            in_specs=[
                own, oth, own, oth, row,
                pl.BlockSpec(dqkv.shape[:2] + (BLOCK,), lambda i, c, s: (0, 0, i)),
                full(wqkv_g.shape), full((1, width)), full(dw_out.shape), full((8, width)),
            ],
            out_specs=[row] + [full((half_rows, 128))] * 2,
            scratch_shapes=[pltpu.VMEM((width, wqkv_g.shape[0]), f32), pltpu.VMEM((8, width), f32)],
        ),
        out_shape=[jax.ShapeDtypeStruct((rows, width), bf16)]
        + [jax.ShapeDtypeStruct((half_rows, 128), bf16)] * 2,
        compiler_params=pltpu.CompilerParams(vmem_limit_bytes=56 * 2**20),
        name="input_backward",
    )(place, skip, tokens, other, cot, cot_other, gh, dqkv, wqkv_g, gain_one, dw_out, dgain_two)


def rotary_rows(rows):
    frequency = theta_base ** (-2.0 * np.arange(HD // 2, dtype=np.float64) / HD)
    angles = frequency[:, None] * np.arange(rows, dtype=np.float64)[None, :]
    return np.cos(angles).astype(np.float32), np.sin(angles).astype(np.float32)


def combine_kernel(bit_ref, kept_a, kept_b, got_a, got_b, keep_ref, send_ref):
    keep_ref[...] = (kept_a[...].astype(f32) + got_a[...].astype(f32)).astype(bf16)
    send_ref[...] = (kept_b[...].astype(f32) + got_b[...].astype(f32)).astype(bf16)


def combine(bit, kept, got):
    rows = kept.shape[0] // 2
    spec_a = pl.BlockSpec((rows, 128), lambda i, b: (b[0], 0))
    spec_b = pl.BlockSpec((rows, 128), lambda i, b: (1 - b[0], 0))
    return pl.pallas_call(
        combine_kernel,
        grid_spec=pltpu.PrefetchScalarGridSpec(
            num_scalar_prefetch=1,
            grid=(1,),
            in_specs=[spec_a, spec_b, spec_a, spec_b],
            out_specs=[full((rows, 128))] * 2,
        ),
        out_shape=[jax.ShapeDtypeStruct((rows, 128), bf16)] * 2,
        name="combine",
    )(bit, kept, kept, got, got)


def add_kernel(kept_ref, got_ref, out_ref):
    out_ref[...] = (kept_ref[...].astype(f32) + got_ref[...].astype(f32)).astype(bf16)


def add(kept, got):
    return pl.pallas_call(add_kernel, out_shape=jax.ShapeDtypeStruct(kept.shape, bf16), name="add")(kept, got)


def join_kernel(bit_ref, own_ref, got_ref, out_ref):
    rows = own_ref.shape[0]
    out_ref[pl.ds(pl.multiple_of(bit_ref[0] * rows, 16), rows)] = own_ref[...]
    out_ref[pl.ds(pl.multiple_of((1 - bit_ref[0]) * rows, 16), rows)] = got_ref[...]


def join(bit, own, got):
    rows = own.shape[0]
    return pl.pallas_call(
        join_kernel,
        grid_spec=pltpu.PrefetchScalarGridSpec(
            num_scalar_prefetch=1,
            grid=(1,),
            in_specs=[full((rows, 128))] * 2,
            out_specs=full((2 * rows, 128)),
        ),
        out_shape=jax.ShapeDtypeStruct((2 * rows, 128), bf16),
        name="join",
    )(bit, own, got)


def swap_core(array):
    return lax.ppermute(array, "narrow", [(0, 1), (1, 0)])


def axis_orders(bits, turn):
    if bits == 4:
        table = (((0, 1, 2, 3), (1, 2, 3, 0)), ((1, 0, 2, 3), (2, 3, 0, 1)), ((0, 1, 2, 3), (1, 2, 3, 0)))
        return table[turn]
    base = tuple(range(bits))
    shift = bits // 2
    return base, base[shift:] + base[:shift]


class Summer:
    def __init__(self, core, chips, turn):
        self.core = core
        self.chips = chips
        self.bits = chips.bit_length() - 1
        self.orders = axis_orders(self.bits, turn)
        self.place = lax.axis_index("wide")

    def bit(self, step):
        by_core = [(self.place >> order[step]) & 1 for order in self.orders]
        return jnp.where(self.core == 0, by_core[0], by_core[1]).astype(jnp.int32).reshape(1)

    def swap(self, array, step):
        pairs = [
            (2 * chip + c, 2 * (chip ^ (1 << self.orders[c][step])) + c) for chip in range(self.chips) for c in range(2)
        ]
        return lax.ppermute(array, ("wide", "narrow"), pairs)

    def run(self, keep, send):
        got = swap_core(send)
        for step in range(self.bits):
            keep, send = combine(self.bit(step), keep, got)
            got = self.swap(send, step)
        whole = add(keep, got)
        for step in reversed(range(self.bits)):
            whole = join(self.bit(step), whole, self.swap(whole, step))
        return whole, swap_core(whole)


def unpack_mlp_kernel(place_ref, *refs):
    sources, (gate_ref, up_ref, down_ref) = refs[:-3], refs[-3:]
    step = pl.program_id(0)
    width, cols = gate_ref.shape
    for part in range(len(sources) // 2):
        for h in range(2):
            def take(source):
                spot = 0
                for target in (gate_ref, up_ref):
                    for k in range(cols // 128):
                        target[:, k * 128 : (k + 1) * 128] = source[spot : spot + width].astype(f32)
                        spot += width
                for k in range(cols // 128):
                    down_ref[k * 128 : (k + 1) * 128] = source[spot : spot + width].astype(f32).T
                    spot += width

            here = step == 2 * part + h
            pl.when(here & (place_ref[0] == h))(lambda part=part: take(sources[2 * part]))
            pl.when(here & (place_ref[0] != h))(lambda part=part: take(sources[2 * part + 1]))


def unpack_mlp(place, buffers, width, inner):
    count = len(buffers)
    cols = inner // count
    return pl.pallas_call(
        unpack_mlp_kernel,
        grid_spec=pltpu.PrefetchScalarGridSpec(
            num_scalar_prefetch=1,
            grid=(count,),
            in_specs=[full(b.shape) for b in buffers],
            out_specs=[
                pl.BlockSpec((width, cols), lambda i, c: (0, i)),
                pl.BlockSpec((width, cols), lambda i, c: (0, i)),
                pl.BlockSpec((cols, width), lambda i, c: (i, 0)),
            ],
        ),
        out_shape=[
            jax.ShapeDtypeStruct((width, inner), f32),
            jax.ShapeDtypeStruct((width, inner), f32),
            jax.ShapeDtypeStruct((inner, width), f32),
        ],
        compiler_params=pltpu.CompilerParams(vmem_limit_bytes=56 * 2**20),
        name="unpack_mlp",
    )(place, *buffers)


def unpack_rest_kernel(place_ref, own_ref, got_ref, dq_ref, dk_ref, dv_ref, dw_out_ref, gain_one_ref, gain_two_ref):
    width = dq_ref.shape[0]
    blocks = (dq_ref.shape[1] + dk_ref.shape[1] + dv_ref.shape[1] + dw_out_ref.shape[1]) // 256

    def take(first, second):
        both = jnp.concatenate(
            [ref[k * width : (k + 1) * width] for ref in (first, second) for k in range(blocks)], 1
        ).astype(f32)
        per = (GROUPS + 2) * HD
        q_cols = GROUPS * HD
        for g in range(KVH):
            dq_ref[:, g * q_cols : (g + 1) * q_cols] = both[:, g * per : g * per + q_cols]
            dk_ref[:, g * HD : (g + 1) * HD] = both[:, g * per + q_cols : g * per + q_cols + HD]
            dv_ref[:, g * HD : (g + 1) * HD] = both[:, g * per + q_cols + HD : (g + 1) * per]
        dw_out_ref[...] = both[:, KVH * per :]
        spot = blocks * width
        for target in (gain_one_ref, gain_two_ref):
            rows = first[spot : spot + GAIN_ROWS].astype(f32)
            line = jnp.concatenate([rows[k : k + 1] for k in range(lanes_up(width) // 128)], 1)
            target[...] = line[:, :width]
            spot += GAIN_ROWS

    pl.when(place_ref[0] == 0)(lambda: take(own_ref, got_ref))
    pl.when(place_ref[0] != 0)(lambda: take(got_ref, own_ref))


def unpack_rest(place, own, got, shapes):
    return pl.pallas_call(
        unpack_rest_kernel,
        grid_spec=pltpu.PrefetchScalarGridSpec(
            num_scalar_prefetch=1,
            grid=(1,),
            in_specs=[full(own.shape)] * 2,
            out_specs=[full(shape) for shape in shapes],
        ),
        out_shape=[jax.ShapeDtypeStruct(shape, f32) for shape in shapes],
        compiler_params=pltpu.CompilerParams(vmem_limit_bytes=56 * 2**20),
        name="unpack_rest",
    )(place, own, got)


def halves_kernel(place_ref, own_ref, got_ref, out_ref):
    out_ref[pl.ds(place_ref[0], 1)] = own_ref[...][None]
    out_ref[pl.ds(1 - place_ref[0], 1)] = got_ref[...][None]


def back_to_halves(core, place, sample):
    rows, width = sample.shape
    near = rows // 2
    got = swap_core(lax.dynamic_slice_in_dim(sample, (1 - core) * near, near, 0))
    return pl.pallas_call(
        halves_kernel,
        grid_spec=pltpu.PrefetchScalarGridSpec(
            num_scalar_prefetch=1,
            grid=(1,),
            in_specs=[pl.BlockSpec((near, width), lambda i, c: (c[0], 0)), full((near, width))],
            out_specs=full((2, near, width)),
        ),
        out_shape=jax.ShapeDtypeStruct((2, near, width), sample.dtype),
        name="halves",
    )(place, sample, got)


def per_device(tokens, doc_starts, skip_flags, cotangent, attn_gain, wq, wk, wv, w_out, mlp_gain, wg, wu, wd):
    core = lax.axis_index("narrow")
    chips = lax.axis_size("wide")
    rows = 2 * tokens.shape[1]
    width = tokens.shape[2]
    inner = wg.shape[1]
    place = core.astype(jnp.int32).reshape(1)
    skip = lax.dynamic_slice_in_dim(skip_flags, core, 1, 0)
    starts = lax.dynamic_index_in_dim(doc_starts, core, 0, keepdims=False)
    other = swap_core(lax.dynamic_index_in_dim(tokens, 1 - core, 0, keepdims=False))
    cot_other = swap_core(lax.dynamic_index_in_dim(cotangent, 1 - core, 0, keepdims=False))
    cos_t, sin_t = rotary_rows(rows)
    pos = jnp.arange(rows, dtype=jnp.int32)
    start_row = jnp.max(jnp.where(starts[:, None] <= pos[None, :], starts[:, None], 0), 0, keepdims=True)
    gain_one = attn_gain.astype(f32)[None]
    gain_two = mlp_gain.astype(f32)[None]
    per_q = GROUPS * HD
    wqkv_t = jnp.concatenate(
        [
            part
            for g in range(KVH)
            for part in (
                wq[:, g * per_q : (g + 1) * per_q],
                wk[:, g * HD : (g + 1) * HD],
                wv[:, g * HD : (g + 1) * HD],
            )
        ],
        1,
    ).T
    unit = 16 * chips

    def half_rows(count):
        return -(-count // unit) * unit

    mlp_rows = half_rows(3 * width * inner // PARTS // 2 // 128)
    rest_rows = half_rows(width * (wqkv_t.shape[0] + w_out.shape[0]) // 2 // 128 + 2 * GAIN_ROWS)

    qn, kt, vn, soft, mixed_t, hidden, n2, n2t, g, gt = forward(
        place, skip, tokens, other, cotangent, cot_other, gain_one, wqkv_t, w_out, gain_two, cos_t, sin_t, start_row
    )
    sums, gn2 = hidden, hidden
    buffers = []
    for part in range(PARTS):
        extra = (tokens, other, hidden, gain_two, w_out, mixed_t) if part == PARTS - 1 else ()
        res = mlp_part(part, PARTS, mlp_rows, place, skip, n2, n2t, g, gt, wg, wu, wd, sums, gn2, extra)
        buffers += Summer(core, chips, part).run(res[-2], res[-1])
        if part < PARTS - 1:
            sums, gn2 = res[0], res[1]
        else:
            mixed_out, gh, dot_t, dop, delta, dw_out, dgain_two = res[:-2]
    parts = [back(g, 1, soft, qn, kt, vn, dot_t, dop, delta, cos_t, sin_t) for g in range(KVH)]
    dqkv = jnp.concatenate(parts, 0)
    grad_x, keep, send = last(
        rest_rows, place, skip, tokens, other, cotangent, cot_other, gh, dqkv, wqkv_t, gain_one, dw_out, dgain_two
    )
    own, got = Summer(core, chips, 2).run(keep, send)
    dwg, dwu, dwd = unpack_mlp(place, buffers, width, inner)
    dq, dk, dv, dwo, dgain_one, dgain_two = unpack_rest(
        place, own, got, (wq.shape, wk.shape, wv.shape, w_out.shape, (1, width), (1, width))
    )
    return (
        back_to_halves(core, place, mixed_out),
        back_to_halves(core, place, grad_x),
        dgain_one[0], dq, dk, dv, dwo, dgain_two[0], dwg, dwu, dwd,
    )


def solution(mesh):
    split = P("wide", "narrow", None)
    in_specs = (split, P("wide", None), P("wide"), split) + (P(),) * 9
    out_specs = (split, split) + (P(),) * 9
    return jax.shard_map(per_device, mesh=mesh, in_specs=in_specs, out_specs=out_specs, check_vma=False)
```

```python
import functools

import jax
import jax.numpy as jnp
import numpy as np
from jax import lax
from jax.experimental import pallas as pl
from jax.experimental.pallas import tpu as pltpu
from jax.sharding import PartitionSpec as P

HQ = 9
KVH = 3
HD = 64
GROUPS = HQ // KVH
PER = (GROUPS + 2) * HD
theta_base = 100000.0
eps_norm = 1e-05
masked_score = -1e30
BLOCK = 256
PARTS = 2
GAIN_ROWS = 16
VMEM = 56 * 2**20
f32 = jnp.float32
bf16 = jnp.bfloat16


def dot(a, b, ca=1, cb=0):
    return lax.dot_general(a, b, (((ca,), (cb,)), ((), ())), preferred_element_type=f32)


def turn(rows, cosine, sine, sign):
    half = HD // 2
    first, second = rows[:half], rows[half:]
    if sign > 0:
        return jnp.concatenate([first * cosine - second * sine, second * cosine + first * sine], 0)
    return jnp.concatenate([first * cosine + second * sine, second * cosine - first * sine], 0)


def lanes_up(count):
    return -(-count // 128) * 128


def full(shape):
    return pl.BlockSpec(shape, lambda *_: (0,) * len(shape))


def widen(matrix):
    extra = lanes_up(matrix.shape[1]) - matrix.shape[1]
    return jnp.concatenate([matrix, jnp.zeros((matrix.shape[0], extra), matrix.dtype)], 1)


def pack_blocks(target, spot, matrix):
    for k in range(matrix.shape[1] // 128):
        target[spot : spot + matrix.shape[0]] = matrix[:, k * 128 : (k + 1) * 128]
        spot += matrix.shape[0]
    return spot


def pack_thin(target, spot, h, matrix):
    rows = matrix.shape[0]
    quarter = rows // 4
    base = matrix.shape[1] // 128
    for k in range(h * base // 2, (h + 1) * base // 2):
        target[spot : spot + rows] = matrix[:, k * 128 : (k + 1) * 128]
        spot += rows
    left = matrix[2 * h * quarter : (2 * h + 1) * quarter, base * 128 :]
    right = matrix[(2 * h + 1) * quarter : (2 * h + 2) * quarter, base * 128 :]
    target[spot : spot + quarter] = jnp.concatenate([left, right], 1)
    return spot + quarter


def unpack_thin(target, first, second, spot):
    rows, width = target.shape
    quarter = rows // 4
    base = width // 128
    for h, source in enumerate((first, second)):
        at = spot
        for k in range(h * base // 2, (h + 1) * base // 2):
            target[:, k * 128 : (k + 1) * 128] = source[at : at + rows].astype(f32)
            at += rows
        last = source[at : at + quarter].astype(f32)
        target[2 * h * quarter : (2 * h + 1) * quarter, base * 128 :] = last[:, : width - base * 128]
        target[(2 * h + 1) * quarter : (2 * h + 2) * quarter, base * 128 :] = last[:, width - base * 128 :]


def prelude_kernel(wq_ref, wkt_ref, wvt_ref, w_out_ref, gain_one_ref, gain_two_ref, t_ref, n_ref, out_t_ref, g1_ref, g2_ref):
    q_cols = GROUPS * HD
    wqt = wq_ref[...].T
    for g in range(KVH):
        t_ref[g * PER : g * PER + q_cols] = wqt[g * q_cols : (g + 1) * q_cols]
        t_ref[g * PER + q_cols : g * PER + q_cols + HD] = wkt_ref[g * HD : (g + 1) * HD]
        t_ref[g * PER + q_cols + HD : (g + 1) * PER] = wvt_ref[g * HD : (g + 1) * HD]
    n_ref[...] = t_ref[...].T
    out_t_ref[...] = w_out_ref[...].T
    for source, target in ((gain_one_ref, g1_ref), (gain_two_ref, g2_ref)):
        target[...] = jnp.broadcast_to(source[...], (128, source.shape[1])).T


def prelude(wq, wkt, wvt, w_out, gain_one, gain_two):
    width = wq.shape[0]
    return pl.pallas_call(
        prelude_kernel,
        out_shape=[
            jax.ShapeDtypeStruct((KVH * PER, width), bf16),
            jax.ShapeDtypeStruct((width, KVH * PER), bf16),
            jax.ShapeDtypeStruct((width, w_out.shape[0]), bf16),
            jax.ShapeDtypeStruct((width, 128), f32),
            jax.ShapeDtypeStruct((width, 128), f32),
        ],
        compiler_params=pltpu.CompilerParams(vmem_limit_bytes=VMEM),
        name="prelude",
    )(wq, wkt, wvt, w_out, gain_one, gain_two)


def forward_kernel(
    place_ref, skip_ref, own_ref, other_ref, cot_own_ref, cot_other_ref,
    gain_one_ref, wqkv_ref, w_out_ref, gain_two_ref, cos_ref, sin_ref, start_ref,
    qn_ref, kt_ref, vn_ref, soft_ref, mixed_ref, hidden_ref, n1_ref, n2_ref, n2t_ref, g_ref, gt_ref,
    kn_all, vt_all, qt_ref,
):
    step = pl.program_id(0)
    mine = (step >= 2).astype(jnp.int32) == place_ref[0]
    x = jnp.where(mine, own_ref[0], other_ref[...]).astype(f32)
    cot = jnp.where(mine, cot_own_ref[0], cot_other_ref[...])
    g = jnp.where(skip_ref[0] == 1, jnp.zeros_like(cot), cot)
    gt_ref[...] = g
    g_ref[...] = g.T
    inverse = lax.rsqrt(jnp.mean(x * x, 0, keepdims=True) + eps_norm)
    n1 = (x * inverse * gain_one_ref[:, :1]).astype(bf16)
    n1_ref[...] = widen(n1.T)
    qkv = dot(wqkv_ref[...], n1)
    cosine, sine = cos_ref[...], sin_ref[...]
    zero = jnp.zeros((HD, BLOCK), bf16)
    here = pl.ds(pl.multiple_of(step * BLOCK, BLOCK), BLOCK)
    for group in range(KVH):
        for r in range(GROUPS):
            head = group * GROUPS + r
            base = group * PER + r * HD
            rows = (turn(qkv[base : base + HD], cosine, sine, 1) * (HD**-0.5)).astype(bf16)
            qt_ref[head * HD : (head + 1) * HD] = rows
            qn_ref[head] = jnp.concatenate([rows, zero], 0).T
        base = group * PER + GROUPS * HD
        rows = turn(qkv[base : base + HD], cosine, sine, 1).astype(bf16)
        kt_ref[group * HD : (group + 1) * HD] = rows
        kn_all[group, here] = rows.T
        rows = qkv[base + HD : base + 2 * HD].astype(bf16)
        vt_all[step, group * HD : (group + 1) * HD] = rows
        vn_ref[group] = rows.T

    start_row = start_ref[...]

    def attend(count):
        t = lax.broadcasted_iota(jnp.int32, (BLOCK, BLOCK), 0)
        s_pos = lax.broadcasted_iota(jnp.int32, (BLOCK, BLOCK), 1)

        def one_group(group, carry):
            for r in range(GROUPS):
                head = group * GROUPS + r
                rows = pl.ds(pl.multiple_of(head * HD, HD), HD)
                q = qt_ref[rows]
                scores = []
                for kb in range(count):
                    s = dot(kn_all[group, kb * BLOCK : (kb + 1) * BLOCK], q)
                    ok = t + kb * BLOCK >= start_row
                    if kb == count - 1:
                        ok = ok & (t <= s_pos)
                    scores.append(jnp.where(ok, s, masked_score))
                peak = scores[0].max(0, keepdims=True)
                for s in scores[1:]:
                    peak = jnp.maximum(peak, s.max(0, keepdims=True))
                exps = [jnp.exp(s - peak) for s in scores]
                total = exps[0].sum(0, keepdims=True)
                for e in exps[1:]:
                    total = total + e.sum(0, keepdims=True)
                scale = 1.0 / total
                out = None
                for kb in range(count):
                    p = (exps[kb] * scale).astype(bf16)
                    soft_ref[0, head, kb * BLOCK : (kb + 1) * BLOCK] = p
                    v = vt_all[kb, pl.ds(pl.multiple_of(group * HD, HD), HD)]
                    term = dot(v, p)
                    out = term if out is None else out + term
                mixed_ref[rows] = out.astype(bf16)
            return carry

        lax.fori_loop(0, KVH, one_group, 0)

    for count in range(1, 5):
        pl.when(step == count - 1)(lambda count=count: attend(count))

    hidden = x + dot(w_out_ref[...], mixed_ref[...])
    hidden_ref[...] = hidden
    inverse = lax.rsqrt(jnp.mean(hidden * hidden, 0, keepdims=True) + eps_norm)
    n2 = (hidden * inverse * gain_two_ref[:, :1]).astype(bf16)
    n2t_ref[...] = n2
    n2_ref[...] = n2.T


def own_specs(width, near):
    own = pl.BlockSpec((1, width, BLOCK), lambda i, c, s: (c[0], 0, jnp.where(i >= near, i - near, i)))
    oth = pl.BlockSpec((width, BLOCK), lambda i, c, s: (0, jnp.where(i >= near, i - near, i)))
    return own, oth


def out_specs_halves(width, near):
    mine = pl.BlockSpec((width, BLOCK), lambda i, c, s: (0, jnp.clip(i - near * c[0], 0, near - 1)))
    away = pl.BlockSpec((width, BLOCK), lambda i, c, s: (0, jnp.clip(i - near * (1 - c[0]), 0, near - 1)))
    return mine, away


def forward(place, skip, tokens, other, cot, cot_other, gain_one, wqkv_t, w_out_t, gain_two, cos_t, sin_t, start_row):
    rows = 2 * tokens.shape[2]
    width = tokens.shape[1]
    wide = lanes_up(width)
    blocks = rows // BLOCK
    own, oth = own_specs(width, blocks // 2)
    col = pl.BlockSpec((width, BLOCK), lambda i, c, s: (0, i))
    row = pl.BlockSpec((BLOCK, width), lambda i, c, s: (i, 0))
    row_wide = pl.BlockSpec((BLOCK, wide), lambda i, c, s: (i, 0))
    small = pl.BlockSpec((HD // 2, BLOCK), lambda i, c, s: (0, i))
    return pl.pallas_call(
        forward_kernel,
        grid_spec=pltpu.PrefetchScalarGridSpec(
            num_scalar_prefetch=2,
            grid=(blocks,),
            in_specs=[
                own, oth, own, oth, full((width, 128)), full(wqkv_t.shape), full(w_out_t.shape), full((width, 128)),
                small, small, pl.BlockSpec((1, BLOCK), lambda i, c, s: (0, i)),
            ],
            out_specs=[
                pl.BlockSpec((HQ, BLOCK, 2 * HD), lambda i, c, s: (0, i, 0)),
                pl.BlockSpec((KVH * HD, BLOCK), lambda i, c, s: (0, i)),
                pl.BlockSpec((KVH, BLOCK, HD), lambda i, c, s: (0, i, 0)),
                pl.BlockSpec((1, HQ, rows, BLOCK), lambda i, c, s: (i, 0, 0, 0)),
                pl.BlockSpec((HQ * HD, BLOCK), lambda i, c, s: (0, i)),
                col, row_wide, row, col, row, col,
            ],
            scratch_shapes=[
                pltpu.VMEM((KVH, rows, HD), bf16),
                pltpu.VMEM((blocks, KVH * HD, BLOCK), bf16),
                pltpu.VMEM((HQ * HD, BLOCK), bf16),
            ],
        ),
        out_shape=[
            jax.ShapeDtypeStruct((HQ, rows, 2 * HD), bf16),
            jax.ShapeDtypeStruct((KVH * HD, rows), bf16),
            jax.ShapeDtypeStruct((KVH, rows, HD), bf16),
            jax.ShapeDtypeStruct((blocks, HQ, rows, BLOCK), bf16),
            jax.ShapeDtypeStruct((HQ * HD, rows), bf16),
            jax.ShapeDtypeStruct((width, rows), f32),
            jax.ShapeDtypeStruct((rows, wide), bf16),
            jax.ShapeDtypeStruct((rows, width), bf16),
            jax.ShapeDtypeStruct((width, rows), bf16),
            jax.ShapeDtypeStruct((rows, width), bf16),
            jax.ShapeDtypeStruct((width, rows), bf16),
        ],
        compiler_params=pltpu.CompilerParams(vmem_limit_bytes=VMEM),
        name="attention_forward",
    )(place, skip, tokens, other, cot, cot_other, gain_one, wqkv_t, w_out_t, gain_two, cos_t, sin_t, start_row)


def mlp_kernel(
    final, place_ref, skip_ref, n2_ref, n2t_ref, g_ref, gt_ref, w_gate_ref, w_up_ref, w_down_ref, *refs,
):
    if final:
        (
            sum_ref, gn2_in_ref, own_ref, other_ref, hidden_ref, gain_two_ref, w_out_ref, mixed_ref,
            res_own_ref, res_away_ref, gh_ref, dot_ref, dop_ref, delta_ref, keep_ref, send_ref,
            inner_sc, grads_sc, in_t_sc, down_sc, ga_sc, dgain_sc,
        ) = refs
    else:
        (out_ref, gn2_ref, keep_ref, send_ref, inner_sc, grads_sc, in_t_sc, down_sc) = refs
    step = pl.program_id(0)
    width = n2t_ref.shape[0]
    cols = w_gate_ref.shape[1]
    half = cols // 2

    @pl.when(step == 0)
    def _():
        for k, ref in enumerate((w_gate_ref, w_up_ref)):
            in_t_sc[k * cols : (k + 1) * cols] = widen(ref[...].T)
        down_sc[...] = widen(w_down_ref[...].T)
        if final:
            dgain_sc[...] = jnp.zeros_like(dgain_sc)

    here = pl.ds(pl.multiple_of(step * BLOCK, BLOCK), BLOCK)
    n2 = n2_ref[...]
    g = g_ref[...]
    for c in range(0, cols, BLOCK):
        gate = dot(n2, w_gate_ref[:, c : c + BLOCK])
        up = dot(n2, w_up_ref[:, c : c + BLOCK])
        sig = jax.nn.sigmoid(gate)
        act = gate * sig
        inner_sc[here, c : c + BLOCK] = (act * up).astype(bf16)
        grad_inner = dot(g, w_down_ref[:, c : c + BLOCK])
        grads_sc[here, c : c + BLOCK] = (grad_inner * up * (sig + act * (1.0 - sig))).astype(bf16)
        grads_sc[here, cols + c : cols + c + BLOCK] = (grad_inner * act).astype(bf16)
    out = dot(inner_sc[here], down_sc[...])
    gn2 = dot(grads_sc[here], in_t_sc[...])
    if final:
        mine = (step >= 2).astype(jnp.int32) == place_ref[0]
        x = jnp.where(mine, own_ref[0], other_ref[...])
        skipped = skip_ref[0] == 1
        hidden = hidden_ref[...]
        result = hidden + (out + sum_ref[...]).T[:width]
        result = jnp.where(skipped, x, result.astype(bf16))

        @pl.when(mine)
        def _():
            res_own_ref[...] = result

        @pl.when(jnp.logical_not(mine))
        def _():
            res_away_ref[...] = result

        gn2 = (gn2 + gn2_in_ref[...]).T[:width]
        inverse = lax.rsqrt(jnp.mean(hidden * hidden, 0, keepdims=True) + eps_norm)
        c = gn2 * gain_two_ref[:, :1]
        normed = hidden * inverse
        dgain_sc[:, :1] += jnp.sum(gn2 * normed, 1, keepdims=True)
        gt = gt_ref[:, here]
        gh = gt.astype(f32) + inverse * (c - normed * jnp.mean(c * normed, 0, keepdims=True))
        gh_ref[...] = gh
        ga = gh.astype(bf16)
        ga_sc[here] = widen(ga.T)
        mixed = mixed_ref[:, here]
        back = dot(w_out_ref[...], ga).astype(bf16)
        dot_ref[...] = back
        zero = jnp.zeros((HD, BLOCK), bf16)
        for head in range(HQ):
            rows = back[head * HD : (head + 1) * HD]
            dop_ref[head] = jnp.concatenate([zero, rows], 0).T
            delta_ref[head // GROUPS, head % GROUPS : head % GROUPS + 1] = jnp.sum(
                rows.astype(f32) * mixed[head * HD : (head + 1) * HD].astype(f32), 0, keepdims=True
            )
    else:
        out_ref[...] = out
        gn2_ref[...] = gn2

    @pl.when(step == pl.num_programs(0) - 1)
    def _():
        if final:
            dw_out = dot(mixed_ref[...], ga_sc[...])[:, :width].astype(bf16)
            line = dgain_sc[...].T[0:1]
            line = jnp.concatenate([line, jnp.zeros((1, lanes_up(width) - width), f32)], 1)
            lines = [line[:, k * 128 : (k + 1) * 128] for k in range(line.shape[1] // 128)]
            lines.append(jnp.zeros((GAIN_ROWS - len(lines), 128), f32))
            gain_rows = jnp.concatenate(lines, 0).astype(bf16)
        for h in range(2):
            def emit(target):
                spot = 0
                for left, right, at in (
                    (n2t_ref, grads_sc, h * half),
                    (n2t_ref, grads_sc, cols + h * half),
                    (gt_ref, inner_sc, h * half),
                ):
                    spot = pack_blocks(target, spot, dot(left[...], right[:, at : at + half]).astype(bf16))
                if final:
                    spot = pack_thin(target, spot, h, dw_out)
                    target[spot : spot + GAIN_ROWS] = gain_rows
                    spot += GAIN_ROWS
                target[spot:] = jnp.zeros((target.shape[0] - spot, 128), bf16)

            pl.when(place_ref[0] == h)(lambda: emit(keep_ref))
            pl.when(place_ref[0] != h)(lambda: emit(send_ref))


def mlp_part(part, half_rows, place, skip, n2, n2t, g, gt, wg, wu, wdt, extra=()):
    final = part == PARTS - 1
    width, rows = n2t.shape
    wide = lanes_up(width)
    blocks = rows // BLOCK
    cols = wg.shape[1] // PARTS
    row = pl.BlockSpec((BLOCK, width), lambda i, c, s: (i, 0))
    row_wide = pl.BlockSpec((BLOCK, wide), lambda i, c, s: (i, 0))
    col = pl.BlockSpec((width, BLOCK), lambda i, c, s: (0, i))
    own, oth = own_specs(width, blocks // 2)
    weight = pl.BlockSpec((width, cols), lambda i, c, s: (0, part))
    in_specs = [row, full((width, rows)), row, full((width, rows)), weight, weight, weight]
    halves = [full((half_rows, 128))] * 2
    half_shapes = [jax.ShapeDtypeStruct((half_rows, 128), bf16)] * 2
    scratch = [
        pltpu.VMEM((rows, cols), bf16),
        pltpu.VMEM((rows, 2 * cols), bf16),
        pltpu.VMEM((2 * cols, wide), bf16),
        pltpu.VMEM((cols, wide), bf16),
    ]
    if final:
        in_specs += [row_wide, row_wide, own, oth, col, full((width, 128)), full((HQ * HD, width)), full((HQ * HD, rows))]
        out_specs = [
            *out_specs_halves(width, blocks // 2),
            col, col,
            pl.BlockSpec((HQ, BLOCK, 2 * HD), lambda i, c, s: (0, i, 0)),
            pl.BlockSpec((KVH, GROUPS, BLOCK), lambda i, c, s: (0, 0, i)),
        ] + halves
        out_shape = [
            jax.ShapeDtypeStruct((width, rows // 2), bf16),
            jax.ShapeDtypeStruct((width, rows // 2), bf16),
            jax.ShapeDtypeStruct((width, rows), f32),
            jax.ShapeDtypeStruct((HQ * HD, rows), bf16),
            jax.ShapeDtypeStruct((HQ, rows, 2 * HD), bf16),
            jax.ShapeDtypeStruct((KVH, GROUPS, rows), f32),
        ] + half_shapes
        scratch += [pltpu.VMEM((rows, wide), bf16), pltpu.VMEM((width, 128), f32)]
    else:
        out_specs = [row_wide, row_wide] + halves
        out_shape = [jax.ShapeDtypeStruct((rows, wide), f32)] * 2 + half_shapes
    return pl.pallas_call(
        functools.partial(mlp_kernel, final),
        grid_spec=pltpu.PrefetchScalarGridSpec(
            num_scalar_prefetch=2, grid=(blocks,), in_specs=in_specs, out_specs=out_specs, scratch_shapes=scratch
        ),
        out_shape=out_shape,
        compiler_params=pltpu.CompilerParams(vmem_limit_bytes=VMEM),
        name="mlp_both_ways",
    )(place, skip, n2, n2t, g, gt, wg, wu, wdt, *extra)


def back_kernel(
    soft_ref, qn_ref, kt_ref, vn_ref, dot_ref, dop_ref, delta_ref, cos_ref, sin_ref,
    dqkv_ref,
    acc,
):
    step = pl.program_id(0)
    cosine, sine = cos_ref[...], sin_ref[...]

    def attend(count):
        last = count - 1
        terms = [None] * count
        for r in range(GROUPS):
            up = dot_ref[r * HD : (r + 1) * HD]
            delta = delta_ref[0, r : r + 1]
            dq = None
            pads = jnp.concatenate([qn_ref[r], dop_ref[r]], 0)
            for kb in range(count):
                span = slice(kb * BLOCK, (kb + 1) * BLOCK)
                p = soft_ref[0, r, span]
                ds = (p.astype(f32) * (dot(vn_ref[0, span], up) - delta)).astype(bf16)
                term = dot(kt_ref[:, span], ds)
                dq = term if dq is None else dq + term
                kv = dot(jnp.concatenate([ds, p], 1), pads)
                terms[kb] = kv if terms[kb] is None else terms[kb] + kv
            dqkv_ref[r * HD : (r + 1) * HD] = turn(dq * (HD**-0.5), cosine, sine, -1).astype(bf16)
        for kb in range(count):
            span = slice(kb * BLOCK, (kb + 1) * BLOCK)
            total = terms[kb] if count == 4 else acc[span] + terms[kb]
            if kb < last:
                acc[span] = total
            else:
                done = total.T
                base = GROUPS * HD
                dqkv_ref[base : base + HD] = turn(done[:HD], cosine, sine, -1).astype(bf16)
                dqkv_ref[base + HD : base + 2 * HD] = done[HD:].astype(bf16)

    for count in range(1, 5):
        pl.when(step == 4 - count)(lambda count=count: attend(count))


def back(g, soft, qn, kt, vn, dot_t, dop, delta, cos_t, sin_t):
    blocks, _, rows, _ = soft.shape
    last = blocks - 1
    small = pl.BlockSpec((HD // 2, BLOCK), lambda i: (0, last - i))
    return pl.pallas_call(
        back_kernel,
        grid=(blocks,),
        in_specs=[
            pl.BlockSpec((1, GROUPS, rows, BLOCK), lambda i: (last - i, g, 0, 0)),
            pl.BlockSpec((GROUPS, BLOCK, 2 * HD), lambda i: (g, last - i, 0)),
            pl.BlockSpec((HD, rows), lambda i: (g, 0)),
            pl.BlockSpec((1, rows, HD), lambda i: (g, 0, 0)),
            pl.BlockSpec((GROUPS * HD, BLOCK), lambda i: (g, last - i)),
            pl.BlockSpec((GROUPS, BLOCK, 2 * HD), lambda i: (g, last - i, 0)),
            pl.BlockSpec((1, GROUPS, BLOCK), lambda i: (g, 0, last - i)),
            small, small,
        ],
        out_specs=pl.BlockSpec((PER, BLOCK), lambda i: (0, last - i)),
        out_shape=jax.ShapeDtypeStruct((PER, rows), bf16),
        scratch_shapes=[pltpu.VMEM((rows, 2 * HD), f32)],
        compiler_params=pltpu.CompilerParams(vmem_limit_bytes=VMEM),
        name="attention_backward",
    )(soft, qn, kt, vn, dot_t, dop, delta, cos_t, sin_t)


def weight_kernel(width, place_ref, d0_ref, d1_ref, d2_ref, n1_ref, keep_ref, send_ref):
    n1 = n1_ref[...]
    dw = jnp.concatenate([dot(ref[...], n1)[:, :width].astype(bf16) for ref in (d0_ref, d1_ref, d2_ref)], 0)

    def emit(h, target):
        spot = pack_thin(target, 0, h, dw)
        target[spot:] = jnp.zeros((target.shape[0] - spot, 128), bf16)

    for h in range(2):
        pl.when(place_ref[0] == h)(lambda h=h: emit(h, keep_ref))
        pl.when(place_ref[0] != h)(lambda h=h: emit(h, send_ref))


def weight(half_rows, width, place, parts, n1):
    return pl.pallas_call(
        functools.partial(weight_kernel, width),
        grid_spec=pltpu.PrefetchScalarGridSpec(
            num_scalar_prefetch=1,
            grid=(1,),
            in_specs=[full(part.shape) for part in parts] + [full(n1.shape)],
            out_specs=[full((half_rows, 128))] * 2,
        ),
        out_shape=[jax.ShapeDtypeStruct((half_rows, 128), bf16)] * 2,
        compiler_params=pltpu.CompilerParams(vmem_limit_bytes=VMEM),
        name="attention_weights",
    )(place, *parts, n1)


def last_kernel(
    place_ref, skip_ref, own_ref, other_ref, cot_own_ref, cot_other_ref, gh_ref, d0_ref, d1_ref, d2_ref,
    wqkv_ref, gain_one_ref,
    grad_own_ref, grad_away_ref,
):
    step = pl.program_id(0)
    mine = (step >= 2).astype(jnp.int32) == place_ref[0]
    x = jnp.where(mine, own_ref[0], other_ref[...]).astype(f32)
    cot = jnp.where(mine, cot_own_ref[0], cot_other_ref[...])
    skipped = skip_ref[0] == 1
    inverse = lax.rsqrt(jnp.mean(x * x, 0, keepdims=True) + eps_norm)
    normed = x * inverse
    dqkv = jnp.concatenate([d0_ref[...], d1_ref[...], d2_ref[...]], 0)
    c = dot(wqkv_ref[...], dqkv) * gain_one_ref[:, :1]
    gx = gh_ref[...] + inverse * (c - normed * jnp.mean(c * normed, 0, keepdims=True))
    gx = jnp.where(skipped, cot, gx.astype(bf16))

    @pl.when(mine)
    def _():
        grad_own_ref[...] = gx

    @pl.when(jnp.logical_not(mine))
    def _():
        grad_away_ref[...] = gx


def last(place, skip, tokens, other, cot, cot_other, gh, parts, wqkv_n, gain_one):
    width, rows = gh.shape
    blocks = rows // BLOCK
    own, oth = own_specs(width, blocks // 2)
    col = pl.BlockSpec((width, BLOCK), lambda i, c, s: (0, i))
    part = pl.BlockSpec((PER, BLOCK), lambda i, c, s: (0, i))
    return pl.pallas_call(
        last_kernel,
        grid_spec=pltpu.PrefetchScalarGridSpec(
            num_scalar_prefetch=2,
            grid=(blocks,),
            in_specs=[own, oth, own, oth, col, part, part, part, full(wqkv_n.shape), full((width, 128))],
            out_specs=[*out_specs_halves(width, blocks // 2)],
        ),
        out_shape=[jax.ShapeDtypeStruct((width, rows // 2), bf16)] * 2,
        compiler_params=pltpu.CompilerParams(vmem_limit_bytes=VMEM),
        name="input_backward",
    )(place, skip, tokens, other, cot, cot_other, gh, *parts, wqkv_n, gain_one)


def rotary_rows(rows):
    frequency = theta_base ** (-2.0 * np.arange(HD // 2, dtype=np.float64) / HD)
    angles = frequency[:, None] * np.arange(rows, dtype=np.float64)[None, :]
    return np.cos(angles).astype(np.float32), np.sin(angles).astype(np.float32)


def swap_core(array):
    return lax.ppermute(array, "narrow", [(0, 1), (1, 0)])


def axis_orders(bits, turn_index):
    if bits == 4:
        table = (((0, 1, 2, 3), (1, 2, 3, 0)), ((1, 0, 2, 3), (2, 3, 0, 1)), ((0, 1, 2, 3), (1, 2, 3, 0)))
        return table[turn_index]
    base = tuple(range(bits))
    shift = bits // 2
    return base, base[shift:] + base[:shift]


class Summer:
    def __init__(self, core, chips, turn_index):
        self.core = core
        self.chips = chips
        self.bits = chips.bit_length() - 1
        self.orders = axis_orders(self.bits, turn_index)
        self.place = lax.axis_index("wide")

    def bit(self, step):
        by_core = [(self.place >> order[step]) & 1 for order in self.orders]
        return jnp.where(self.core == 0, by_core[0], by_core[1])

    def swap(self, array, step):
        pairs = [
            (2 * chip + c, 2 * (chip ^ (1 << self.orders[c][step])) + c) for chip in range(self.chips) for c in range(2)
        ]
        return lax.ppermute(array, ("wide", "narrow"), pairs)

    def run(self, keep, send):
        got = swap_core(send)
        for step in range(self.bits):
            bit = self.bit(step)
            half = keep.shape[0] // 2

            def part(which):
                a = lax.dynamic_slice_in_dim(keep, which * half, half, 0).astype(f32)
                b = lax.dynamic_slice_in_dim(got, which * half, half, 0).astype(f32)
                return (a + b).astype(bf16)

            send = part(1 - bit)
            following = self.swap(send, step)
            keep, got = part(bit), following
        whole = (keep.astype(f32) + got.astype(f32)).astype(bf16)
        for step in reversed(range(self.bits)):
            got = self.swap(whole, step)
            whole = jnp.where(
                self.bit(step) == 0, jnp.concatenate([whole, got], 0), jnp.concatenate([got, whole], 0)
            )
        return whole, swap_core(whole)


def unpack_kernel(place_ref, a_own, a_got, b_own, b_got, gate_ref, up_ref, down_ref, w_out_ref, gain_ref):
    step = pl.program_id(0)
    width, cols = gate_ref.shape
    per = cols // 128
    for part, (own, got) in enumerate(((a_own, a_got), (b_own, b_got))):
        for h in range(2):
            def take(source):
                spot = 0
                for target in (gate_ref, up_ref, down_ref):
                    for k in range(per):
                        target[:, k * 128 : (k + 1) * 128] = source[spot : spot + width].astype(f32)
                        spot += width

            here = step == 2 * part + h
            pl.when(here & (place_ref[0] == h))(lambda own=own: take(own))
            pl.when(here & (place_ref[0] != h))(lambda got=got: take(got))

    @pl.when(step == 0)
    def _():
        def take_rest(first, second):
            spot = 3 * per * width
            unpack_thin(w_out_ref, first, second, spot)
            spot += width // 128 // 2 * width + width // 4
            rows = first[spot : spot + GAIN_ROWS].astype(f32)
            line = jnp.concatenate([rows[k : k + 1] for k in range(lanes_up(width) // 128)], 1)
            gain_ref[...] = line[:, :width]

        pl.when(place_ref[0] == 0)(lambda: take_rest(b_own, b_got))
        pl.when(place_ref[0] != 0)(lambda: take_rest(b_got, b_own))


def unpack(place, buffers, width, inner):
    cols = inner // 4
    spec = pl.BlockSpec((width, cols), lambda i, c: (0, i))
    return pl.pallas_call(
        unpack_kernel,
        grid_spec=pltpu.PrefetchScalarGridSpec(
            num_scalar_prefetch=1,
            grid=(4,),
            in_specs=[full(b.shape) for b in buffers],
            out_specs=[spec, spec, spec, full((HQ * HD, width)), full((1, width))],
        ),
        out_shape=[jax.ShapeDtypeStruct((width, inner), f32)] * 3
        + [jax.ShapeDtypeStruct((HQ * HD, width), f32), jax.ShapeDtypeStruct((1, width), f32)],
        compiler_params=pltpu.CompilerParams(vmem_limit_bytes=VMEM),
        name="unpack_mlp",
    )(place, *buffers)


def unpack_last_kernel(place_ref, own_ref, got_ref, wqkv_ref, gain_one_ref, dq_ref, dkt_ref, dvt_ref, gain_ref, all_sc):
    q_cols = GROUPS * HD

    def take(first, second):
        unpack_thin(all_sc, first, second, 0)

    pl.when(place_ref[0] == 0)(lambda: take(own_ref, got_ref))
    pl.when(place_ref[0] != 0)(lambda: take(got_ref, own_ref))
    both = all_sc[...]
    dq = []
    for g in range(KVH):
        dq.append(both[g * PER : g * PER + q_cols])
        dkt_ref[g * HD : (g + 1) * HD] = both[g * PER + q_cols : g * PER + q_cols + HD]
        dvt_ref[g * HD : (g + 1) * HD] = both[g * PER + q_cols + HD : (g + 1) * PER]
    dq_ref[...] = jnp.concatenate(dq, 0).T
    gain_ref[...] = jnp.sum(both * wqkv_ref[...].astype(f32), 0, keepdims=True) / gain_one_ref[...]


def unpack_last(place, own, got, wqkv_t, gain_one):
    width = wqkv_t.shape[1]
    shapes = [(width, HQ * HD), (KVH * HD, width), (KVH * HD, width), (1, width)]
    return pl.pallas_call(
        unpack_last_kernel,
        grid_spec=pltpu.PrefetchScalarGridSpec(
            num_scalar_prefetch=1,
            grid=(1,),
            in_specs=[full(own.shape)] * 2 + [full(wqkv_t.shape), full((1, width))],
            out_specs=[full(shape) for shape in shapes],
            scratch_shapes=[pltpu.VMEM(wqkv_t.shape, f32)],
        ),
        out_shape=[jax.ShapeDtypeStruct(shape, f32) for shape in shapes],
        compiler_params=pltpu.CompilerParams(vmem_limit_bytes=VMEM),
        name="unpack_attention",
    )(place, own, got, wqkv_t, gain_one)


def both_halves(core, own, away):
    got = swap_core(away)
    return jnp.where(core == 0, jnp.stack([own, got]), jnp.stack([got, own]))


def flip(array):
    return jnp.swapaxes(array, -1, -2)


def per_device(tokens, doc_starts, skip_flags, cotangent, attn_gain, wq, wk, wv, w_out, mlp_gain, wg, wu, wd):
    core = lax.axis_index("narrow")
    chips = lax.axis_size("wide")
    tokens, cotangent = flip(tokens), flip(cotangent)
    rows = 2 * tokens.shape[2]
    width = tokens.shape[1]
    inner = wg.shape[1]
    place = core.astype(jnp.int32).reshape(1)
    skip = lax.dynamic_slice_in_dim(skip_flags, core, 1, 0)
    starts = lax.dynamic_index_in_dim(doc_starts, core, 0, keepdims=False)
    other = swap_core(lax.dynamic_index_in_dim(tokens, 1 - core, 0, keepdims=False))
    cot_other = swap_core(lax.dynamic_index_in_dim(cotangent, 1 - core, 0, keepdims=False))
    cos_t, sin_t = rotary_rows(rows)
    pos = jnp.arange(rows, dtype=jnp.int32)
    start_row = jnp.max(jnp.where(starts[:, None] <= pos[None, :], starts[:, None], 0), 0, keepdims=True)
    gain_line = attn_gain.astype(f32)[None]
    wdt = flip(wd)
    wqkv_t, wqkv_n, w_out_t, gain_one, gain_two = prelude(
        wq, flip(wk), flip(wv), w_out, gain_line, mlp_gain.astype(f32)[None]
    )
    unit = 16 * chips

    def half_rows(count):
        return -(-count // unit) * unit

    mlp_rows = 3 * width * inner // PARTS // 2 // 128
    thin = width // 128 // 2
    out_rows = thin * HQ * HD + HQ * HD // 4 + GAIN_ROWS
    rest_rows = thin * KVH * PER + KVH * PER // 4

    qn, kt, vn, soft, mixed_t, hidden, n1, n2, n2t, g, gt = forward(
        place, skip, tokens, other, cotangent, cot_other, gain_one, wqkv_t, w_out_t, gain_two, cos_t, sin_t, start_row
    )
    sums, gn2, keep_a, send_a = mlp_part(0, half_rows(mlp_rows), place, skip, n2, n2t, g, gt, wg, wu, wdt)
    a_own, a_got = Summer(core, chips, 0).run(keep_a, send_a)
    res_own, res_away, gh, dot_t, dop, delta, keep_b, send_b = mlp_part(
        1, half_rows(mlp_rows + out_rows), place, skip, n2, n2t, g, gt, wg, wu, wdt,
        (sums, gn2, tokens, other, hidden, gain_two, w_out, mixed_t),
    )
    b_own, b_got = Summer(core, chips, 1).run(keep_b, send_b)
    parts = [back(g, soft, qn, kt, vn, dot_t, dop, delta, cos_t, sin_t) for g in range(KVH)]
    keep_c, send_c = weight(half_rows(rest_rows), width, place, parts, n1)
    c_own, c_got = Summer(core, chips, 2).run(keep_c, send_c)
    grad_own, grad_away = last(place, skip, tokens, other, cotangent, cot_other, gh, parts, wqkv_n, gain_one)
    dwg, dwu, dwdt, dwo, dgain_two = unpack(place, (a_own, a_got, b_own, b_got), width, inner)
    dq, dkt, dvt, dgain_one = unpack_last(place, c_own, c_got, wqkv_t, gain_line)
    return (
        flip(both_halves(core, res_own, res_away)),
        flip(both_halves(core, grad_own, grad_away)),
        dgain_one[0], dq, flip(dkt), flip(dvt), dwo, dgain_two[0], dwg, dwu, flip(dwdt),
    )


def solution(mesh):
    split = P("wide", "narrow", None)
    in_specs = (split, P("wide", None), P("wide"), split) + (P(),) * 9
    out_specs = (split, split) + (P(),) * 9
    return jax.shard_map(per_device, mesh=mesh, in_specs=in_specs, out_specs=out_specs, check_vma=False)
```

```python
import functools

import jax
import jax.numpy as jnp
import numpy as np
from jax import lax
from jax.experimental import pallas as pl
from jax.experimental.pallas import tpu as pltpu
from jax.sharding import PartitionSpec as P

HQ = 9
KVH = 3
HD = 64
GROUPS = HQ // KVH
PER = (GROUPS + 2) * HD
theta_base = 100000.0
eps_norm = 1e-05
masked_score = -1e30
BLOCK = 256
GAIN_ROWS = 16
VMEM = 60 * 2**20
f32 = jnp.float32
bf16 = jnp.bfloat16


def cost(microseconds):
    return pl.CostEstimate(flops=int(microseconds * 1.0e9), bytes_accessed=1024, transcendentals=0)


def dot(a, b, ca=1, cb=0):
    return lax.dot_general(a, b, (((ca,), (cb,)), ((), ())), preferred_element_type=f32)


def turn(rows, cosine, sine, sign):
    half = HD // 2
    first, second = rows[:half], rows[half:]
    if sign > 0:
        return jnp.concatenate([first * cosine - second * sine, second * cosine + first * sine], 0)
    return jnp.concatenate([first * cosine + second * sine, second * cosine - first * sine], 0)


def lanes_up(count):
    return -(-count // 128) * 128


ANY = pl.BlockSpec(memory_space=pl.ANY)


def without(kernel, inputs, after):
    return lambda *refs: kernel(*refs[:inputs], *refs[inputs + len(after) :])


def full(shape):
    return pl.BlockSpec(shape, lambda *_: (0,) * len(shape))


def widen(matrix):
    extra = lanes_up(matrix.shape[1]) - matrix.shape[1]
    return jnp.concatenate([matrix, jnp.zeros((matrix.shape[0], extra), matrix.dtype)], 1)


def pack_blocks(target, spot, matrix):
    for k in range(matrix.shape[1] // 128):
        target[spot : spot + matrix.shape[0]] = matrix[:, k * 128 : (k + 1) * 128]
        spot += matrix.shape[0]
    return spot


def pack_thin(target, spot, h, matrix):
    rows = matrix.shape[0]
    quarter = rows // 4
    base = matrix.shape[1] // 128
    for k in range(h * base // 2, (h + 1) * base // 2):
        target[spot : spot + rows] = matrix[:, k * 128 : (k + 1) * 128]
        spot += rows
    left = matrix[2 * h * quarter : (2 * h + 1) * quarter, base * 128 :]
    right = matrix[(2 * h + 1) * quarter : (2 * h + 2) * quarter, base * 128 :]
    target[spot : spot + quarter] = jnp.concatenate([left, right], 1)
    return spot + quarter


def unpack_thin(target, first, second, spot):
    rows, width = target.shape
    quarter = rows // 4
    base = width // 128
    for h, source in enumerate((first, second)):
        at = spot
        for k in range(h * base // 2, (h + 1) * base // 2):
            target[:, k * 128 : (k + 1) * 128] = source[at : at + rows].astype(f32)
            at += rows
        last = source[at : at + quarter].astype(f32)
        target[2 * h * quarter : (2 * h + 1) * quarter, base * 128 :] = last[:, : width - base * 128]
        target[(2 * h + 1) * quarter : (2 * h + 2) * quarter, base * 128 :] = last[:, width - base * 128 :]


def prelude_kernel(wq_ref, wkt_ref, wvt_ref, w_out_ref, gain_one_ref, gain_two_ref, t_ref, n_ref, out_t_ref, g1_ref, g2_ref):
    q_cols = GROUPS * HD
    wqt = wq_ref[...].T
    for g in range(KVH):
        t_ref[g * PER : g * PER + q_cols] = wqt[g * q_cols : (g + 1) * q_cols]
        t_ref[g * PER + q_cols : g * PER + q_cols + HD] = wkt_ref[g * HD : (g + 1) * HD]
        t_ref[g * PER + q_cols + HD : (g + 1) * PER] = wvt_ref[g * HD : (g + 1) * HD]
    n_ref[...] = t_ref[...].T
    out_t_ref[...] = w_out_ref[...].T
    for source, target in ((gain_one_ref, g1_ref), (gain_two_ref, g2_ref)):
        target[...] = jnp.broadcast_to(source[...], (128, source.shape[1])).T


def prelude(wq, wkt, wvt, w_out, gain_one, gain_two):
    width = wq.shape[0]
    return pl.pallas_call(
        prelude_kernel,
        out_shape=[
            jax.ShapeDtypeStruct((KVH * PER, width), bf16),
            jax.ShapeDtypeStruct((width, KVH * PER), bf16),
            jax.ShapeDtypeStruct((width, w_out.shape[0]), bf16),
            jax.ShapeDtypeStruct((width, 128), f32),
            jax.ShapeDtypeStruct((width, 128), f32),
        ],
        compiler_params=pltpu.CompilerParams(vmem_limit_bytes=VMEM),
        name="prelude",
        cost_estimate=cost(4),
    )(wq, wkt, wvt, w_out, gain_one, gain_two)


def layer_kernel(
    place_ref, skip_ref, own_ref, other_ref, cot_own_ref, cot_other_ref,
    gain_one_ref, wqkv_ref, w_out_t_ref, gain_two_ref, cos_ref, sin_ref, start_ref,
    w_out_ref, w_gate_hbm, w_up_hbm, w_down_hbm,
    qt_ref, kt_ref, vn_ref, soft_hbm, n1_ref,
    res_own_ref, res_away_ref, gh_ref, dot_ref, delta_ref, keep_a_hbm, send_a_hbm, keep_b_hbm, send_b_hbm,
    kn_all, vt_all, mixed_sc, n2t_sc, gt_sc, inner_sc, grads_sc, ga_sc, dgain_sc,
    scale_sc, soft_sc, w_gate_ref, w_up_ref, w_down_ref, pack_sc, weight_sem, soft_sem, pack_sem,
):
    step = pl.program_id(0)
    mine = (step >= 2).astype(jnp.int32) == place_ref[0]
    width = other_ref.shape[0]
    cols = w_gate_hbm.shape[1]

    weight_copies = [
        pltpu.make_async_copy(source, target, weight_sem.at[k])
        for k, (source, target) in enumerate(
            ((w_gate_hbm, w_gate_ref), (w_up_hbm, w_up_ref), (w_down_hbm, w_down_ref))
        )
    ]

    @pl.when(step == 0)
    def _():
        for copy in weight_copies:
            copy.start()
        dgain_sc[...] = jnp.zeros_like(dgain_sc)

    low = jnp.where(mine, own_ref[0], other_ref[...])
    x = low.astype(f32)
    cot = jnp.where(mine, cot_own_ref[0], cot_other_ref[...])
    g = jnp.where(skip_ref[0] == 1, jnp.zeros_like(cot), cot)
    gt_sc[step] = g
    inverse = lax.rsqrt(jnp.mean(x * x, 0, keepdims=True) + eps_norm)
    n1 = (x * inverse * gain_one_ref[:, :1]).astype(bf16)
    n1_ref[...] = widen(n1.T)
    qkv = dot(wqkv_ref[...], n1)
    cosine, sine = cos_ref[...], sin_ref[...]
    here = pl.ds(pl.multiple_of(step * BLOCK, BLOCK), BLOCK)
    for group in range(KVH):
        for r in range(GROUPS):
            head = group * GROUPS + r
            base = group * PER + r * HD
            rows = (turn(qkv[base : base + HD], cosine, sine, 1) * (HD**-0.5)).astype(bf16)
            qt_ref[head * HD : (head + 1) * HD] = rows
        base = group * PER + GROUPS * HD
        rows = turn(qkv[base : base + HD], cosine, sine, 1).astype(bf16)
        kt_ref[group * HD : (group + 1) * HD] = rows
        kn_all[group, here] = rows.T
        rows = qkv[base + HD : base + 2 * HD].astype(bf16)
        vt_all[step, group] = jnp.concatenate([rows, jnp.ones((16, BLOCK), bf16)], 0)
        vn_ref[group] = rows.T

    start_row = start_ref[...]

    def soft_copy(count):
        used = pl.ds(0, count * BLOCK)
        return pltpu.make_async_copy(soft_sc.at[:, used], soft_hbm.at[count - 1, :, used], soft_sem)

    def attend(count):
        t = lax.broadcasted_iota(jnp.int32, (BLOCK, BLOCK), 0)
        s_pos = lax.broadcasted_iota(jnp.int32, (BLOCK, BLOCK), 1)
        if count > 1:
            soft_copy(count - 1).wait()

        def one_group(group, carry):
            for r in range(GROUPS):
                head = group * GROUPS + r
                rows = pl.ds(pl.multiple_of(head * HD, HD), HD)
                q = qt_ref[rows]
                scores = []
                for kb in range(count):
                    s = dot(kn_all[group, kb * BLOCK : (kb + 1) * BLOCK], q)
                    ok = t + kb * BLOCK >= start_row
                    if kb == count - 1:
                        ok = ok & (t <= s_pos)
                    scores.append(jnp.where(ok, s, masked_score))
                peak = scores[0].max(0, keepdims=True)
                for s in scores[1:]:
                    peak = jnp.maximum(peak, s.max(0, keepdims=True))
                out = None
                for kb in range(count):
                    p = jnp.exp(scores[kb] - peak).astype(bf16)
                    soft_sc[head, kb * BLOCK : (kb + 1) * BLOCK] = p
                    term = dot(vt_all[kb, group], p)
                    out = term if out is None else out + term
                scale = 1.0 / out[HD : HD + 1]
                scale_sc[head] = jnp.broadcast_to(scale, scale_sc.shape[1:])
                mixed_sc[step, rows] = (out[:HD] * scale).astype(bf16)
            return carry

        lax.fori_loop(0, KVH, one_group, 0)
        soft_copy(count).start()

    for count in range(1, 5):
        pl.when(step == count - 1)(lambda count=count: attend(count))

    @pl.when(step == 0)
    def _():
        for copy in weight_copies:
            copy.wait()

    mixed = mixed_sc[step]
    hidden = x + dot(w_out_t_ref[...], mixed)
    inverse = lax.rsqrt(jnp.mean(hidden * hidden, 0, keepdims=True) + eps_norm)
    normed = hidden * inverse
    n2t = (normed * gain_two_ref[:, :1]).astype(bf16)
    n2t_sc[step] = n2t
    n2 = n2t.T
    gn = g.T

    def chunk(k, carry):
        for c in range(2):
            at = pl.ds(pl.multiple_of((2 * k + c) * BLOCK, BLOCK), BLOCK)
            at_up = pl.ds(pl.multiple_of(cols + (2 * k + c) * BLOCK, BLOCK), BLOCK)
            gate = dot(n2, w_gate_ref[:, at])
            up = dot(n2, w_up_ref[:, at])
            sig = jax.nn.sigmoid(gate)
            act = gate * sig
            inner_sc[here, at] = (act * up).astype(bf16)
            grad_inner = dot(gn, w_down_ref[:, at])
            grads_sc[here, at] = (grad_inner * up * (sig + act * (1.0 - sig))).astype(bf16)
            grads_sc[here, at_up] = (grad_inner * act).astype(bf16)
        return carry

    lax.fori_loop(0, cols // BLOCK // 2, chunk, 0)
    result = hidden + dot(w_down_ref[...], inner_sc[here], 1, 1)
    result = jnp.where(skip_ref[0] == 1, low, result.astype(bf16))

    @pl.when(mine)
    def _():
        res_own_ref[...] = result

    @pl.when(jnp.logical_not(mine))
    def _():
        res_away_ref[...] = result

    gn2 = dot(w_gate_ref[...], grads_sc[here, :cols], 1, 1) + dot(w_up_ref[...], grads_sc[here, cols:], 1, 1)
    c = gn2 * gain_two_ref[:, :1]
    dgain_sc[:, :1] += jnp.sum(gn2 * normed, 1, keepdims=True)
    gh = g.astype(f32) + inverse * (c - normed * jnp.mean(c * normed, 0, keepdims=True))
    gh_ref[...] = gh
    ga = gh.astype(bf16)
    ga_sc[here] = widen(ga.T)
    back_t = dot(w_out_ref[...], ga)
    for head in range(HQ):
        rows = (back_t[head * HD : (head + 1) * HD] * scale_sc[head, 0:1]).astype(bf16)
        dot_ref[head * HD : (head + 1) * HD] = rows
        delta_ref[head // GROUPS, head % GROUPS : head % GROUPS + 1] = jnp.sum(
            rows.astype(f32) * mixed[head * HD : (head + 1) * HD].astype(f32), 0, keepdims=True
        )

    @pl.when(step == pl.num_programs(0) - 1)
    def _():
        blocks = mixed_sc.shape[0]
        whole = lambda ref: jnp.concatenate([ref[k] for k in range(blocks)], 1)
        n2t_all, gt_all = whole(n2t_sc), whole(gt_sc)
        dw_out = dot(whole(mixed_sc), ga_sc[...])[:, :width].astype(bf16)
        line = dgain_sc[...].T[0:1]
        line = jnp.concatenate([line, jnp.zeros((1, lanes_up(width) - width), f32)], 1)
        lines = [line[:, k * 128 : (k + 1) * 128] for k in range(line.shape[1] // 128)]
        lines.append(jnp.zeros((GAIN_ROWS - len(lines), 128), f32))
        gain_rows = jnp.concatenate(lines, 0).astype(bf16)
        quarter = cols // 4
        thin = 3 * quarter // 128 * width
        for h in range(2):
            target = pack_sc.at[2 + h]
            spot = pack_thin(target, thin, h, dw_out)
            target[spot : spot + GAIN_ROWS] = gain_rows

        def one_quarter(k, carry):
            at = pl.ds(pl.multiple_of(k * quarter, 128), quarter)
            at_up = pl.ds(pl.multiple_of(cols + k * quarter, 128), quarter)
            target = pack_sc.at[k]
            spot = 0
            for left, right in (
                (n2t_all, grads_sc[:, at]),
                (n2t_all, grads_sc[:, at_up]),
                (gt_all, inner_sc[:, at]),
            ):
                spot = pack_blocks(target, spot, dot(left, right).astype(bf16))
            for q in range(4):
                keep, send = pack_copies[q]
                pl.when((k == q) & (place_ref[0] == q % 2))(keep.start)
                pl.when((k == q) & (place_ref[0] != q % 2))(send.start)
            return carry

        pack_copies = []
        for q in range(4):
            targets = (keep_a_hbm, send_a_hbm) if q < 2 else (keep_b_hbm, send_b_hbm)
            source = pack_sc.at[q, pl.ds(0, targets[0].shape[0])]
            pack_copies.append([pltpu.make_async_copy(source, target, pack_sem.at[q]) for target in targets])
        lax.fori_loop(0, 4, one_quarter, 0)
        for keep, _ in pack_copies:
            keep.wait()
        soft_copy(blocks).wait()


def own_specs(width, near):
    own = pl.BlockSpec((1, width, BLOCK), lambda i, c, s: (c[0], 0, jnp.where(i >= near, i - near, i)))
    oth = pl.BlockSpec((width, BLOCK), lambda i, c, s: (0, jnp.where(i >= near, i - near, i)))
    return own, oth


def out_specs_halves(width, near):
    mine = pl.BlockSpec((width, BLOCK), lambda i, c, s: (0, jnp.clip(i - near * c[0], 0, near - 1)))
    away = pl.BlockSpec((width, BLOCK), lambda i, c, s: (0, jnp.clip(i - near * (1 - c[0]), 0, near - 1)))
    return mine, away


def layer(
    rows_a, rows_b, place, skip, tokens, other, cot, cot_other, gain_one, wqkv_t, w_out_t, gain_two, cos_t, sin_t,
    start_row, w_out, wg, wu, wdt,
):
    rows = 2 * tokens.shape[2]
    width = tokens.shape[1]
    cols = wg.shape[1]
    wide = lanes_up(width)
    blocks = rows // BLOCK
    own, oth = own_specs(width, blocks // 2)
    col = pl.BlockSpec((width, BLOCK), lambda i, c, s: (0, i))
    row_wide = pl.BlockSpec((BLOCK, wide), lambda i, c, s: (i, 0))
    small = pl.BlockSpec((HD // 2, BLOCK), lambda i, c, s: (0, i))
    const = lambda array: pl.BlockSpec(
        array.shape, lambda *_: (0,) * array.ndim, pipeline_mode=pl.Buffered(1)
    )
    any_spec = pl.BlockSpec(memory_space=pl.ANY)
    halves = [(rows_a, 128), (rows_a, 128), (rows_b, 128), (rows_b, 128)]
    out_shape = [
        jax.ShapeDtypeStruct((HQ * HD, rows), bf16),
        jax.ShapeDtypeStruct((KVH * HD, rows), bf16),
        jax.ShapeDtypeStruct((KVH, rows, HD), bf16),
        jax.ShapeDtypeStruct((blocks, HQ, rows, BLOCK), bf16),
        jax.ShapeDtypeStruct((rows, wide), bf16),
        jax.ShapeDtypeStruct((width, rows // 2), bf16),
        jax.ShapeDtypeStruct((width, rows // 2), bf16),
        jax.ShapeDtypeStruct((width, rows), f32),
        jax.ShapeDtypeStruct((HQ * HD, rows), bf16),
        jax.ShapeDtypeStruct((KVH, GROUPS, rows), f32),
    ] + [jax.ShapeDtypeStruct(shape, bf16) for shape in halves]
    return pl.pallas_call(
        layer_kernel,
        grid_spec=pltpu.PrefetchScalarGridSpec(
            num_scalar_prefetch=2,
            grid=(blocks,),
            in_specs=[
                own, oth, own, oth, const(gain_one), const(wqkv_t), const(w_out_t), const(gain_two),
                small, small, pl.BlockSpec((1, BLOCK), lambda i, c, s: (0, i)),
                const(w_out), any_spec, any_spec, any_spec,
            ],
            out_specs=[
                col,
                pl.BlockSpec((KVH * HD, BLOCK), lambda i, c, s: (0, i)),
                pl.BlockSpec((KVH, BLOCK, HD), lambda i, c, s: (0, i, 0)),
                any_spec,
                row_wide,
                *out_specs_halves(width, blocks // 2),
                col, col,
                pl.BlockSpec((KVH, GROUPS, BLOCK), lambda i, c, s: (0, 0, i)),
            ] + [any_spec] * 4,
            scratch_shapes=[
                pltpu.VMEM((KVH, rows, HD), bf16),
                pltpu.VMEM((blocks, KVH, HD + 16, BLOCK), bf16),
                pltpu.VMEM((blocks, HQ * HD, BLOCK), bf16),
                pltpu.VMEM((blocks, width, BLOCK), bf16),
                pltpu.VMEM((blocks, width, BLOCK), bf16),
                pltpu.VMEM((rows, cols), bf16),
                pltpu.VMEM((rows, 2 * cols), bf16),
                pltpu.VMEM((rows, wide), bf16),
                pltpu.VMEM((width, 128), f32),
                pltpu.VMEM((HQ, 8, BLOCK), f32),
                pltpu.VMEM((HQ, rows, BLOCK), bf16),
                pltpu.VMEM(wg.shape, bf16),
                pltpu.VMEM(wu.shape, bf16),
                pltpu.VMEM(wdt.shape, bf16),
                pltpu.VMEM((4, rows_b, 128), bf16),
                pltpu.SemaphoreType.DMA((3,)),
                pltpu.SemaphoreType.DMA,
                pltpu.SemaphoreType.DMA((4,)),
            ],
        ),
        out_shape=out_shape,
        compiler_params=pltpu.CompilerParams(vmem_limit_bytes=VMEM),
        name="layer_forward",
        cost_estimate=cost(50),
    )(
        place, skip, tokens, other, cot, cot_other, gain_one, wqkv_t, w_out_t, gain_two, cos_t, sin_t, start_row,
        w_out, wg, wu, wdt,
    )


def back_kernel(
    soft_ref, qt_ref, kt_ref, vn_ref, dot_ref, delta_ref, cos_ref, sin_ref,
    dqkv_ref,
    acc,
):
    step = pl.program_id(0)
    cosine, sine = cos_ref[...], sin_ref[...]

    def attend(count):
        last = count - 1
        terms = [None] * count
        for r in range(GROUPS):
            up = dot_ref[r * HD : (r + 1) * HD]
            delta = delta_ref[0, r : r + 1]
            dq = None
            pair = jnp.concatenate([qt_ref[r * HD : (r + 1) * HD], up], 0).T
            left = lax.broadcasted_iota(jnp.int32, pair.shape, 1) < HD
            zero = jnp.zeros_like(pair)
            pads = jnp.concatenate([jnp.where(left, pair, zero), jnp.where(left, zero, pair)], 0)
            for kb in range(count):
                span = slice(kb * BLOCK, (kb + 1) * BLOCK)
                p = soft_ref[0, r, span]
                ds = (p.astype(f32) * (dot(vn_ref[0, span], up) - delta)).astype(bf16)
                term = dot(kt_ref[:, span], ds)
                dq = term if dq is None else dq + term
                kv = dot(jnp.concatenate([ds, p], 1), pads)
                terms[kb] = kv if terms[kb] is None else terms[kb] + kv
            dqkv_ref[r * HD : (r + 1) * HD] = turn(dq * (HD**-0.5), cosine, sine, -1).astype(bf16)
        for kb in range(count):
            span = slice(kb * BLOCK, (kb + 1) * BLOCK)
            total = terms[kb] if count == 4 else acc[span] + terms[kb]
            if kb < last:
                acc[span] = total
            else:
                done = total.T
                base = GROUPS * HD
                dqkv_ref[base : base + HD] = turn(done[:HD], cosine, sine, -1).astype(bf16)
                dqkv_ref[base + HD : base + 2 * HD] = done[HD:].astype(bf16)

    for count in range(1, 5):
        pl.when(step == 4 - count)(lambda count=count: attend(count))


def back(g, soft, qt, kt, vn, dot_t, delta, cos_t, sin_t, after=()):
    blocks, _, rows, _ = soft.shape
    last = blocks - 1
    small = pl.BlockSpec((HD // 2, BLOCK), lambda i: (0, last - i))
    return pl.pallas_call(
        without(back_kernel, 8, after),
        grid=(blocks,),
        in_specs=[
            pl.BlockSpec((1, GROUPS, rows, BLOCK), lambda i: (last - i, g, 0, 0)),
            pl.BlockSpec((GROUPS * HD, BLOCK), lambda i: (g, last - i)),
            pl.BlockSpec((HD, rows), lambda i: (g, 0)),
            pl.BlockSpec((1, rows, HD), lambda i: (g, 0, 0)),
            pl.BlockSpec((GROUPS * HD, BLOCK), lambda i: (g, last - i)),
            pl.BlockSpec((1, GROUPS, BLOCK), lambda i: (g, 0, last - i)),
            small, small,
        ] + [ANY] * len(after),
        out_specs=pl.BlockSpec((PER, BLOCK), lambda i: (0, last - i)),
        out_shape=jax.ShapeDtypeStruct((PER, rows), bf16),
        scratch_shapes=[pltpu.VMEM((rows, 2 * HD), f32)],
        compiler_params=pltpu.CompilerParams(vmem_limit_bytes=VMEM),
        name="attention_backward",
        cost_estimate=cost(9),
    )(soft, qt, kt, vn, dot_t, delta, cos_t, sin_t, *after)


def weight_kernel(width, place_ref, d0_ref, d1_ref, d2_ref, n1_ref, keep_ref, send_ref):
    n1 = n1_ref[...]
    dw = jnp.concatenate([dot(ref[...], n1)[:, :width].astype(bf16) for ref in (d0_ref, d1_ref, d2_ref)], 0)

    def emit(h, target):
        spot = pack_thin(target, 0, h, dw)
        target[spot:] = jnp.zeros((target.shape[0] - spot, 128), bf16)

    for h in range(2):
        pl.when(place_ref[0] == h)(lambda h=h: emit(h, keep_ref))
        pl.when(place_ref[0] != h)(lambda h=h: emit(h, send_ref))


def weight(half_rows, width, place, parts, n1, after=()):
    return pl.pallas_call(
        without(functools.partial(weight_kernel, width), 5, after),
        grid_spec=pltpu.PrefetchScalarGridSpec(
            num_scalar_prefetch=1,
            grid=(1,),
            in_specs=[full(part.shape) for part in parts] + [full(n1.shape)] + [ANY] * len(after),
            out_specs=[full((half_rows, 128))] * 2,
        ),
        out_shape=[jax.ShapeDtypeStruct((half_rows, 128), bf16)] * 2,
        compiler_params=pltpu.CompilerParams(vmem_limit_bytes=VMEM),
        name="attention_weights",
        cost_estimate=cost(4),
    )(place, *parts, n1, *after)


def last_kernel(
    place_ref, skip_ref, x_ref, cot_ref, gh_ref, d0_ref, d1_ref, d2_ref, wqkv_ref, gain_one_ref, grad_ref,
):
    x = x_ref[...].reshape(gh_ref.shape).astype(f32)
    skipped = skip_ref[0] == 1
    inverse = lax.rsqrt(jnp.mean(x * x, 0, keepdims=True) + eps_norm)
    normed = x * inverse
    dqkv = jnp.concatenate([d0_ref[...], d1_ref[...], d2_ref[...]], 0)
    c = dot(wqkv_ref[...], dqkv) * gain_one_ref[:, :1]
    gx = gh_ref[...] + inverse * (c - normed * jnp.mean(c * normed, 0, keepdims=True))
    grad_ref[...] = jnp.where(skipped, cot_ref[...].reshape(gh_ref.shape), gx.astype(bf16))


def last(mine, place, skip, x, cot, gh, parts, wqkv_n, gain_one, after=()):
    width, rows = gh.shape
    near = rows // BLOCK // 2
    if mine:
        source = pl.BlockSpec((1, width, BLOCK), lambda i, c, s: (c[0], 0, i))
        at = lambda i, c, s: (0, near * c[0] + i)
    else:
        source = pl.BlockSpec((width, BLOCK), lambda i, c, s: (0, i))
        at = lambda i, c, s: (0, near * (1 - c[0]) + i)
    col = pl.BlockSpec((width, BLOCK), at)
    part = pl.BlockSpec((PER, BLOCK), at)
    return pl.pallas_call(
        without(last_kernel, 10, after),
        grid_spec=pltpu.PrefetchScalarGridSpec(
            num_scalar_prefetch=2,
            grid=(near,),
            in_specs=[source, source, col, part, part, part, full(wqkv_n.shape), full((width, 128))]
            + [ANY] * len(after),
            out_specs=pl.BlockSpec((width, BLOCK), lambda i, c, s: (0, i)),
        ),
        out_shape=jax.ShapeDtypeStruct((width, rows // 2), bf16),
        compiler_params=pltpu.CompilerParams(vmem_limit_bytes=VMEM),
        name="input_backward",
        cost_estimate=cost(4),
    )(place, skip, x, cot, gh, *parts, wqkv_n, gain_one, *after)


def rotary_rows(rows):
    frequency = theta_base ** (-2.0 * np.arange(HD // 2, dtype=np.float64) / HD)
    angles = frequency[:, None] * np.arange(rows, dtype=np.float64)[None, :]
    return np.cos(angles).astype(np.float32), np.sin(angles).astype(np.float32)


def swap_core(array):
    return lax.ppermute(array, "narrow", [(0, 1), (1, 0)])


def axis_orders(bits, turn_index):
    if bits == 4:
        table = (((0, 1, 2, 3), (1, 2, 3, 0)), ((1, 0, 2, 3), (2, 3, 0, 1)), ((0, 1, 2, 3), (1, 2, 3, 0)))
        return table[turn_index]
    base = tuple(range(bits))
    shift = bits // 2
    return base, base[shift:] + base[:shift]


class Summer:
    def __init__(self, core, chips, turn_index):
        self.core = core
        self.chips = chips
        self.bits = chips.bit_length() - 1
        self.orders = axis_orders(self.bits, turn_index)
        self.place = lax.axis_index("wide")

    def bit(self, step):
        by_core = [(self.place >> order[step]) & 1 for order in self.orders]
        return jnp.where(self.core == 0, by_core[0], by_core[1])

    def swap(self, array, step):
        pairs = [
            (2 * chip + c, 2 * (chip ^ (1 << self.orders[c][step])) + c) for chip in range(self.chips) for c in range(2)
        ]
        return lax.ppermute(array, ("wide", "narrow"), pairs)

    def first(self, keep, send):
        self.keep, self.got, self.step = keep, swap_core(send), 0

    def halve(self):
        bit = self.bit(self.step)
        half = self.keep.shape[0] // 2

        def part(which):
            a = lax.dynamic_slice_in_dim(self.keep, which * half, half, 0).astype(f32)
            b = lax.dynamic_slice_in_dim(self.got, which * half, half, 0).astype(f32)
            return (a + b).astype(bf16)

        send = part(1 - bit)
        following = self.swap(send, self.step)
        self.keep, self.got, self.step = part(bit), following, self.step + 1
        return send

    def middle(self):
        self.keep = (self.keep.astype(f32) + self.got.astype(f32)).astype(bf16)
        self.got = self.swap(self.keep, self.step - 1)
        return self.keep

    def double(self):
        self.step -= 1
        low = self.bit(self.step) == 0
        self.keep = jnp.where(
            low, jnp.concatenate([self.keep, self.got], 0), jnp.concatenate([self.got, self.keep], 0)
        )
        if self.step:
            self.got = self.swap(self.keep, self.step - 1)
        return self.keep

    def finish(self):
        while self.step < self.bits:
            self.halve()
        self.middle()
        while self.step:
            self.double()
        return self.keep, swap_core(self.keep)


def unpack_kernel(place_ref, a_own, a_got, b_own, b_got, gate_ref, up_ref, down_ref, w_out_ref, gain_ref):
    step = pl.program_id(0)
    width, cols = gate_ref.shape
    per = cols // 128
    for part, (own, got) in enumerate(((a_own, a_got), (b_own, b_got))):
        for h in range(2):
            def take(source):
                spot = 0
                for target in (gate_ref, up_ref, down_ref):
                    for k in range(per):
                        target[:, k * 128 : (k + 1) * 128] = source[spot : spot + width].astype(f32)
                        spot += width

            here = step == 2 * part + h
            pl.when(here & (place_ref[0] == h))(lambda own=own: take(own))
            pl.when(here & (place_ref[0] != h))(lambda got=got: take(got))

    @pl.when(step == 0)
    def _():
        def take_rest(first, second):
            spot = 3 * per * width
            unpack_thin(w_out_ref, first, second, spot)
            spot += width // 128 // 2 * width + width // 4
            rows = first[spot : spot + GAIN_ROWS].astype(f32)
            line = jnp.concatenate([rows[k : k + 1] for k in range(lanes_up(width) // 128)], 1)
            gain_ref[...] = line[:, :width]

        pl.when(place_ref[0] == 0)(lambda: take_rest(b_own, b_got))
        pl.when(place_ref[0] != 0)(lambda: take_rest(b_got, b_own))


def unpack(place, buffers, width, inner):
    cols = inner // 4
    spec = pl.BlockSpec((width, cols), lambda i, c: (0, i))
    return pl.pallas_call(
        unpack_kernel,
        grid_spec=pltpu.PrefetchScalarGridSpec(
            num_scalar_prefetch=1,
            grid=(4,),
            in_specs=[full(b.shape) for b in buffers],
            out_specs=[spec, spec, spec, full((HQ * HD, width)), full((1, width))],
        ),
        out_shape=[jax.ShapeDtypeStruct((width, inner), f32)] * 3
        + [jax.ShapeDtypeStruct((HQ * HD, width), f32), jax.ShapeDtypeStruct((1, width), f32)],
        compiler_params=pltpu.CompilerParams(vmem_limit_bytes=VMEM),
        name="unpack_mlp",
        cost_estimate=cost(7),
    )(place, *buffers)


def unpack_last_kernel(place_ref, own_ref, got_ref, wqkv_ref, gain_one_ref, dq_ref, dkt_ref, dvt_ref, gain_ref, all_sc):
    q_cols = GROUPS * HD

    def take(first, second):
        unpack_thin(all_sc, first, second, 0)

    pl.when(place_ref[0] == 0)(lambda: take(own_ref, got_ref))
    pl.when(place_ref[0] != 0)(lambda: take(got_ref, own_ref))
    both = all_sc[...]
    dq = []
    for g in range(KVH):
        dq.append(both[g * PER : g * PER + q_cols])
        dkt_ref[g * HD : (g + 1) * HD] = both[g * PER + q_cols : g * PER + q_cols + HD]
        dvt_ref[g * HD : (g + 1) * HD] = both[g * PER + q_cols + HD : (g + 1) * PER]
    dq_ref[...] = jnp.concatenate(dq, 0).T
    gain_ref[...] = jnp.sum(both * wqkv_ref[...].astype(f32), 0, keepdims=True) / gain_one_ref[...]


def unpack_last(place, own, got, wqkv_t, gain_one):
    width = wqkv_t.shape[1]
    shapes = [(width, HQ * HD), (KVH * HD, width), (KVH * HD, width), (1, width)]
    return pl.pallas_call(
        unpack_last_kernel,
        grid_spec=pltpu.PrefetchScalarGridSpec(
            num_scalar_prefetch=1,
            grid=(1,),
            in_specs=[full(own.shape)] * 2 + [full(wqkv_t.shape), full((1, width))],
            out_specs=[full(shape) for shape in shapes],
            scratch_shapes=[pltpu.VMEM(wqkv_t.shape, f32)],
        ),
        out_shape=[jax.ShapeDtypeStruct(shape, f32) for shape in shapes],
        compiler_params=pltpu.CompilerParams(vmem_limit_bytes=VMEM),
        name="unpack_attention",
        cost_estimate=cost(3),
    )(place, own, got, wqkv_t, gain_one)


def both_halves(core, own, away):
    got = swap_core(away)
    return jnp.where(core == 0, jnp.stack([own, got]), jnp.stack([got, own]))


def flip(array):
    return jnp.swapaxes(array, -1, -2)


def per_device(tokens, doc_starts, skip_flags, cotangent, attn_gain, wq, wk, wv, w_out, mlp_gain, wg, wu, wd):
    core = lax.axis_index("narrow")
    chips = lax.axis_size("wide")
    tokens, cotangent = flip(tokens), flip(cotangent)
    rows = 2 * tokens.shape[2]
    width = tokens.shape[1]
    inner = wg.shape[1]
    place = core.astype(jnp.int32).reshape(1)
    skip = lax.dynamic_slice_in_dim(skip_flags, core, 1, 0)
    starts = lax.dynamic_index_in_dim(doc_starts, core, 0, keepdims=False)
    other = swap_core(lax.dynamic_index_in_dim(tokens, 1 - core, 0, keepdims=False))
    cot_other = swap_core(lax.dynamic_index_in_dim(cotangent, 1 - core, 0, keepdims=False))
    cos_t, sin_t = rotary_rows(rows)
    pos = jnp.arange(rows, dtype=jnp.int32)
    start_row = jnp.max(jnp.where(starts[:, None] <= pos[None, :], starts[:, None], 0), 0, keepdims=True)
    gain_line = attn_gain.astype(f32)[None]
    wdt = flip(wd)
    wqkv_t, wqkv_n, w_out_t, gain_one, gain_two = prelude(
        wq, flip(wk), flip(wv), w_out, gain_line, mlp_gain.astype(f32)[None]
    )
    unit = 16 * chips

    def half_rows(count):
        return -(-count // unit) * unit

    mlp_rows = 3 * width * inner // 4 // 128
    thin = width // 128 // 2
    out_rows = thin * HQ * HD + HQ * HD // 4 + GAIN_ROWS
    rest_rows = thin * KVH * PER + KVH * PER // 4

    (
        qt, kt, vn, soft, n1, res_own, res_away, gh, dot_t, delta, keep_a, send_a, keep_b, send_b,
    ) = layer(
        half_rows(mlp_rows), half_rows(mlp_rows + out_rows),
        place, skip, tokens, other, cotangent, cot_other, gain_one, wqkv_t, w_out_t, gain_two, cos_t, sin_t,
        start_row, w_out, wg, wu, wdt,
    )
    a_sum, b_sum, c_sum = (Summer(core, chips, k) for k in range(3))
    a_sum.first(keep_a, send_a)
    b_sum.first(keep_b, send_b)
    parts = []
    after = ()
    for g in range(KVH):
        parts.append(back(g, soft, qt, kt, vn, dot_t, delta, cos_t, sin_t, after))
        after = (a_sum.halve(), b_sum.halve())
    keep_c, send_c = weight(half_rows(rest_rows), width, place, parts, n1, after)
    c_sum.first(keep_c, send_c)
    grad_away = last(False, place, skip, other, cot_other, gh, parts, wqkv_n, gain_one)
    after = (c_sum.halve(),)
    grad_own = last(True, place, skip, tokens, cotangent, gh, parts, wqkv_n, gain_one, after)
    c_own, c_got = c_sum.finish()
    a_own, a_got = a_sum.finish()
    b_own, b_got = b_sum.finish()
    dwg, dwu, dwdt, dwo, dgain_two = unpack(place, (a_own, a_got, b_own, b_got), width, inner)
    dq, dkt, dvt, dgain_one = unpack_last(place, c_own, c_got, wqkv_t, gain_line)
    return (
        flip(both_halves(core, res_own, res_away)),
        flip(both_halves(core, grad_own, grad_away)),
        dgain_one[0], dq, flip(dkt), flip(dvt), dwo, dgain_two[0], dwg, dwu, flip(dwdt),
    )


def solution(mesh):
    split = P("wide", "narrow", None)
    in_specs = (split, P("wide", None), P("wide"), split) + (P(),) * 9
    out_specs = (split, split) + (P(),) * 9
    return jax.shard_map(per_device, mesh=mesh, in_specs=in_specs, out_specs=out_specs, check_vma=False)
```

```python
import functools

import jax
import jax.numpy as jnp
import numpy as np
from jax import lax
from jax.experimental import pallas as pl
from jax.experimental.pallas import tpu as pltpu
from jax.sharding import PartitionSpec as P

HQ = 9
KVH = 3
HD = 64
GROUPS = HQ // KVH
PER = (GROUPS + 2) * HD
theta_base = 100000.0
eps_norm = 1e-05
masked_score = -1e30
BLOCK = 256
GAIN_ROWS = 16
VMEM = 60 * 2**20
f32 = jnp.float32
bf16 = jnp.bfloat16


def cost(microseconds):
    return pl.CostEstimate(flops=int(microseconds * 1.0e9), bytes_accessed=1024, transcendentals=0)


def dot(a, b, ca=1, cb=0):
    return lax.dot_general(a, b, (((ca,), (cb,)), ((), ())), preferred_element_type=f32)


def turn(rows, cosine, sine, sign):
    half = HD // 2
    first, second = rows[:half], rows[half:]
    if sign > 0:
        return jnp.concatenate([first * cosine - second * sine, second * cosine + first * sine], 0)
    return jnp.concatenate([first * cosine + second * sine, second * cosine - first * sine], 0)


def lanes_up(count):
    return -(-count // 128) * 128


ANY = pl.BlockSpec(memory_space=pl.ANY)


def without(kernel, inputs, after):
    return lambda *refs: kernel(*refs[:inputs], *refs[inputs + len(after) :])


def full(shape):
    return pl.BlockSpec(shape, lambda *_: (0,) * len(shape))


def widen(matrix):
    extra = lanes_up(matrix.shape[1]) - matrix.shape[1]
    return jnp.concatenate([matrix, jnp.zeros((matrix.shape[0], extra), matrix.dtype)], 1)


def pack_blocks(target, spot, matrix):
    for k in range(matrix.shape[1] // 128):
        target[spot : spot + matrix.shape[0]] = matrix[:, k * 128 : (k + 1) * 128]
        spot += matrix.shape[0]
    return spot


def pack_thin(target, spot, h, matrix):
    rows = matrix.shape[0]
    quarter = rows // 4
    base = matrix.shape[1] // 128
    for k in range(h * base // 2, (h + 1) * base // 2):
        target[spot : spot + rows] = matrix[:, k * 128 : (k + 1) * 128]
        spot += rows
    left = matrix[2 * h * quarter : (2 * h + 1) * quarter, base * 128 :]
    right = matrix[(2 * h + 1) * quarter : (2 * h + 2) * quarter, base * 128 :]
    target[spot : spot + quarter] = jnp.concatenate([left, right], 1)
    return spot + quarter


def unpack_thin(target, first, second, spot):
    rows, width = target.shape
    quarter = rows // 4
    base = width // 128
    for h, source in enumerate((first, second)):
        at = spot
        for k in range(h * base // 2, (h + 1) * base // 2):
            target[:, k * 128 : (k + 1) * 128] = source[at : at + rows].astype(f32)
            at += rows
        last = source[at : at + quarter].astype(f32)
        target[2 * h * quarter : (2 * h + 1) * quarter, base * 128 :] = last[:, : width - base * 128]
        target[(2 * h + 1) * quarter : (2 * h + 2) * quarter, base * 128 :] = last[:, width - base * 128 :]


def prelude_kernel(wq_ref, wkt_ref, wvt_ref, w_out_ref, gain_one_ref, gain_two_ref, t_ref, n_ref, out_t_ref, g1_ref, g2_ref):
    q_cols = GROUPS * HD
    wqt = wq_ref[...].T
    for g in range(KVH):
        t_ref[g * PER : g * PER + q_cols] = wqt[g * q_cols : (g + 1) * q_cols]
        t_ref[g * PER + q_cols : g * PER + q_cols + HD] = wkt_ref[g * HD : (g + 1) * HD]
        t_ref[g * PER + q_cols + HD : (g + 1) * PER] = wvt_ref[g * HD : (g + 1) * HD]
    n_ref[...] = t_ref[...].T
    out_t_ref[...] = w_out_ref[...].T
    for source, target in ((gain_one_ref, g1_ref), (gain_two_ref, g2_ref)):
        target[...] = jnp.broadcast_to(source[...], (128, source.shape[1])).T


def prelude(wq, wkt, wvt, w_out, gain_one, gain_two):
    width = wq.shape[0]
    return pl.pallas_call(
        prelude_kernel,
        out_shape=[
            jax.ShapeDtypeStruct((KVH * PER, width), bf16),
            jax.ShapeDtypeStruct((width, KVH * PER), bf16),
            jax.ShapeDtypeStruct((width, w_out.shape[0]), bf16),
            jax.ShapeDtypeStruct((width, 128), f32),
            jax.ShapeDtypeStruct((width, 128), f32),
        ],
        compiler_params=pltpu.CompilerParams(vmem_limit_bytes=VMEM),
        name="prelude",
        cost_estimate=cost(4),
    )(wq, wkt, wvt, w_out, gain_one, gain_two)


def layer_kernel(
    place_ref, skip_ref, own_ref, other_ref, cot_own_ref, cot_other_ref,
    gain_one_ref, wqkv_ref, w_out_t_ref, gain_two_ref, cos_ref, sin_ref, start_ref,
    w_out_ref, w_gate_hbm, w_up_hbm, w_down_hbm,
    qt_ref, kt_ref, vn_ref, soft_hbm, n1_ref,
    res_own_ref, res_away_ref, gh_ref, dot_ref, delta_ref, keep_a_hbm, send_a_hbm, keep_b_hbm, send_b_hbm,
    kn_all, vt_all, mixed_sc, n2t_sc, gt_sc, inner_sc, grads_sc, in_t_sc, down_sc, ga_sc, dgain_sc,
    scale_sc, soft_sc, w_gate_ref, w_up_ref, w_down_ref, pack_sc, weight_sem, soft_sem, pack_sem,
):
    step = pl.program_id(0)
    mine = (step >= 2).astype(jnp.int32) == place_ref[0]
    width = other_ref.shape[0]
    cols = w_gate_hbm.shape[1]

    weight_copies = [
        pltpu.make_async_copy(source, target, weight_sem.at[k])
        for k, (source, target) in enumerate(
            ((w_gate_hbm, w_gate_ref), (w_up_hbm, w_up_ref), (w_down_hbm, w_down_ref))
        )
    ]

    @pl.when(step == 0)
    def _():
        for copy in weight_copies:
            copy.start()
        dgain_sc[...] = jnp.zeros_like(dgain_sc)

    low = jnp.where(mine, own_ref[0], other_ref[...])
    x = low.astype(f32)
    cot = jnp.where(mine, cot_own_ref[0], cot_other_ref[...])
    g = jnp.where(skip_ref[0] == 1, jnp.zeros_like(cot), cot)
    gt_sc[step] = g
    inverse = lax.rsqrt(jnp.mean(x * x, 0, keepdims=True) + eps_norm)
    n1 = (x * inverse * gain_one_ref[:, :1]).astype(bf16)
    n1_ref[...] = widen(n1.T)
    qkv = dot(wqkv_ref[...], n1)
    cosine, sine = cos_ref[...], sin_ref[...]
    here = pl.ds(pl.multiple_of(step * BLOCK, BLOCK), BLOCK)
    for group in range(KVH):
        for r in range(GROUPS):
            head = group * GROUPS + r
            base = group * PER + r * HD
            rows = (turn(qkv[base : base + HD], cosine, sine, 1) * (HD**-0.5)).astype(bf16)
            qt_ref[head * HD : (head + 1) * HD] = rows
        base = group * PER + GROUPS * HD
        rows = turn(qkv[base : base + HD], cosine, sine, 1).astype(bf16)
        kt_ref[group * HD : (group + 1) * HD] = rows
        kn_all[group, here] = rows.T
        rows = qkv[base + HD : base + 2 * HD].astype(bf16)
        vt_all[step, group] = jnp.concatenate([rows, jnp.ones((16, BLOCK), bf16)], 0)
        vn_ref[group] = rows.T

    start_row = start_ref[...]

    def soft_copy(count):
        used = pl.ds(0, count * BLOCK)
        return pltpu.make_async_copy(soft_sc.at[:, used], soft_hbm.at[count - 1, :, used], soft_sem)

    def attend(count):
        t = lax.broadcasted_iota(jnp.int32, (BLOCK, BLOCK), 0)
        s_pos = lax.broadcasted_iota(jnp.int32, (BLOCK, BLOCK), 1)
        if count > 1:
            soft_copy(count - 1).wait()

        def one_group(group, carry):
            def scores_of(r):
                rows = pl.ds(pl.multiple_of((group * GROUPS + r) * HD, HD), HD)
                q = qt_ref[rows]
                scores = []
                for kb in range(count):
                    s = dot(kn_all[group, kb * BLOCK : (kb + 1) * BLOCK], q)
                    ok = t + kb * BLOCK >= start_row
                    if kb == count - 1:
                        ok = ok & (t <= s_pos)
                    scores.append(jnp.where(ok, s, masked_score))
                return scores

            def finish(r, scores):
                head = group * GROUPS + r
                rows = pl.ds(pl.multiple_of(head * HD, HD), HD)
                peak = scores[0].max(0, keepdims=True)
                for s in scores[1:]:
                    peak = jnp.maximum(peak, s.max(0, keepdims=True))
                out = None
                for kb in range(count):
                    p = jnp.exp(scores[kb] - peak).astype(bf16)
                    soft_sc[head, kb * BLOCK : (kb + 1) * BLOCK] = p
                    term = dot(vt_all[kb, group], p)
                    out = term if out is None else out + term
                scale = 1.0 / out[HD : HD + 1]
                scale_sc[head] = jnp.broadcast_to(scale, scale_sc.shape[1:])
                mixed_sc[step, rows] = (out[:HD] * scale).astype(bf16)

            every = [scores_of(r) for r in range(GROUPS)]
            for r in range(GROUPS):
                finish(r, every[r])
            return carry

        lax.fori_loop(0, KVH, one_group, 0)
        soft_copy(count).start()

    for count in range(1, 5):
        pl.when(step == count - 1)(lambda count=count: attend(count))

    @pl.when(step == 0)
    def _():
        for copy in weight_copies:
            copy.wait()
        for k, ref in enumerate((w_gate_ref, w_up_ref)):
            in_t_sc[k * cols : (k + 1) * cols] = widen(ref[...].T)
        down_sc[...] = widen(w_down_ref[...].T)

    mixed = mixed_sc[step]
    hidden = x + dot(w_out_t_ref[...], mixed)
    inverse = lax.rsqrt(jnp.mean(hidden * hidden, 0, keepdims=True) + eps_norm)
    normed = hidden * inverse
    n2t = (normed * gain_two_ref[:, :1]).astype(bf16)
    n2t_sc[step] = n2t
    n2 = n2t.T
    gn = g.T

    def chunk(k, carry):
        work = []
        for c in range(3):
            at = pl.ds(pl.multiple_of((3 * k + c) * BLOCK, BLOCK), BLOCK)
            at_up = pl.ds(pl.multiple_of(cols + (3 * k + c) * BLOCK, BLOCK), BLOCK)
            work.append((at, at_up, dot(n2, w_gate_ref[:, at]), dot(n2, w_up_ref[:, at]), dot(gn, w_down_ref[:, at])))
        for at, at_up, gate, up, grad_inner in work:
            sig = jax.nn.sigmoid(gate)
            act = gate * sig
            inner_sc[here, at] = (act * up).astype(bf16)
            grads_sc[here, at] = (grad_inner * up * (sig + act * (1.0 - sig))).astype(bf16)
            grads_sc[here, at_up] = (grad_inner * act).astype(bf16)
        return carry

    lax.fori_loop(0, cols // BLOCK // 3, chunk, 0)
    result = hidden + dot(inner_sc[here], down_sc[...]).T[:width]
    result = jnp.where(skip_ref[0] == 1, low, result.astype(bf16))

    @pl.when(mine)
    def _():
        res_own_ref[...] = result

    @pl.when(jnp.logical_not(mine))
    def _():
        res_away_ref[...] = result

    gn2 = dot(grads_sc[here], in_t_sc[...]).T[:width]
    c = gn2 * gain_two_ref[:, :1]
    dgain_sc[:, :1] += jnp.sum(gn2 * normed, 1, keepdims=True)
    gh = g.astype(f32) + inverse * (c - normed * jnp.mean(c * normed, 0, keepdims=True))
    gh_ref[...] = gh
    ga = gh.astype(bf16)
    ga_sc[here] = widen(ga.T)
    back_t = dot(w_out_ref[...], ga)
    for head in range(HQ):
        rows = (back_t[head * HD : (head + 1) * HD] * scale_sc[head, 0:1]).astype(bf16)
        dot_ref[head * HD : (head + 1) * HD] = rows
        delta_ref[head // GROUPS, head % GROUPS : head % GROUPS + 1] = jnp.sum(
            rows.astype(f32) * mixed[head * HD : (head + 1) * HD].astype(f32), 0, keepdims=True
        )

    @pl.when(step == pl.num_programs(0) - 1)
    def _():
        blocks = mixed_sc.shape[0]
        whole = lambda ref: jnp.concatenate([ref[k] for k in range(blocks)], 1)
        n2t_all, gt_all = whole(n2t_sc), whole(gt_sc)
        dw_out = dot(whole(mixed_sc), ga_sc[...])[:, :width].astype(bf16)
        line = dgain_sc[...].T[0:1]
        line = jnp.concatenate([line, jnp.zeros((1, lanes_up(width) - width), f32)], 1)
        lines = [line[:, k * 128 : (k + 1) * 128] for k in range(line.shape[1] // 128)]
        lines.append(jnp.zeros((GAIN_ROWS - len(lines), 128), f32))
        gain_rows = jnp.concatenate(lines, 0).astype(bf16)
        quarter = cols // 4
        thin = 3 * quarter // 128 * width
        for h in range(2):
            target = pack_sc.at[2 + h]
            spot = pack_thin(target, thin, h, dw_out)
            target[spot : spot + GAIN_ROWS] = gain_rows

        def one_quarter(k, carry):
            at = pl.ds(pl.multiple_of(k * quarter, 128), quarter)
            at_up = pl.ds(pl.multiple_of(cols + k * quarter, 128), quarter)
            target = pack_sc.at[k]
            spot = 0
            for left, right in (
                (n2t_all, grads_sc[:, at]),
                (n2t_all, grads_sc[:, at_up]),
                (gt_all, inner_sc[:, at]),
            ):
                spot = pack_blocks(target, spot, dot(left, right).astype(bf16))
            for q in range(4):
                keep, send = pack_copies[q]
                pl.when((k == q) & (place_ref[0] == q % 2))(keep.start)
                pl.when((k == q) & (place_ref[0] != q % 2))(send.start)
            return carry

        pack_copies = []
        for q in range(4):
            targets = (keep_a_hbm, send_a_hbm) if q < 2 else (keep_b_hbm, send_b_hbm)
            source = pack_sc.at[q, pl.ds(0, targets[0].shape[0])]
            pack_copies.append([pltpu.make_async_copy(source, target, pack_sem.at[q]) for target in targets])
        lax.fori_loop(0, 4, one_quarter, 0)
        for keep, _ in pack_copies:
            keep.wait()
        soft_copy(blocks).wait()


def own_specs(width, near):
    own = pl.BlockSpec((1, width, BLOCK), lambda i, c, s: (c[0], 0, jnp.where(i >= near, i - near, i)))
    oth = pl.BlockSpec((width, BLOCK), lambda i, c, s: (0, jnp.where(i >= near, i - near, i)))
    return own, oth


def out_specs_halves(width, near):
    mine = pl.BlockSpec((width, BLOCK), lambda i, c, s: (0, jnp.clip(i - near * c[0], 0, near - 1)))
    away = pl.BlockSpec((width, BLOCK), lambda i, c, s: (0, jnp.clip(i - near * (1 - c[0]), 0, near - 1)))
    return mine, away


def layer(
    rows_a, rows_b, place, skip, tokens, other, cot, cot_other, gain_one, wqkv_t, w_out_t, gain_two, cos_t, sin_t,
    start_row, w_out, wg, wu, wdt,
):
    rows = 2 * tokens.shape[2]
    width = tokens.shape[1]
    cols = wg.shape[1]
    wide = lanes_up(width)
    blocks = rows // BLOCK
    own, oth = own_specs(width, blocks // 2)
    col = pl.BlockSpec((width, BLOCK), lambda i, c, s: (0, i))
    row_wide = pl.BlockSpec((BLOCK, wide), lambda i, c, s: (i, 0))
    small = pl.BlockSpec((HD // 2, BLOCK), lambda i, c, s: (0, i))
    const = lambda array: pl.BlockSpec(
        array.shape, lambda *_: (0,) * array.ndim, pipeline_mode=pl.Buffered(1)
    )
    any_spec = pl.BlockSpec(memory_space=pl.ANY)
    halves = [(rows_a, 128), (rows_a, 128), (rows_b, 128), (rows_b, 128)]
    out_shape = [
        jax.ShapeDtypeStruct((HQ * HD, rows), bf16),
        jax.ShapeDtypeStruct((KVH * HD, rows), bf16),
        jax.ShapeDtypeStruct((KVH, rows, HD), bf16),
        jax.ShapeDtypeStruct((blocks, HQ, rows, BLOCK), bf16),
        jax.ShapeDtypeStruct((rows, wide), bf16),
        jax.ShapeDtypeStruct((width, rows // 2), bf16),
        jax.ShapeDtypeStruct((width, rows // 2), bf16),
        jax.ShapeDtypeStruct((width, rows), f32),
        jax.ShapeDtypeStruct((HQ * HD, rows), bf16),
        jax.ShapeDtypeStruct((KVH, GROUPS, rows), f32),
    ] + [jax.ShapeDtypeStruct(shape, bf16) for shape in halves]
    return pl.pallas_call(
        layer_kernel,
        grid_spec=pltpu.PrefetchScalarGridSpec(
            num_scalar_prefetch=2,
            grid=(blocks,),
            in_specs=[
                own, oth, own, oth, const(gain_one), const(wqkv_t), const(w_out_t), const(gain_two),
                small, small, pl.BlockSpec((1, BLOCK), lambda i, c, s: (0, i)),
                const(w_out), any_spec, any_spec, any_spec,
            ],
            out_specs=[
                col,
                pl.BlockSpec((KVH * HD, BLOCK), lambda i, c, s: (0, i)),
                pl.BlockSpec((KVH, BLOCK, HD), lambda i, c, s: (0, i, 0)),
                any_spec,
                row_wide,
                *out_specs_halves(width, blocks // 2),
                col, col,
                pl.BlockSpec((KVH, GROUPS, BLOCK), lambda i, c, s: (0, 0, i)),
            ] + [any_spec] * 4,
            scratch_shapes=[
                pltpu.VMEM((KVH, rows, HD), bf16),
                pltpu.VMEM((blocks, KVH, HD + 16, BLOCK), bf16),
                pltpu.VMEM((blocks, HQ * HD, BLOCK), bf16),
                pltpu.VMEM((blocks, width, BLOCK), bf16),
                pltpu.VMEM((blocks, width, BLOCK), bf16),
                pltpu.VMEM((rows, cols), bf16),
                pltpu.VMEM((rows, 2 * cols), bf16),
                pltpu.VMEM((2 * cols, wide), bf16),
                pltpu.VMEM((cols, wide), bf16),
                pltpu.VMEM((rows, wide), bf16),
                pltpu.VMEM((width, 128), f32),
                pltpu.VMEM((HQ, 8, BLOCK), f32),
                pltpu.VMEM((HQ, rows, BLOCK), bf16),
                pltpu.VMEM(wg.shape, bf16),
                pltpu.VMEM(wu.shape, bf16),
                pltpu.VMEM(wdt.shape, bf16),
                pltpu.VMEM((4, rows_b, 128), bf16),
                pltpu.SemaphoreType.DMA((3,)),
                pltpu.SemaphoreType.DMA,
                pltpu.SemaphoreType.DMA((4,)),
            ],
        ),
        out_shape=out_shape,
        compiler_params=pltpu.CompilerParams(vmem_limit_bytes=VMEM),
        name="layer_forward",
        cost_estimate=cost(50),
    )(
        place, skip, tokens, other, cot, cot_other, gain_one, wqkv_t, w_out_t, gain_two, cos_t, sin_t, start_row,
        w_out, wg, wu, wdt,
    )


def back_kernel(
    soft_ref, qt_ref, kt_ref, vn_ref, dot_ref, delta_ref, cos_ref, sin_ref,
    dqkv_ref,
    acc, ds_sc,
):
    step = pl.program_id(0)
    cosine, sine = cos_ref[...], sin_ref[...]

    @pl.when(step == 0)
    def _():
        acc[...] = jnp.zeros_like(acc)

    def attend(count):
        last = count - 1
        used = slice(0, count * BLOCK)

        work = []
        for r in range(GROUPS):
            rows = slice(r * HD, (r + 1) * HD)
            up = dot_ref[rows]
            work.append([dot(vn_ref[0, kb * BLOCK : (kb + 1) * BLOCK], up) for kb in range(count)])
        for r in range(GROUPS):
            rows = slice(r * HD, (r + 1) * HD)
            up = dot_ref[rows]
            delta = delta_ref[0, r : r + 1]
            pair = jnp.concatenate([qt_ref[rows], up], 0).T
            left = lax.broadcasted_iota(jnp.int32, pair.shape, 1) < HD
            zero = jnp.zeros_like(pair)
            pads = jnp.concatenate([jnp.where(left, pair, zero), jnp.where(left, zero, pair)], 0)
            for kb in range(count):
                span = slice(kb * BLOCK, (kb + 1) * BLOCK)
                p = soft_ref[0, r, span]
                ds_sc[r, span, :BLOCK] = (p.astype(f32) * (work[r][kb] - delta)).astype(bf16)
                ds_sc[r, span, BLOCK:] = p
            acc[used] += dot(ds_sc[r, used], pads)
            dq = dot(kt_ref[:, used], ds_sc[r, used, :BLOCK])
            dqkv_ref[rows] = turn(dq * (HD**-0.5), cosine, sine, -1).astype(bf16)

        done = acc[last * BLOCK : count * BLOCK].T
        base = GROUPS * HD
        dqkv_ref[base : base + HD] = turn(done[:HD], cosine, sine, -1).astype(bf16)
        dqkv_ref[base + HD : base + 2 * HD] = done[HD:].astype(bf16)

    for count in range(1, 5):
        pl.when(step == 4 - count)(lambda count=count: attend(count))


def back(g, soft, qt, kt, vn, dot_t, delta, cos_t, sin_t, after=()):
    blocks, _, rows, _ = soft.shape
    last = blocks - 1
    small = pl.BlockSpec((HD // 2, BLOCK), lambda i: (0, last - i))
    return pl.pallas_call(
        without(back_kernel, 8, after),
        grid=(blocks,),
        in_specs=[
            pl.BlockSpec((1, GROUPS, rows, BLOCK), lambda i: (last - i, g, 0, 0)),
            pl.BlockSpec((GROUPS * HD, BLOCK), lambda i: (g, last - i)),
            pl.BlockSpec((HD, rows), lambda i: (g, 0)),
            pl.BlockSpec((1, rows, HD), lambda i: (g, 0, 0)),
            pl.BlockSpec((GROUPS * HD, BLOCK), lambda i: (g, last - i)),
            pl.BlockSpec((1, GROUPS, BLOCK), lambda i: (g, 0, last - i)),
            small, small,
        ] + [ANY] * len(after),
        out_specs=pl.BlockSpec((PER, BLOCK), lambda i: (0, last - i)),
        out_shape=jax.ShapeDtypeStruct((PER, rows), bf16),
        scratch_shapes=[pltpu.VMEM((rows, 2 * HD), f32), pltpu.VMEM((GROUPS, rows, 2 * BLOCK), bf16)],
        compiler_params=pltpu.CompilerParams(vmem_limit_bytes=VMEM),
        name="attention_backward",
        cost_estimate=cost(9),
    )(soft, qt, kt, vn, dot_t, delta, cos_t, sin_t, *after)


def weight_kernel(width, place_ref, d0_ref, d1_ref, d2_ref, n1_ref, keep_ref, send_ref):
    n1 = n1_ref[...]
    dw = jnp.concatenate([dot(ref[...], n1)[:, :width].astype(bf16) for ref in (d0_ref, d1_ref, d2_ref)], 0)

    def emit(h, target):
        spot = pack_thin(target, 0, h, dw)
        target[spot:] = jnp.zeros((target.shape[0] - spot, 128), bf16)

    for h in range(2):
        pl.when(place_ref[0] == h)(lambda h=h: emit(h, keep_ref))
        pl.when(place_ref[0] != h)(lambda h=h: emit(h, send_ref))


def weight(half_rows, width, place, parts, n1, after=()):
    return pl.pallas_call(
        without(functools.partial(weight_kernel, width), 5, after),
        grid_spec=pltpu.PrefetchScalarGridSpec(
            num_scalar_prefetch=1,
            grid=(1,),
            in_specs=[full(part.shape) for part in parts] + [full(n1.shape)] + [ANY] * len(after),
            out_specs=[full((half_rows, 128))] * 2,
        ),
        out_shape=[jax.ShapeDtypeStruct((half_rows, 128), bf16)] * 2,
        compiler_params=pltpu.CompilerParams(vmem_limit_bytes=VMEM),
        name="attention_weights",
        cost_estimate=cost(4),
    )(place, *parts, n1, *after)


def last_kernel(
    place_ref, skip_ref, x_ref, cot_ref, gh_ref, d0_ref, d1_ref, d2_ref, wqkv_ref, gain_one_ref, grad_ref,
):
    x = x_ref[...].reshape(gh_ref.shape).astype(f32)
    skipped = skip_ref[0] == 1
    inverse = lax.rsqrt(jnp.mean(x * x, 0, keepdims=True) + eps_norm)
    normed = x * inverse
    dqkv = jnp.concatenate([d0_ref[...], d1_ref[...], d2_ref[...]], 0)
    c = dot(wqkv_ref[...], dqkv) * gain_one_ref[:, :1]
    gx = gh_ref[...] + inverse * (c - normed * jnp.mean(c * normed, 0, keepdims=True))
    grad_ref[...] = jnp.where(skipped, cot_ref[...].reshape(gh_ref.shape), gx.astype(bf16))


def last(mine, place, skip, x, cot, gh, parts, wqkv_n, gain_one, after=()):
    width, rows = gh.shape
    near = rows // BLOCK // 2
    if mine:
        source = pl.BlockSpec((1, width, BLOCK), lambda i, c, s: (c[0], 0, i))
        at = lambda i, c, s: (0, near * c[0] + i)
    else:
        source = pl.BlockSpec((width, BLOCK), lambda i, c, s: (0, i))
        at = lambda i, c, s: (0, near * (1 - c[0]) + i)
    col = pl.BlockSpec((width, BLOCK), at)
    part = pl.BlockSpec((PER, BLOCK), at)
    return pl.pallas_call(
        without(last_kernel, 10, after),
        grid_spec=pltpu.PrefetchScalarGridSpec(
            num_scalar_prefetch=2,
            grid=(near,),
            in_specs=[source, source, col, part, part, part, full(wqkv_n.shape), full((width, 128))]
            + [ANY] * len(after),
            out_specs=pl.BlockSpec((width, BLOCK), lambda i, c, s: (0, i)),
        ),
        out_shape=jax.ShapeDtypeStruct((width, rows // 2), bf16),
        compiler_params=pltpu.CompilerParams(vmem_limit_bytes=VMEM),
        name="input_backward",
        cost_estimate=cost(4),
    )(place, skip, x, cot, gh, *parts, wqkv_n, gain_one, *after)


def rotary_rows(rows):
    frequency = theta_base ** (-2.0 * np.arange(HD // 2, dtype=np.float64) / HD)
    angles = frequency[:, None] * np.arange(rows, dtype=np.float64)[None, :]
    return np.cos(angles).astype(np.float32), np.sin(angles).astype(np.float32)


def swap_core(array):
    return lax.ppermute(array, "narrow", [(0, 1), (1, 0)])


def axis_orders(bits, turn_index):
    if bits == 4:
        table = (((0, 1, 2, 3), (1, 2, 3, 0)), ((1, 0, 2, 3), (2, 3, 0, 1)), ((0, 1, 2, 3), (1, 2, 3, 0)))
        return table[turn_index]
    base = tuple(range(bits))
    shift = bits // 2
    return base, base[shift:] + base[:shift]


class Summer:
    def __init__(self, core, chips, turn_index):
        self.core = core
        self.chips = chips
        self.bits = chips.bit_length() - 1
        self.orders = axis_orders(self.bits, turn_index)
        self.place = lax.axis_index("wide")

    def bit(self, step):
        by_core = [(self.place >> order[step]) & 1 for order in self.orders]
        return jnp.where(self.core == 0, by_core[0], by_core[1])

    def swap(self, array, step):
        pairs = [
            (2 * chip + c, 2 * (chip ^ (1 << self.orders[c][step])) + c) for chip in range(self.chips) for c in range(2)
        ]
        return lax.ppermute(array, ("wide", "narrow"), pairs)

    def first(self, keep, send):
        self.keep, self.got, self.step = keep, swap_core(send), 0

    def tie(self, line):
        if line.last is not None:
            self.keep, self.got, _ = lax.optimization_barrier((self.keep, self.got, line.last))

    def halve(self, line):
        self.tie(line)
        bit = self.bit(self.step)
        half = self.keep.shape[0] // 2

        def part(which):
            a = lax.dynamic_slice_in_dim(self.keep, which * half, half, 0).astype(f32)
            b = lax.dynamic_slice_in_dim(self.got, which * half, half, 0).astype(f32)
            return (a + b).astype(bf16)

        line.last = part(1 - bit)
        following = self.swap(line.last, self.step)
        self.keep, self.got, self.step = part(bit), following, self.step + 1

    def middle(self, line):
        self.tie(line)
        self.keep = (self.keep.astype(f32) + self.got.astype(f32)).astype(bf16)
        self.got = self.swap(self.keep, self.step - 1)
        line.last = self.keep

    def double(self, line):
        self.tie(line)
        self.step -= 1
        low = self.bit(self.step) == 0
        self.keep = jnp.where(
            low, jnp.concatenate([self.keep, self.got], 0), jnp.concatenate([self.got, self.keep], 0)
        )
        self.got = self.swap(self.keep, self.step - 1) if self.step else swap_core(self.keep)
        line.last = self.keep


class Line:
    last = None

    def after(self):
        return () if self.last is None else (self.last,)

    def both_halves(self, core, own, got):
        own, got, _ = lax.optimization_barrier((own, got, self.last))
        self.last = jnp.where(core == 0, jnp.stack([own, got]), jnp.stack([got, own]))
        return self.last


def unpack_kernel(chain, place_ref, own, got, *refs):
    gate_ref, up_ref, down_ref = refs[-5:-2] if chain else refs
    step = pl.program_id(0)
    width, cols = gate_ref.shape
    per = cols // 128

    def take(source):
        spot = 0
        for target in (gate_ref, up_ref, down_ref):
            for k in range(per):
                target[:, k * 128 : (k + 1) * 128] = source[spot : spot + width].astype(f32)
                spot += width

    pl.when(place_ref[0] == step)(lambda: take(own))
    pl.when(place_ref[0] != step)(lambda: take(got))

    if chain:
        w_out_ref, gain_ref = refs[-2:]

        def take_rest(first, second):
            spot = 3 * per * width
            unpack_thin(w_out_ref, first, second, spot)
            spot += width // 128 // 2 * width + width // 4
            rows = first[spot : spot + GAIN_ROWS].astype(f32)
            line = jnp.concatenate([rows[k : k + 1] for k in range(lanes_up(width) // 128)], 1)
            gain_ref[...] = line[:, :width].reshape(width)

        pl.when((step == 0) & (place_ref[0] == 0))(lambda: take_rest(own, got))
        pl.when((step == 0) & (place_ref[0] != 0))(lambda: take_rest(got, own))


def unpack(chain, place, buffers, width, inner, earlier):
    cols = inner // 4
    spec = pl.BlockSpec((width, cols), lambda i, c: (0, 2 * chain + i))
    out_specs = [spec, spec, spec]
    out_shape = [jax.ShapeDtypeStruct((width, inner), f32)] * 3
    if chain:
        out_specs += [full((HQ * HD, width)), full((width,))]
        out_shape += [jax.ShapeDtypeStruct((HQ * HD, width), f32), jax.ShapeDtypeStruct((width,), f32)]
    return pl.pallas_call(
        functools.partial(unpack_kernel, chain),
        grid_spec=pltpu.PrefetchScalarGridSpec(
            num_scalar_prefetch=1,
            grid=(2,),
            in_specs=[full(b.shape) for b in buffers] + [ANY] * len(earlier),
            out_specs=out_specs,
        ),
        out_shape=out_shape,
        input_output_aliases={3 + k: k for k in range(len(earlier))},
        compiler_params=pltpu.CompilerParams(vmem_limit_bytes=VMEM),
        name="unpack_mlp",
        cost_estimate=cost(4),
    )(place, *buffers, *earlier)


def unpack_last_kernel(place_ref, own_ref, got_ref, wqkv_ref, gain_one_ref, dq_ref, dkt_ref, dvt_ref, gain_ref, all_sc):
    q_cols = GROUPS * HD

    def take(first, second):
        unpack_thin(all_sc, first, second, 0)

    pl.when(place_ref[0] == 0)(lambda: take(own_ref, got_ref))
    pl.when(place_ref[0] != 0)(lambda: take(got_ref, own_ref))
    both = all_sc[...]
    dq = []
    for g in range(KVH):
        dq.append(both[g * PER : g * PER + q_cols])
        dkt_ref[g * HD : (g + 1) * HD] = both[g * PER + q_cols : g * PER + q_cols + HD]
        dvt_ref[g * HD : (g + 1) * HD] = both[g * PER + q_cols + HD : (g + 1) * PER]
    dq_ref[...] = jnp.concatenate(dq, 0).T
    gain = jnp.sum(both * wqkv_ref[...].astype(f32), 0, keepdims=True) / gain_one_ref[...]
    gain_ref[...] = gain.reshape(gain_ref.shape)


def unpack_last(place, own, got, wqkv_t, gain_one, after):
    width = wqkv_t.shape[1]
    shapes = [(width, HQ * HD), (KVH * HD, width), (KVH * HD, width), (width,)]
    return pl.pallas_call(
        without(unpack_last_kernel, 5, after),
        grid_spec=pltpu.PrefetchScalarGridSpec(
            num_scalar_prefetch=1,
            grid=(1,),
            in_specs=[full(own.shape)] * 2 + [full(wqkv_t.shape), full((1, width))] + [ANY] * len(after),
            out_specs=[full(shape) for shape in shapes],
            scratch_shapes=[pltpu.VMEM(wqkv_t.shape, f32)],
        ),
        out_shape=[jax.ShapeDtypeStruct(shape, f32) for shape in shapes],
        compiler_params=pltpu.CompilerParams(vmem_limit_bytes=VMEM),
        name="unpack_attention",
        cost_estimate=cost(3),
    )(place, own, got, wqkv_t, gain_one, *after)


def flip(array):
    return jnp.swapaxes(array, -1, -2)


def per_device(tokens, doc_starts, skip_flags, cotangent, attn_gain, wq, wk, wv, w_out, mlp_gain, wg, wu, wd):
    core = lax.axis_index("narrow")
    chips = lax.axis_size("wide")
    tokens, cotangent = flip(tokens), flip(cotangent)
    rows = 2 * tokens.shape[2]
    width = tokens.shape[1]
    inner = wg.shape[1]
    place = core.astype(jnp.int32).reshape(1)
    skip = lax.dynamic_slice_in_dim(skip_flags, core, 1, 0)
    starts = lax.dynamic_index_in_dim(doc_starts, core, 0, keepdims=False)
    other = swap_core(lax.dynamic_index_in_dim(tokens, 1 - core, 0, keepdims=False))
    cot_other = swap_core(lax.dynamic_index_in_dim(cotangent, 1 - core, 0, keepdims=False))
    cos_t, sin_t = rotary_rows(rows)
    pos = jnp.arange(rows, dtype=jnp.int32)
    start_row = jnp.max(jnp.where(starts[:, None] <= pos[None, :], starts[:, None], 0), 0, keepdims=True)
    gain_line = attn_gain.astype(f32)[None]
    wdt = flip(wd)
    wqkv_t, wqkv_n, w_out_t, gain_one, gain_two = prelude(
        wq, flip(wk), flip(wv), w_out, gain_line, mlp_gain.astype(f32)[None]
    )
    unit = 16 * chips

    def half_rows(count):
        return -(-count // unit) * unit

    mlp_rows = 3 * width * inner // 4 // 128
    thin = width // 128 // 2
    out_rows = thin * HQ * HD + HQ * HD // 4 + GAIN_ROWS
    rest_rows = thin * KVH * PER + KVH * PER // 4

    (
        qt, kt, vn, soft, n1, res_own, res_away, gh, dot_t, delta, keep_a, send_a, keep_b, send_b,
    ) = layer(
        half_rows(mlp_rows), half_rows(mlp_rows + out_rows),
        place, skip, tokens, other, cotangent, cot_other, gain_one, wqkv_t, w_out_t, gain_two, cos_t, sin_t,
        start_row, w_out, wg, wu, wdt,
    )
    a_sum, b_sum, c_sum = (Summer(core, chips, k) for k in range(3))
    a_sum.first(keep_a, send_a)
    b_sum.first(keep_b, send_b)
    line = Line()
    parts = []
    for g in range(KVH):
        parts.append(back(g, soft, qt, kt, vn, dot_t, delta, cos_t, sin_t, line.after()))
        a_sum.halve(line)
        b_sum.halve(line)
    keep_c, send_c = weight(half_rows(rest_rows), width, place, parts, n1, line.after())
    c_sum.first(keep_c, send_c)
    line.last = keep_c
    a_sum.halve(line)
    b_sum.halve(line)
    grad_away = line.last = last(
        False, place, skip, other, cot_other, gh, parts, wqkv_n, gain_one, line.after()
    )
    c_sum.halve(line)
    a_sum.middle(line)
    b_sum.middle(line)
    grad_got = swap_core(grad_away)
    grad_own = line.last = last(True, place, skip, tokens, cotangent, gh, parts, wqkv_n, gain_one, line.after())
    c_sum.halve(line)
    a_sum.double(line)
    b_sum.double(line)
    grad_x = line.both_halves(core, grad_own, grad_got)
    c_sum.halve(line)
    result = line.both_halves(core, res_own, swap_core(res_away))
    c_sum.halve(line)
    a_sum.double(line)
    b_sum.double(line)
    c_sum.middle(line)
    c_sum.double(line)
    a_sum.double(line)
    b_sum.double(line)
    c_sum.double(line)
    c_sum.double(line)
    a_sum.double(line)
    c_sum.double(line)
    b_sum.double(line)
    first = unpack(0, place, (a_sum.keep, a_sum.got), width, inner, ())
    dq, dkt, dvt, dgain_one = unpack_last(place, c_sum.keep, c_sum.got, wqkv_t, gain_line, first[:1])
    dwg, dwu, dwdt, dwo, dgain_two = unpack(1, place, (b_sum.keep, b_sum.got), width, inner, first)
    return (
        flip(result), flip(grad_x),
        dgain_one, dq, flip(dkt), flip(dvt), dwo, dgain_two, dwg, dwu, flip(dwdt),
    )


def solution(mesh):
    split = P("wide", "narrow", None)
    in_specs = (split, P("wide", None), P("wide"), split) + (P(),) * 9
    out_specs = (split, split) + (P(),) * 9
    return jax.shard_map(per_device, mesh=mesh, in_specs=in_specs, out_specs=out_specs, check_vma=False)
```

```python
import functools

import jax
import jax.numpy as jnp
import numpy as np
from jax import lax
from jax.experimental import pallas as pl
from jax.experimental.pallas import tpu as pltpu
from jax.sharding import PartitionSpec as P

HQ = 9
KVH = 3
HD = 64
GROUPS = HQ // KVH
PER = (GROUPS + 2) * HD
theta_base = 100000.0
eps_norm = 1e-05
masked_score = -1e30
BLOCK = 256
GAIN_ROWS = 16
VMEM = 60 * 2**20
f32 = jnp.float32
bf16 = jnp.bfloat16


def cost(microseconds):
    return pl.CostEstimate(flops=int(microseconds * 1.0e9), bytes_accessed=1024, transcendentals=0)


def dot(a, b, ca=1, cb=0):
    return lax.dot_general(a, b, (((ca,), (cb,)), ((), ())), preferred_element_type=f32)


def turn(rows, cosine, sine, sign):
    half = HD // 2
    first, second = rows[:half], rows[half:]
    if sign > 0:
        return jnp.concatenate([first * cosine - second * sine, second * cosine + first * sine], 0)
    return jnp.concatenate([first * cosine + second * sine, second * cosine - first * sine], 0)


def lanes_up(count):
    return -(-count // 128) * 128


ANY = pl.BlockSpec(memory_space=pl.ANY)


def without(kernel, inputs, after):
    return lambda *refs: kernel(*refs[:inputs], *refs[inputs + len(after) :])


def full(shape):
    return pl.BlockSpec(shape, lambda *_: (0,) * len(shape))


def widen(matrix):
    extra = lanes_up(matrix.shape[1]) - matrix.shape[1]
    return jnp.concatenate([matrix, jnp.zeros((matrix.shape[0], extra), matrix.dtype)], 1)


def pack_blocks(target, spot, matrix):
    for k in range(matrix.shape[1] // 128):
        target[spot : spot + matrix.shape[0]] = matrix[:, k * 128 : (k + 1) * 128]
        spot += matrix.shape[0]
    return spot


def pack_thin(target, spot, h, matrix):
    rows = matrix.shape[0]
    quarter = rows // 4
    base = matrix.shape[1] // 128
    for k in range(h * base // 2, (h + 1) * base // 2):
        target[spot : spot + rows] = matrix[:, k * 128 : (k + 1) * 128]
        spot += rows
    left = matrix[2 * h * quarter : (2 * h + 1) * quarter, base * 128 :]
    right = matrix[(2 * h + 1) * quarter : (2 * h + 2) * quarter, base * 128 :]
    target[spot : spot + quarter] = jnp.concatenate([left, right], 1)
    return spot + quarter


def unpack_thin(target, first, second, spot):
    rows, width = target.shape
    quarter = rows // 4
    base = width // 128
    for h, source in enumerate((first, second)):
        at = spot
        for k in range(h * base // 2, (h + 1) * base // 2):
            target[:, k * 128 : (k + 1) * 128] = source[at : at + rows].astype(f32)
            at += rows
        last = source[at : at + quarter].astype(f32)
        target[2 * h * quarter : (2 * h + 1) * quarter, base * 128 :] = last[:, : width - base * 128]
        target[(2 * h + 1) * quarter : (2 * h + 2) * quarter, base * 128 :] = last[:, width - base * 128 :]


def prelude_kernel(wq_ref, wkt_ref, wvt_ref, w_out_ref, gain_one_ref, gain_two_ref, t_ref, n_ref, out_t_ref, g1_ref, g2_ref, line_ref):
    q_cols = GROUPS * HD
    wqt = wq_ref[...].T
    for g in range(KVH):
        t_ref[g * PER : g * PER + q_cols] = wqt[g * q_cols : (g + 1) * q_cols]
        t_ref[g * PER + q_cols : g * PER + q_cols + HD] = wkt_ref[g * HD : (g + 1) * HD]
        t_ref[g * PER + q_cols + HD : (g + 1) * PER] = wvt_ref[g * HD : (g + 1) * HD]
    n_ref[...] = t_ref[...].T
    out_t_ref[...] = w_out_ref[...].T
    for source, target in ((gain_one_ref, g1_ref), (gain_two_ref, g2_ref)):
        gain = source[...].astype(f32).reshape(1, source.shape[0])
        target[...] = jnp.broadcast_to(gain, (128, source.shape[0])).T
    line_ref[...] = gain_one_ref[...].astype(f32).reshape(line_ref.shape)


def prelude(wq, wkt, wvt, w_out, gain_one, gain_two):
    width = wq.shape[0]
    return pl.pallas_call(
        prelude_kernel,
        out_shape=[
            jax.ShapeDtypeStruct((KVH * PER, width), bf16),
            jax.ShapeDtypeStruct((width, KVH * PER), bf16),
            jax.ShapeDtypeStruct((width, w_out.shape[0]), bf16),
            jax.ShapeDtypeStruct((width, 128), f32),
            jax.ShapeDtypeStruct((width, 128), f32),
            jax.ShapeDtypeStruct((1, width), f32),
        ],
        compiler_params=pltpu.CompilerParams(vmem_limit_bytes=VMEM),
        name="prelude",
        cost_estimate=cost(4),
    )(wq, wkt, wvt, w_out, gain_one, gain_two)


def layer_kernel(
    place_ref, skip_ref, own_ref, other_ref, cot_own_ref, cot_other_ref,
    gain_one_ref, wqkv_ref, w_out_t_ref, gain_two_ref, cos_ref, sin_ref, start_ref,
    w_out_ref, w_gate_hbm, w_up_hbm, w_down_hbm,
    qt_ref, kt_ref, vn_ref, soft_hbm, n1_ref,
    res_own_ref, res_away_ref, gh_ref, dot_ref, delta_ref, keep_a_hbm, send_a_hbm, keep_b_hbm, send_b_hbm,
    kn_all, vt_all, mixed_sc, n2t_sc, gt_sc, inner_sc, grads_sc, in_t_sc, down_sc, ga_sc, dgain_sc,
    scale_sc, soft_sc, w_gate_ref, w_up_ref, w_down_ref, pack_sc, weight_sem, soft_sem, pack_sem,
):
    step = pl.program_id(0)
    mine = (step >= 2).astype(jnp.int32) == place_ref[0]
    width = other_ref.shape[0]
    cols = w_gate_hbm.shape[1]

    weight_copies = [
        pltpu.make_async_copy(source, target, weight_sem.at[k])
        for k, (source, target) in enumerate(
            ((w_gate_hbm, w_gate_ref), (w_up_hbm, w_up_ref), (w_down_hbm, w_down_ref))
        )
    ]

    @pl.when(step == 0)
    def _():
        for copy in weight_copies:
            copy.start()
        dgain_sc[...] = jnp.zeros_like(dgain_sc)

    low = jnp.where(mine, own_ref[0], other_ref[...])
    x = low.astype(f32)
    cot = jnp.where(mine, cot_own_ref[0], cot_other_ref[...])
    g = jnp.where(skip_ref[place_ref[0]] == 1, jnp.zeros_like(cot), cot)
    gt_sc[step] = g
    inverse = lax.rsqrt(jnp.mean(x * x, 0, keepdims=True) + eps_norm)
    n1 = (x * inverse * gain_one_ref[:, :1]).astype(bf16)
    n1_ref[...] = widen(n1.T)
    qkv = dot(wqkv_ref[...], n1)
    cosine, sine = cos_ref[...], sin_ref[...]
    here = pl.ds(pl.multiple_of(step * BLOCK, BLOCK), BLOCK)
    for group in range(KVH):
        for r in range(GROUPS):
            head = group * GROUPS + r
            base = group * PER + r * HD
            rows = (turn(qkv[base : base + HD], cosine, sine, 1) * (HD**-0.5)).astype(bf16)
            qt_ref[head * HD : (head + 1) * HD] = rows
        base = group * PER + GROUPS * HD
        rows = turn(qkv[base : base + HD], cosine, sine, 1).astype(bf16)
        kt_ref[group * HD : (group + 1) * HD] = rows
        kn_all[group, here] = rows.T
        rows = qkv[base + HD : base + 2 * HD].astype(bf16)
        vt_all[step, group] = jnp.concatenate([rows, jnp.ones((16, BLOCK), bf16)], 0)
        vn_ref[group] = rows.T

    pos = step * BLOCK + lax.broadcasted_iota(jnp.int32, (1, BLOCK), 1)
    start_row = jnp.zeros((1, BLOCK), jnp.int32)
    for k in range(start_ref.shape[1]):
        first = start_ref[place_ref[0], k]
        start_row = jnp.where(pos >= first, first, start_row)

    def soft_copy(count):
        used = pl.ds(0, count * BLOCK)
        return pltpu.make_async_copy(soft_sc.at[:, used], soft_hbm.at[count - 1, :, used], soft_sem)

    def attend(count):
        t = lax.broadcasted_iota(jnp.int32, (BLOCK, BLOCK), 0)
        s_pos = lax.broadcasted_iota(jnp.int32, (BLOCK, BLOCK), 1)
        if count > 1:
            soft_copy(count - 1).wait()

        def one_group(group, carry):
            def scores_of(r):
                rows = pl.ds(pl.multiple_of((group * GROUPS + r) * HD, HD), HD)
                q = qt_ref[rows]
                scores = []
                for kb in range(count):
                    s = dot(kn_all[group, kb * BLOCK : (kb + 1) * BLOCK], q)
                    ok = t + kb * BLOCK >= start_row
                    if kb == count - 1:
                        ok = ok & (t <= s_pos)
                    scores.append(jnp.where(ok, s, masked_score))
                return scores

            def finish(r, scores):
                head = group * GROUPS + r
                rows = pl.ds(pl.multiple_of(head * HD, HD), HD)
                peak = scores[0].max(0, keepdims=True)
                for s in scores[1:]:
                    peak = jnp.maximum(peak, s.max(0, keepdims=True))
                out = None
                for kb in range(count):
                    p = jnp.exp(scores[kb] - peak).astype(bf16)
                    soft_sc[head, kb * BLOCK : (kb + 1) * BLOCK] = p
                    term = dot(vt_all[kb, group], p)
                    out = term if out is None else out + term
                scale = 1.0 / out[HD : HD + 1]
                scale_sc[head] = jnp.broadcast_to(scale, scale_sc.shape[1:])
                mixed_sc[step, rows] = (out[:HD] * scale).astype(bf16)

            every = [scores_of(r) for r in range(GROUPS)]
            for r in range(GROUPS):
                finish(r, every[r])
            return carry

        lax.fori_loop(0, KVH, one_group, 0)
        soft_copy(count).start()

    for count in range(1, 5):
        pl.when(step == count - 1)(lambda count=count: attend(count))

    @pl.when(step == 0)
    def _():
        for copy in weight_copies:
            copy.wait()
        for k, ref in enumerate((w_gate_ref, w_up_ref)):
            in_t_sc[k * cols : (k + 1) * cols] = widen(ref[...].T)
        down_sc[...] = widen(w_down_ref[...].T)

    mixed = mixed_sc[step]
    hidden = x + dot(w_out_t_ref[...], mixed)
    inverse = lax.rsqrt(jnp.mean(hidden * hidden, 0, keepdims=True) + eps_norm)
    normed = hidden * inverse
    n2t = (normed * gain_two_ref[:, :1]).astype(bf16)
    n2t_sc[step] = n2t
    n2 = n2t.T
    gn = g.T

    def chunk(k, carry):
        work = []
        for c in range(3):
            at = pl.ds(pl.multiple_of((3 * k + c) * BLOCK, BLOCK), BLOCK)
            at_up = pl.ds(pl.multiple_of(cols + (3 * k + c) * BLOCK, BLOCK), BLOCK)
            work.append((at, at_up, dot(n2, w_gate_ref[:, at]), dot(n2, w_up_ref[:, at]), dot(gn, w_down_ref[:, at])))
        for at, at_up, gate, up, grad_inner in work:
            sig = jax.nn.sigmoid(gate)
            act = gate * sig
            inner_sc[here, at] = (act * up).astype(bf16)
            grads_sc[here, at] = (grad_inner * up * (sig + act * (1.0 - sig))).astype(bf16)
            grads_sc[here, at_up] = (grad_inner * act).astype(bf16)
        return carry

    lax.fori_loop(0, cols // BLOCK // 3, chunk, 0)
    result = hidden + dot(inner_sc[here], down_sc[...]).T[:width]
    result = jnp.where(skip_ref[place_ref[0]] == 1, low, result.astype(bf16))

    @pl.when(mine)
    def _():
        res_own_ref[0] = result

    @pl.when(jnp.logical_not(mine))
    def _():
        res_away_ref[...] = result

    gn2 = dot(grads_sc[here], in_t_sc[...]).T[:width]
    c = gn2 * gain_two_ref[:, :1]
    dgain_sc[:, :1] += jnp.sum(gn2 * normed, 1, keepdims=True)
    gh = g.astype(f32) + inverse * (c - normed * jnp.mean(c * normed, 0, keepdims=True))
    gh_ref[...] = gh
    ga = gh.astype(bf16)
    ga_sc[here] = widen(ga.T)
    back_t = dot(w_out_ref[...], ga)
    for head in range(HQ):
        rows = (back_t[head * HD : (head + 1) * HD] * scale_sc[head, 0:1]).astype(bf16)
        dot_ref[head * HD : (head + 1) * HD] = rows
        delta_ref[head // GROUPS, head % GROUPS : head % GROUPS + 1] = jnp.sum(
            rows.astype(f32) * mixed[head * HD : (head + 1) * HD].astype(f32), 0, keepdims=True
        )

    @pl.when(step == pl.num_programs(0) - 1)
    def _():
        blocks = mixed_sc.shape[0]
        whole = lambda ref: jnp.concatenate([ref[k] for k in range(blocks)], 1)
        n2t_all, gt_all = whole(n2t_sc), whole(gt_sc)
        dw_out = dot(whole(mixed_sc), ga_sc[...])[:, :width].astype(bf16)
        line = dgain_sc[...].T[0:1]
        line = jnp.concatenate([line, jnp.zeros((1, lanes_up(width) - width), f32)], 1)
        lines = [line[:, k * 128 : (k + 1) * 128] for k in range(line.shape[1] // 128)]
        lines.append(jnp.zeros((GAIN_ROWS - len(lines), 128), f32))
        gain_rows = jnp.concatenate(lines, 0).astype(bf16)
        thin = 9 * width
        for h in range(2):
            target = pack_sc.at[2 + h]
            spot = pack_thin(target, thin, h, dw_out)
            target[spot : spot + GAIN_ROWS] = gain_rows

        def one_chunk(k, carry):
            at = pl.ds(pl.multiple_of(k * BLOCK, BLOCK), BLOCK)
            at_up = pl.ds(pl.multiple_of(cols + k * BLOCK, BLOCK), BLOCK)
            chain = jnp.where(k >= 3, 1, 0)
            third = k - 3 * chain
            for m, (left, right) in enumerate(
                ((n2t_all, grads_sc[:, at]), (n2t_all, grads_sc[:, at_up]), (gt_all, inner_sc[:, at]))
            ):
                both = dot(left, right).astype(bf16)
                for b in range(2):
                    half = jnp.where(third == 2, b, third)
                    spot = (3 * m + jnp.where(third == 2, 2, b)) * width
                    pack_sc[2 * chain + half, pl.ds(pl.multiple_of(spot, 16), width)] = both[:, b * 128 : (b + 1) * 128]
            for q in range(4):
                keep, send = pack_copies[q]
                pl.when((k == 3 * (q // 2) + 2) & (place_ref[0] == q % 2))(keep.start)
                pl.when((k == 3 * (q // 2) + 2) & (place_ref[0] != q % 2))(send.start)
            return carry

        pack_copies = []
        for q in range(4):
            targets = (keep_a_hbm, send_a_hbm) if q < 2 else (keep_b_hbm, send_b_hbm)
            source = pack_sc.at[q, pl.ds(0, targets[0].shape[0])]
            pack_copies.append([pltpu.make_async_copy(source, target, pack_sem.at[q]) for target in targets])
        lax.fori_loop(0, 6, one_chunk, 0)
        for keep, _ in pack_copies:
            keep.wait()
        soft_copy(blocks).wait()


def own_specs(width, near):
    own = pl.BlockSpec((1, width, BLOCK), lambda i, c, s: (c[0], 0, jnp.where(i >= near, i - near, i)))
    oth = pl.BlockSpec((width, BLOCK), lambda i, c, s: (0, jnp.where(i >= near, i - near, i)))
    return own, oth


def out_specs_halves(width, near):
    mine = pl.BlockSpec((1, width, BLOCK), lambda i, c, s: (c[0], 0, jnp.clip(i - near * c[0], 0, near - 1)))
    away = pl.BlockSpec((width, BLOCK), lambda i, c, s: (0, jnp.clip(i - near * (1 - c[0]), 0, near - 1)))
    return mine, away


def layer(
    rows_a, rows_b, place, skip, tokens, other, cot, cot_other, gain_one, wqkv_t, w_out_t, gain_two, cos_t, sin_t,
    starts, w_out, wg, wu, wdt,
):
    rows = 2 * tokens.shape[2]
    width = tokens.shape[1]
    cols = wg.shape[1]
    wide = lanes_up(width)
    blocks = rows // BLOCK
    own, oth = own_specs(width, blocks // 2)
    col = pl.BlockSpec((width, BLOCK), lambda i, c, s: (0, i))
    row_wide = pl.BlockSpec((BLOCK, wide), lambda i, c, s: (i, 0))
    small = pl.BlockSpec((HD // 2, BLOCK), lambda i, c, s: (0, i))
    const = lambda array: pl.BlockSpec(
        array.shape, lambda *_: (0,) * array.ndim, pipeline_mode=pl.Buffered(1)
    )
    any_spec = pl.BlockSpec(memory_space=pl.ANY)
    halves = [(rows_a, 128), (rows_a, 128), (rows_b, 128), (rows_b, 128)]
    out_shape = [
        jax.ShapeDtypeStruct((HQ * HD, rows), bf16),
        jax.ShapeDtypeStruct((KVH * HD, rows), bf16),
        jax.ShapeDtypeStruct((KVH, rows, HD), bf16),
        jax.ShapeDtypeStruct((blocks, HQ, rows, BLOCK), bf16),
        jax.ShapeDtypeStruct((rows, wide), bf16),
        jax.ShapeDtypeStruct((2, width, rows // 2), bf16),
        jax.ShapeDtypeStruct((width, rows // 2), bf16),
        jax.ShapeDtypeStruct((width, rows), f32),
        jax.ShapeDtypeStruct((HQ * HD, rows), bf16),
        jax.ShapeDtypeStruct((KVH, GROUPS, rows), f32),
    ] + [jax.ShapeDtypeStruct(shape, bf16) for shape in halves]
    return pl.pallas_call(
        layer_kernel,
        grid_spec=pltpu.PrefetchScalarGridSpec(
            num_scalar_prefetch=2,
            grid=(blocks,),
            in_specs=[
                own, oth, own, oth, const(gain_one), const(wqkv_t), const(w_out_t), const(gain_two),
                small, small, pl.BlockSpec(memory_space=pltpu.SMEM),
                const(w_out), any_spec, any_spec, any_spec,
            ],
            out_specs=[
                col,
                pl.BlockSpec((KVH * HD, BLOCK), lambda i, c, s: (0, i)),
                pl.BlockSpec((KVH, BLOCK, HD), lambda i, c, s: (0, i, 0)),
                any_spec,
                row_wide,
                *out_specs_halves(width, blocks // 2),
                col, col,
                pl.BlockSpec((KVH, GROUPS, BLOCK), lambda i, c, s: (0, 0, i)),
            ] + [any_spec] * 4,
            scratch_shapes=[
                pltpu.VMEM((KVH, rows, HD), bf16),
                pltpu.VMEM((blocks, KVH, HD + 16, BLOCK), bf16),
                pltpu.VMEM((blocks, HQ * HD, BLOCK), bf16),
                pltpu.VMEM((blocks, width, BLOCK), bf16),
                pltpu.VMEM((blocks, width, BLOCK), bf16),
                pltpu.VMEM((rows, cols), bf16),
                pltpu.VMEM((rows, 2 * cols), bf16),
                pltpu.VMEM((2 * cols, wide), bf16),
                pltpu.VMEM((cols, wide), bf16),
                pltpu.VMEM((rows, wide), bf16),
                pltpu.VMEM((width, 128), f32),
                pltpu.VMEM((HQ, 8, BLOCK), f32),
                pltpu.VMEM((HQ, rows, BLOCK), bf16),
                pltpu.VMEM(wg.shape, bf16),
                pltpu.VMEM(wu.shape, bf16),
                pltpu.VMEM(wdt.shape, bf16),
                pltpu.VMEM((4, rows_b, 128), bf16),
                pltpu.SemaphoreType.DMA((3,)),
                pltpu.SemaphoreType.DMA,
                pltpu.SemaphoreType.DMA((4,)),
            ],
        ),
        out_shape=out_shape,
        compiler_params=pltpu.CompilerParams(vmem_limit_bytes=VMEM),
        name="layer_forward",
        cost_estimate=cost(50),
    )(
        place, skip, tokens, other, cot, cot_other, gain_one, wqkv_t, w_out_t, gain_two, cos_t, sin_t, starts,
        w_out, wg, wu, wdt,
    )


def back_kernel(
    g, place_ref, soft_ref, qt_ref, kt_ref, vn_ref, dot_ref, delta_ref, cos_ref, sin_ref, n1_ref,
    dqkv_ref, keep_hbm, send_hbm,
    acc, ds_sc, pack_sc, pack_sem,
):
    step = pl.program_id(0)
    blocks = pl.num_programs(0)
    cosine, sine = cos_ref[...], sin_ref[...]

    @pl.when(step == 0)
    def _():
        acc[...] = jnp.zeros_like(acc)

    def attend(count):
        used = slice(0, count * BLOCK)
        here = slice((count - 1) * BLOCK, count * BLOCK)
        ups = [dot_ref[r * HD : (r + 1) * HD] for r in range(GROUPS)]
        soft_grads = [[dot(vn_ref[0, kb * BLOCK : (kb + 1) * BLOCK], up) for kb in range(count)] for up in ups]
        for r in range(GROUPS):
            rows = slice(r * HD, (r + 1) * HD)
            delta = delta_ref[0, r : r + 1]
            pair = jnp.concatenate([qt_ref[rows], ups[r]], 0).T
            left = lax.broadcasted_iota(jnp.int32, pair.shape, 1) < HD
            zero = jnp.zeros_like(pair)
            pads = jnp.concatenate([jnp.where(left, pair, zero), jnp.where(left, zero, pair)], 0)
            for kb in range(count):
                span = slice(kb * BLOCK, (kb + 1) * BLOCK)
                p = soft_ref[0, r, span]
                ds_sc[r, span, :BLOCK] = (p.astype(f32) * (soft_grads[r][kb] - delta)).astype(bf16)
                ds_sc[r, span, BLOCK:] = p
            acc[used] += dot(ds_sc[r, used], pads)
            dq = dot(kt_ref[:, used], ds_sc[r, used, :BLOCK])
            dqkv_ref[rows, here] = turn(dq * (HD**-0.5), cosine, sine, -1).astype(bf16)
        done = acc[here].T
        base = GROUPS * HD
        dqkv_ref[base : base + HD, here] = turn(done[:HD], cosine, sine, -1).astype(bf16)
        dqkv_ref[base + HD : base + 2 * HD, here] = done[HD:].astype(bf16)

    for count in range(1, 5):
        pl.when(step == 4 - count)(lambda count=count: attend(count))

    @pl.when(step == blocks - 1)
    def _():
        width = pack_sc.shape[1] * 128 * 2 // PER
        dw = dot(dqkv_ref[...], n1_ref[...])[:, :width].astype(bf16)
        span = pl.ds(g * pack_sc.shape[1], pack_sc.shape[1])
        copies = []
        for h in range(2):
            pack_thin(pack_sc.at[h], 0, h, dw)
            copies.append([pltpu.make_async_copy(pack_sc.at[h], t.at[span], pack_sem.at[h]) for t in (keep_hbm, send_hbm)])
            pl.when(place_ref[0] == h)(copies[h][0].start)
            pl.when(place_ref[0] != h)(copies[h][1].start)
        for keep, _ in copies:
            keep.wait()


def back(g, half_rows, width, place, soft, qt, kt, vn, dot_t, delta, cos_t, sin_t, n1, packed, after=()):
    blocks, _, rows, _ = soft.shape
    last = blocks - 1
    small = pl.BlockSpec((HD // 2, BLOCK), lambda i, c: (0, last - i))
    inputs = 10
    return pl.pallas_call(
        without(functools.partial(back_kernel, g), inputs, tuple(packed) + tuple(after)),
        grid_spec=pltpu.PrefetchScalarGridSpec(
            num_scalar_prefetch=1,
            grid=(blocks,),
            in_specs=[
                pl.BlockSpec((1, GROUPS, rows, BLOCK), lambda i, c: (last - i, g, 0, 0)),
                pl.BlockSpec((GROUPS * HD, BLOCK), lambda i, c: (g, last - i)),
                pl.BlockSpec((HD, rows), lambda i, c: (g, 0)),
                pl.BlockSpec((1, rows, HD), lambda i, c: (g, 0, 0)),
                pl.BlockSpec((GROUPS * HD, BLOCK), lambda i, c: (g, last - i)),
                pl.BlockSpec((1, GROUPS, BLOCK), lambda i, c: (g, 0, last - i)),
                small, small, full(n1.shape),
            ] + [ANY] * (len(packed) + len(after)),
            out_specs=[full((PER, rows)), ANY, ANY],
            scratch_shapes=[
                pltpu.VMEM((rows, 2 * HD), f32),
                pltpu.VMEM((GROUPS, rows, 2 * BLOCK), bf16),
                pltpu.VMEM((2, PER * width // 256, 128), bf16),
                pltpu.SemaphoreType.DMA((2,)),
            ],
        ),
        out_shape=[jax.ShapeDtypeStruct((PER, rows), bf16)] + [jax.ShapeDtypeStruct((half_rows, 128), bf16)] * 2,
        input_output_aliases={inputs + k: 1 + k for k in range(len(packed))},
        compiler_params=pltpu.CompilerParams(vmem_limit_bytes=VMEM),
        name="attention_backward",
        cost_estimate=cost(9),
    )(place, soft, qt, kt, vn, dot_t, delta, cos_t, sin_t, n1, *packed, *after)


def last_kernel(
    place_ref, skip_ref, x_ref, cot_ref, gh_ref, d0_ref, d1_ref, d2_ref, wqkv_ref, gain_one_ref, grad_ref,
):
    x = x_ref[...].reshape(gh_ref.shape).astype(f32)
    skipped = skip_ref[place_ref[0]] == 1
    inverse = lax.rsqrt(jnp.mean(x * x, 0, keepdims=True) + eps_norm)
    normed = x * inverse
    dqkv = jnp.concatenate([d0_ref[...], d1_ref[...], d2_ref[...]], 0)
    c = dot(wqkv_ref[...], dqkv) * gain_one_ref[:, :1]
    gx = gh_ref[...] + inverse * (c - normed * jnp.mean(c * normed, 0, keepdims=True))
    gx = jnp.where(skipped, cot_ref[...].reshape(gh_ref.shape), gx.astype(bf16))
    grad_ref[...] = gx.reshape(grad_ref.shape)


def last(mine, place, skip, x, cot, gh, parts, wqkv_n, gain_one, after=()):
    width, rows = gh.shape
    near = rows // BLOCK // 2
    if mine:
        source = pl.BlockSpec((1, width, BLOCK), lambda i, c, s: (c[0], 0, i))
        at = lambda i, c, s: (0, near * c[0] + i)
    else:
        source = pl.BlockSpec((width, BLOCK), lambda i, c, s: (0, i))
        at = lambda i, c, s: (0, near * (1 - c[0]) + i)
    col = pl.BlockSpec((width, BLOCK), at)
    part = pl.BlockSpec((PER, BLOCK), at)
    return pl.pallas_call(
        without(last_kernel, 10, after),
        grid_spec=pltpu.PrefetchScalarGridSpec(
            num_scalar_prefetch=2,
            grid=(near,),
            in_specs=[source, source, col, part, part, part, full(wqkv_n.shape), full((width, 128))]
            + [ANY] * len(after),
            out_specs=source,
        ),
        out_shape=jax.ShapeDtypeStruct(x.shape, bf16),
        compiler_params=pltpu.CompilerParams(vmem_limit_bytes=VMEM),
        name="input_backward",
        cost_estimate=cost(4),
    )(place, skip, x, cot, gh, *parts, wqkv_n, gain_one, *after)


def rotary_rows(rows):
    frequency = theta_base ** (-2.0 * np.arange(HD // 2, dtype=np.float64) / HD)
    angles = frequency[:, None] * np.arange(rows, dtype=np.float64)[None, :]
    return np.cos(angles).astype(np.float32), np.sin(angles).astype(np.float32)


def swap_core(array):
    return lax.ppermute(array, "narrow", [(0, 1), (1, 0)])


def axis_orders(bits, turn_index):
    if bits == 4:
        return (((0, 1, 2, 3), (1, 2, 3, 0)), ((1, 0, 2, 3), (2, 3, 0, 1)), ((0, 1, 2, 3), (1, 0, 2, 3)))[turn_index]
    base = tuple(range(bits))
    shift = bits // 2
    return base, base[shift:] + base[:shift]


class Summer:
    def __init__(self, core, chips, turn_index, exchanges):
        self.core = core
        self.chips = chips
        self.bits = chips.bit_length() - 1
        self.halvings = self.bits - exchanges
        self.orders = axis_orders(self.bits, turn_index)
        self.place = lax.axis_index("wide")
        self.stage = 0

    def bit(self, step):
        by_core = [(self.place >> order[step]) & 1 for order in self.orders]
        return jnp.where(self.core == 0, by_core[0], by_core[1])

    def swap(self, array, step):
        pairs = [
            (2 * chip + c, 2 * (chip ^ (1 << self.orders[c][step])) + c) for chip in range(self.chips) for c in range(2)
        ]
        return lax.ppermute(array, ("wide", "narrow"), pairs)

    def first(self, keep, send):
        self.keep, self.got = keep, swap_core(send)

    def advance(self, line):
        if line.last is not None:
            self.keep, self.got, _ = lax.optimization_barrier((self.keep, self.got, line.last))
        if self.stage < self.halvings:
            bit = self.bit(self.stage)
            half = self.keep.shape[0] // 2

            def part(which):
                a = lax.dynamic_slice_in_dim(self.keep, which * half, half, 0).astype(f32)
                b = lax.dynamic_slice_in_dim(self.got, which * half, half, 0).astype(f32)
                return (a + b).astype(bf16)

            line.last = part(1 - bit)
            self.keep, self.got = part(bit), self.swap(line.last, self.stage)
        elif self.stage <= self.bits:
            line.last = self.keep = (self.keep.astype(f32) + self.got.astype(f32)).astype(bf16)
            axis = self.stage if self.stage < self.bits else self.halvings - 1
            self.got = self.swap(self.keep, axis)
        else:
            step = self.halvings + self.bits - self.stage
            low = self.bit(step) == 0
            line.last = self.keep = jnp.where(
                low, jnp.concatenate([self.keep, self.got], 0), jnp.concatenate([self.got, self.keep], 0)
            )
            self.got = self.swap(self.keep, step - 1) if step else swap_core(self.keep)
        self.stage += 1

    @property
    def done(self):
        return self.stage > self.bits + self.halvings


class Line:
    last = None

    def after(self):
        return () if self.last is None else (self.last,)

    def both_halves(self, core, own, got):
        own, got, _ = lax.optimization_barrier((own, got, self.last))
        result = lax.dynamic_update_slice_in_dim(own, got[None], 1 - core, 0)
        self.last = got
        return result


def unpack_kernel(chain, place_ref, own, got, *refs):
    gate_ref, up_ref, down_ref = refs[-5:-2] if chain else refs
    step = pl.program_id(0)
    width = gate_ref.shape[0]

    def take(halves):
        for third in range(3):
            blocks = ((halves[0], 2), (halves[1], 2)) if third == 2 else ((halves[third], 0), (halves[third], 1))

            @pl.when(step == third)
            def _():
                for m, target in enumerate((gate_ref, up_ref, down_ref)):
                    for b, (source, place) in enumerate(blocks):
                        spot = (3 * m + place) * width
                        target[:, b * 128 : (b + 1) * 128] = source[spot : spot + width].astype(f32)

    pl.when(place_ref[0] == 0)(lambda: take((own, got)))
    pl.when(place_ref[0] != 0)(lambda: take((got, own)))

    if chain:
        w_out_ref, gain_ref = refs[-2:]

        def take_rest(first, second):
            spot = 9 * width
            unpack_thin(w_out_ref, first, second, spot)
            spot += width // 128 // 2 * width + width // 4
            rows = first[spot : spot + GAIN_ROWS].astype(f32)
            line = jnp.concatenate([rows[k : k + 1] for k in range(lanes_up(width) // 128)], 1)
            gain_ref[...] = line[:, :width].reshape(width)

        pl.when((step == 0) & (place_ref[0] == 0))(lambda: take_rest(own, got))
        pl.when((step == 0) & (place_ref[0] != 0))(lambda: take_rest(got, own))


def unpack(chain, place, buffers, width, inner, earlier):
    spec = pl.BlockSpec((width, BLOCK), lambda i, c: (0, 3 * chain + i))
    out_specs = [spec, spec, spec]
    out_shape = [jax.ShapeDtypeStruct((width, inner), f32)] * 3
    if chain:
        out_specs += [full((HQ * HD, width)), full((width,))]
        out_shape += [jax.ShapeDtypeStruct((HQ * HD, width), f32), jax.ShapeDtypeStruct((width,), f32)]
    return pl.pallas_call(
        functools.partial(unpack_kernel, chain),
        grid_spec=pltpu.PrefetchScalarGridSpec(
            num_scalar_prefetch=1,
            grid=(3,),
            in_specs=[full(b.shape) for b in buffers] + [ANY] * len(earlier),
            out_specs=out_specs,
        ),
        out_shape=out_shape,
        input_output_aliases={3 + k: k for k in range(len(earlier))},
        compiler_params=pltpu.CompilerParams(vmem_limit_bytes=VMEM),
        name="unpack_mlp",
        cost_estimate=cost(4),
    )(place, *buffers, *earlier)


def unpack_last_kernel(place_ref, own_ref, got_ref, wqkv_ref, gain_one_ref, dq_ref, dkt_ref, dvt_ref, gain_ref, all_sc):
    q_cols = GROUPS * HD

    def take(first, second):
        for g in range(KVH):
            unpack_thin(all_sc.at[g * PER : (g + 1) * PER], first, second, g * PER * all_sc.shape[1] // 256)

    pl.when(place_ref[0] == 0)(lambda: take(own_ref, got_ref))
    pl.when(place_ref[0] != 0)(lambda: take(got_ref, own_ref))
    both = all_sc[...]
    dq = []
    for g in range(KVH):
        dq.append(both[g * PER : g * PER + q_cols])
        dkt_ref[g * HD : (g + 1) * HD] = both[g * PER + q_cols : g * PER + q_cols + HD]
        dvt_ref[g * HD : (g + 1) * HD] = both[g * PER + q_cols + HD : (g + 1) * PER]
    dq_ref[...] = jnp.concatenate(dq, 0).T
    gain = jnp.sum(both * wqkv_ref[...].astype(f32), 0, keepdims=True) / gain_one_ref[...]
    gain_ref[...] = gain.reshape(gain_ref.shape)


def unpack_last(place, own, got, wqkv_t, gain_one, after):
    width = wqkv_t.shape[1]
    shapes = [(width, HQ * HD), (KVH * HD, width), (KVH * HD, width), (width,)]
    return pl.pallas_call(
        without(unpack_last_kernel, 5, after),
        grid_spec=pltpu.PrefetchScalarGridSpec(
            num_scalar_prefetch=1,
            grid=(1,),
            in_specs=[full(own.shape)] * 2 + [full(wqkv_t.shape), full((1, width))] + [ANY] * len(after),
            out_specs=[full(shape) for shape in shapes],
            scratch_shapes=[pltpu.VMEM(wqkv_t.shape, f32)],
        ),
        out_shape=[jax.ShapeDtypeStruct(shape, f32) for shape in shapes],
        compiler_params=pltpu.CompilerParams(vmem_limit_bytes=VMEM),
        name="unpack_attention",
        cost_estimate=cost(3),
    )(place, own, got, wqkv_t, gain_one, *after)


def flip(array):
    return jnp.swapaxes(array, -1, -2)


def per_device(tokens, doc_starts, skip_flags, cotangent, attn_gain, wq, wk, wv, w_out, mlp_gain, wg, wu, wd):
    core = lax.axis_index("narrow")
    chips = lax.axis_size("wide")
    tokens, cotangent = flip(tokens), flip(cotangent)
    rows = 2 * tokens.shape[2]
    width = tokens.shape[1]
    inner = wg.shape[1]
    place = core.astype(jnp.int32).reshape(1)
    skip = skip_flags
    other = swap_core(lax.dynamic_index_in_dim(tokens, 1 - core, 0, keepdims=False))
    cot_other = swap_core(lax.dynamic_index_in_dim(cotangent, 1 - core, 0, keepdims=False))
    cos_t, sin_t = rotary_rows(rows)
    wdt = flip(wd)
    wqkv_t, wqkv_n, w_out_t, gain_one, gain_two, gain_line = prelude(wq, flip(wk), flip(wv), w_out, attn_gain, mlp_gain)
    unit = 16 * chips

    def half_rows(count):
        return -(-count // unit) * unit

    mlp_rows = 3 * width * inner // 4 // 128
    thin = width // 128 // 2
    out_rows = thin * HQ * HD + HQ * HD // 4 + GAIN_ROWS
    rest_rows = thin * KVH * PER + KVH * PER // 4

    (
        qt, kt, vn, soft, n1, res_own, res_away, gh, dot_t, delta, keep_a, send_a, keep_b, send_b,
    ) = layer(
        half_rows(mlp_rows), half_rows(mlp_rows + out_rows),
        place, skip, tokens, other, cotangent, cot_other, gain_one, wqkv_t, w_out_t, gain_two, cos_t, sin_t,
        doc_starts, w_out, wg, wu, wdt,
    )
    a_sum, b_sum, c_sum = (Summer(core, chips, k, exchanges) for k, exchanges in ((0, 0), (1, 0), (2, 2)))
    a_sum.first(keep_a, send_a)
    b_sum.first(keep_b, send_b)
    line = Line()
    parts, packed = [], ()
    for g in range(KVH):
        part, *packed = back(
            g, half_rows(rest_rows), width, place, soft, qt, kt, vn, dot_t, delta, cos_t, sin_t, n1, packed, line.after()
        )
        parts.append(part)
        line.last = part
        if g == KVH - 1:
            c_sum.first(*packed)
        a_sum.advance(line)
        b_sum.advance(line)
    grad_away = last(False, place, skip, other, cot_other, gh, parts, wqkv_n, gain_one, line.after())
    line.last = grad_away
    for chain in (c_sum, a_sum, b_sum):
        chain.advance(line)
    grad_got = swap_core(grad_away)
    for chain in (c_sum, a_sum, b_sum):
        chain.advance(line)
    result = line.both_halves(core, res_own, swap_core(res_away))
    for chain in (c_sum, a_sum, b_sum, c_sum, a_sum, b_sum, c_sum, a_sum, b_sum):
        chain.advance(line)
    c_sum.advance(line)
    c_sum.advance(line)
    grad_own = last(True, place, skip, tokens, cotangent, gh, parts, wqkv_n, gain_one, line.after())
    line.last = grad_own
    a_sum.advance(line)
    for chain in (a_sum, c_sum):
        while not chain.done:
            chain.advance(line)
    dq, dkt, dvt, dgain_one = unpack_last(place, c_sum.keep, c_sum.got, wqkv_t, gain_line, line.after())
    line.last = dgain_one
    while not b_sum.done:
        b_sum.advance(line)
    first = unpack(0, place, (a_sum.keep, a_sum.got), width, inner, ())
    dwg, dwu, dwdt, dwo, dgain_two = unpack(1, place, (b_sum.keep, b_sum.got), width, inner, first)
    grad_x = line.both_halves(core, grad_own, grad_got)
    return (
        flip(result), flip(grad_x),
        dgain_one, dq, flip(dkt), flip(dvt), dwo, dgain_two, dwg, dwu, flip(dwdt),
    )


def solution(mesh):
    split = P("wide", "narrow", None)
    in_specs = (split, P("wide", None), P("wide"), split) + (P(),) * 9
    out_specs = (split, split) + (P(),) * 9
    return jax.shard_map(per_device, mesh=mesh, in_specs=in_specs, out_specs=out_specs, check_vma=False)
```

```python
import functools

import jax
import jax.numpy as jnp
import numpy as np
from jax import lax
from jax.experimental import pallas as pl
from jax.experimental.pallas import tpu as pltpu
from jax.sharding import PartitionSpec as P

HQ = 9
KVH = 3
HD = 64
GROUPS = HQ // KVH
PER = (GROUPS + 2) * HD
theta_base = 100000.0
eps_norm = 1e-05
masked_score = -1e30
BLOCK = 256
GAIN_ROWS = 16
VMEM = 60 * 2**20
f32 = jnp.float32
bf16 = jnp.bfloat16


def cost(microseconds):
    return pl.CostEstimate(flops=int(microseconds * 1.0e9), bytes_accessed=1024, transcendentals=0)


def dot(a, b, ca=1, cb=0):
    return lax.dot_general(a, b, (((ca,), (cb,)), ((), ())), preferred_element_type=f32)


def turn(rows, cosine, sine, sign):
    half = HD // 2
    first, second = rows[:half], rows[half:]
    if sign > 0:
        return jnp.concatenate([first * cosine - second * sine, second * cosine + first * sine], 0)
    return jnp.concatenate([first * cosine + second * sine, second * cosine - first * sine], 0)


def lanes_up(count):
    return -(-count // 128) * 128


ANY = pl.BlockSpec(memory_space=pl.ANY)


def without(kernel, inputs, after):
    return lambda *refs: kernel(*refs[:inputs], *refs[inputs + len(after) :])


def full(shape):
    return pl.BlockSpec(shape, lambda *_: (0,) * len(shape))


def widen(matrix):
    extra = lanes_up(matrix.shape[1]) - matrix.shape[1]
    return jnp.concatenate([matrix, jnp.zeros((matrix.shape[0], extra), matrix.dtype)], 1)


def pack_blocks(target, spot, matrix):
    for k in range(matrix.shape[1] // 128):
        target[spot : spot + matrix.shape[0]] = matrix[:, k * 128 : (k + 1) * 128]
        spot += matrix.shape[0]
    return spot


def pack_thin(target, spot, h, matrix):
    rows = matrix.shape[0]
    quarter = rows // 4
    base = matrix.shape[1] // 128
    for k in range(h * base // 2, (h + 1) * base // 2):
        target[spot : spot + rows] = matrix[:, k * 128 : (k + 1) * 128]
        spot += rows
    left = matrix[2 * h * quarter : (2 * h + 1) * quarter, base * 128 :]
    right = matrix[(2 * h + 1) * quarter : (2 * h + 2) * quarter, base * 128 :]
    target[spot : spot + quarter] = jnp.concatenate([left, right], 1)
    return spot + quarter


def unpack_thin(target, first, second, spot):
    rows, width = target.shape
    quarter = rows // 4
    base = width // 128
    for h, source in enumerate((first, second)):
        at = spot
        for k in range(h * base // 2, (h + 1) * base // 2):
            target[:, k * 128 : (k + 1) * 128] = source[at : at + rows].astype(f32)
            at += rows
        last = source[at : at + quarter].astype(f32)
        target[2 * h * quarter : (2 * h + 1) * quarter, base * 128 :] = last[:, : width - base * 128]
        target[(2 * h + 1) * quarter : (2 * h + 2) * quarter, base * 128 :] = last[:, width - base * 128 :]


def prelude_kernel(wq_ref, wkt_ref, wvt_ref, w_out_ref, gain_one_ref, gain_two_ref, t_ref, n_ref, out_t_ref, g1_ref, g2_ref, line_ref):
    q_cols = GROUPS * HD
    wqt = wq_ref[...].T
    for g in range(KVH):
        t_ref[g * PER : g * PER + q_cols] = wqt[g * q_cols : (g + 1) * q_cols]
        t_ref[g * PER + q_cols : g * PER + q_cols + HD] = wkt_ref[g * HD : (g + 1) * HD]
        t_ref[g * PER + q_cols + HD : (g + 1) * PER] = wvt_ref[g * HD : (g + 1) * HD]
    n_ref[...] = t_ref[...].T
    out_t_ref[...] = w_out_ref[...].T
    for source, target in ((gain_one_ref, g1_ref), (gain_two_ref, g2_ref)):
        gain = source[...].astype(f32).reshape(1, source.shape[0])
        target[...] = jnp.broadcast_to(gain, (128, source.shape[0])).T
    line_ref[...] = gain_one_ref[...].astype(f32).reshape(line_ref.shape)


def prelude(wq, wkt, wvt, w_out, gain_one, gain_two):
    width = wq.shape[0]
    return pl.pallas_call(
        prelude_kernel,
        out_shape=[
            jax.ShapeDtypeStruct((KVH * PER, width), bf16),
            jax.ShapeDtypeStruct((width, KVH * PER), bf16),
            jax.ShapeDtypeStruct((width, w_out.shape[0]), bf16),
            jax.ShapeDtypeStruct((width, 128), f32),
            jax.ShapeDtypeStruct((width, 128), f32),
            jax.ShapeDtypeStruct((1, width), f32),
        ],
        compiler_params=pltpu.CompilerParams(vmem_limit_bytes=VMEM),
        name="prelude",
        cost_estimate=cost(4),
    )(wq, wkt, wvt, w_out, gain_one, gain_two)


def layer_kernel(
    place_ref, skip_ref, own_ref, other_ref, cot_own_ref, cot_other_ref,
    gain_one_ref, wqkv_ref, w_out_t_ref, gain_two_ref, cos_ref, sin_ref, start_ref,
    w_out_ref, w_gate_hbm, w_up_hbm, w_down_hbm,
    qt_ref, kt_ref, vn_ref, soft_hbm, n1_ref,
    res_own_ref, res_away_ref, gh_ref, dot_ref, delta_ref, keep_a_hbm, send_a_hbm, keep_b_hbm, send_b_hbm,
    kn_all, vt_all, mixed_sc, n2t_sc, gt_sc, inner_sc, grads_sc, in_t_sc, down_sc, ga_sc, dgain_sc,
    scale_sc, soft_sc, w_gate_ref, w_up_ref, w_down_ref, pack_sc, weight_sem, soft_sem, pack_sem,
):
    step = pl.program_id(0)
    mine = (step >= 2).astype(jnp.int32) == place_ref[0]
    width = other_ref.shape[0]
    cols = w_gate_hbm.shape[1]

    weight_copies = [
        pltpu.make_async_copy(source, target, weight_sem.at[k])
        for k, (source, target) in enumerate(
            ((w_gate_hbm, w_gate_ref), (w_up_hbm, w_up_ref), (w_down_hbm, w_down_ref))
        )
    ]

    @pl.when(step == 0)
    def _():
        for copy in weight_copies:
            copy.start()
        dgain_sc[...] = jnp.zeros_like(dgain_sc)

    low = jnp.where(mine, own_ref[0], other_ref[...])
    x = low.astype(f32)
    cot = jnp.where(mine, cot_own_ref[0], cot_other_ref[...])
    g = jnp.where(skip_ref[place_ref[0]] == 1, jnp.zeros_like(cot), cot)
    gt_sc[step] = g
    inverse = lax.rsqrt(jnp.mean(x * x, 0, keepdims=True) + eps_norm)
    n1 = (x * inverse * gain_one_ref[:, :1]).astype(bf16)
    n1_ref[...] = widen(n1.T)
    qkv = dot(wqkv_ref[...], n1)
    cosine, sine = cos_ref[...], sin_ref[...]
    here = pl.ds(pl.multiple_of(step * BLOCK, BLOCK), BLOCK)
    for group in range(KVH):
        for r in range(GROUPS):
            head = group * GROUPS + r
            base = group * PER + r * HD
            rows = (turn(qkv[base : base + HD], cosine, sine, 1) * (HD**-0.5)).astype(bf16)
            qt_ref[head * HD : (head + 1) * HD] = rows
        base = group * PER + GROUPS * HD
        rows = turn(qkv[base : base + HD], cosine, sine, 1).astype(bf16)
        kt_ref[group * HD : (group + 1) * HD] = rows
        kn_all[group, here] = rows.T
        rows = qkv[base + HD : base + 2 * HD].astype(bf16)
        vt_all[step, group] = jnp.concatenate([rows, jnp.ones((16, BLOCK), bf16)], 0)
        vn_ref[group] = rows.T

    pos = step * BLOCK + lax.broadcasted_iota(jnp.int32, (1, BLOCK), 1)
    start_row = jnp.zeros((1, BLOCK), jnp.int32)
    for k in range(start_ref.shape[1]):
        first = start_ref[place_ref[0], k]
        start_row = jnp.where(pos >= first, first, start_row)

    def soft_copy(count):
        used = pl.ds(0, count * BLOCK)
        return pltpu.make_async_copy(soft_sc.at[:, used], soft_hbm.at[count - 1, :, used], soft_sem)

    def attend(count):
        t = lax.broadcasted_iota(jnp.int32, (BLOCK, BLOCK), 0)
        s_pos = lax.broadcasted_iota(jnp.int32, (BLOCK, BLOCK), 1)
        if count > 1:
            soft_copy(count - 1).wait()

        def one_group(group, carry):
            def scores_of(r):
                rows = pl.ds(pl.multiple_of((group * GROUPS + r) * HD, HD), HD)
                q = qt_ref[rows]
                scores = []
                for kb in range(count):
                    s = dot(kn_all[group, kb * BLOCK : (kb + 1) * BLOCK], q)
                    ok = t + kb * BLOCK >= start_row
                    if kb == count - 1:
                        ok = ok & (t <= s_pos)
                    scores.append(jnp.where(ok, s, masked_score))
                return scores

            def finish(r, scores):
                head = group * GROUPS + r
                rows = pl.ds(pl.multiple_of(head * HD, HD), HD)
                peak = scores[0].max(0, keepdims=True)
                for s in scores[1:]:
                    peak = jnp.maximum(peak, s.max(0, keepdims=True))
                out = None
                for kb in range(count):
                    p = jnp.exp(scores[kb] - peak).astype(bf16)
                    soft_sc[head, kb * BLOCK : (kb + 1) * BLOCK] = p
                    term = dot(vt_all[kb, group], p)
                    out = term if out is None else out + term
                scale = 1.0 / out[HD : HD + 1]
                scale_sc[head] = jnp.broadcast_to(scale, scale_sc.shape[1:])
                mixed_sc[step, rows] = (out[:HD] * scale).astype(bf16)

            every = [scores_of(r) for r in range(GROUPS)]
            for r in range(GROUPS):
                finish(r, every[r])
            return carry

        lax.fori_loop(0, KVH, one_group, 0)
        soft_copy(count).start()

    for count in range(1, 5):
        pl.when(step == count - 1)(lambda count=count: attend(count))

    @pl.when(step == 0)
    def _():
        for copy in weight_copies:
            copy.wait()
        for k, ref in enumerate((w_gate_ref, w_up_ref)):
            in_t_sc[k * cols : (k + 1) * cols] = widen(ref[...].T)
        down_sc[...] = widen(w_down_ref[...].T)

    mixed = mixed_sc[step]
    hidden = x + dot(w_out_t_ref[...], mixed)
    inverse = lax.rsqrt(jnp.mean(hidden * hidden, 0, keepdims=True) + eps_norm)
    normed = hidden * inverse
    n2t = (normed * gain_two_ref[:, :1]).astype(bf16)
    n2t_sc[step] = n2t
    n2 = n2t.T
    gn = g.T

    def chunk(k, carry):
        work = []
        for c in range(3):
            at = pl.ds(pl.multiple_of((3 * k + c) * BLOCK, BLOCK), BLOCK)
            at_up = pl.ds(pl.multiple_of(cols + (3 * k + c) * BLOCK, BLOCK), BLOCK)
            work.append((at, at_up, dot(n2, w_gate_ref[:, at]), dot(n2, w_up_ref[:, at]), dot(gn, w_down_ref[:, at])))
        for at, at_up, gate, up, grad_inner in work:
            sig = jax.nn.sigmoid(gate)
            act = gate * sig
            inner_sc[here, at] = (act * up).astype(bf16)
            grads_sc[here, at] = (grad_inner * up * (sig + act * (1.0 - sig))).astype(bf16)
            grads_sc[here, at_up] = (grad_inner * act).astype(bf16)
        return carry

    lax.fori_loop(0, cols // BLOCK // 3, chunk, 0)
    result = hidden + dot(inner_sc[here], down_sc[...]).T[:width]
    result = jnp.where(skip_ref[place_ref[0]] == 1, low, result.astype(bf16))

    @pl.when(mine)
    def _():
        res_own_ref[0] = result

    @pl.when(jnp.logical_not(mine))
    def _():
        res_away_ref[...] = result

    gn2 = dot(grads_sc[here], in_t_sc[...]).T[:width]
    c = gn2 * gain_two_ref[:, :1]
    dgain_sc[:, :1] += jnp.sum(gn2 * normed, 1, keepdims=True)
    gh = g.astype(f32) + inverse * (c - normed * jnp.mean(c * normed, 0, keepdims=True))
    gh_ref[...] = gh
    ga = gh.astype(bf16)
    ga_sc[here] = widen(ga.T)
    back_t = dot(w_out_ref[...], ga)
    for head in range(HQ):
        rows = (back_t[head * HD : (head + 1) * HD] * scale_sc[head, 0:1]).astype(bf16)
        dot_ref[head * HD : (head + 1) * HD] = rows
        delta_ref[head // GROUPS, head % GROUPS : head % GROUPS + 1] = jnp.sum(
            rows.astype(f32) * mixed[head * HD : (head + 1) * HD].astype(f32), 0, keepdims=True
        )

    @pl.when(step == pl.num_programs(0) - 1)
    def _():
        blocks = mixed_sc.shape[0]
        whole = lambda ref: jnp.concatenate([ref[k] for k in range(blocks)], 1)
        n2t_all, gt_all = whole(n2t_sc), whole(gt_sc)
        dw_out = dot(whole(mixed_sc), ga_sc[...])[:, :width].astype(bf16)
        line = dgain_sc[...].T[0:1]
        line = jnp.concatenate([line, jnp.zeros((1, lanes_up(width) - width), f32)], 1)
        lines = [line[:, k * 128 : (k + 1) * 128] for k in range(line.shape[1] // 128)]
        lines.append(jnp.zeros((GAIN_ROWS - len(lines), 128), f32))
        gain_rows = jnp.concatenate(lines, 0).astype(bf16)
        thin = 9 * width
        for h in range(2):
            target = pack_sc.at[2 + h]
            spot = pack_thin(target, thin, h, dw_out)
            target[spot : spot + GAIN_ROWS] = gain_rows

        def one_chunk(k, carry):
            at = pl.ds(pl.multiple_of(k * BLOCK, BLOCK), BLOCK)
            at_up = pl.ds(pl.multiple_of(cols + k * BLOCK, BLOCK), BLOCK)
            chain = jnp.where(k >= 3, 1, 0)
            third = k - 3 * chain
            for m, (left, right) in enumerate(
                ((n2t_all, grads_sc[:, at]), (n2t_all, grads_sc[:, at_up]), (gt_all, inner_sc[:, at]))
            ):
                both = dot(left, right).astype(bf16)
                for b in range(2):
                    half = jnp.where(third == 2, b, third)
                    spot = (3 * m + jnp.where(third == 2, 2, b)) * width
                    pack_sc[2 * chain + half, pl.ds(pl.multiple_of(spot, 16), width)] = both[:, b * 128 : (b + 1) * 128]
            for q in range(4):
                keep, send = pack_copies[q]
                pl.when((k == 3 * (q // 2) + 2) & (place_ref[0] == q % 2))(keep.start)
                pl.when((k == 3 * (q // 2) + 2) & (place_ref[0] != q % 2))(send.start)
            return carry

        pack_copies = []
        for q in range(4):
            targets = (keep_a_hbm, send_a_hbm) if q < 2 else (keep_b_hbm, send_b_hbm)
            source = pack_sc.at[q, pl.ds(0, targets[0].shape[0])]
            pack_copies.append([pltpu.make_async_copy(source, target, pack_sem.at[q]) for target in targets])
        lax.fori_loop(0, 6, one_chunk, 0)
        for keep, _ in pack_copies:
            keep.wait()
        soft_copy(blocks).wait()


def own_specs(width, near):
    own = pl.BlockSpec((1, width, BLOCK), lambda i, c, s: (c[0], 0, jnp.where(i >= near, i - near, i)))
    oth = pl.BlockSpec((width, BLOCK), lambda i, c, s: (0, jnp.where(i >= near, i - near, i)))
    return own, oth


def out_specs_halves(width, near):
    mine = pl.BlockSpec((1, width, BLOCK), lambda i, c, s: (c[0], 0, jnp.clip(i - near * c[0], 0, near - 1)))
    away = pl.BlockSpec((width, BLOCK), lambda i, c, s: (0, jnp.clip(i - near * (1 - c[0]), 0, near - 1)))
    return mine, away


def layer(
    rows_a, rows_b, place, skip, tokens, other, cot, cot_other, gain_one, wqkv_t, w_out_t, gain_two, cos_t, sin_t,
    starts, w_out, wg, wu, wdt,
):
    rows = 2 * tokens.shape[2]
    width = tokens.shape[1]
    cols = wg.shape[1]
    wide = lanes_up(width)
    blocks = rows // BLOCK
    own, oth = own_specs(width, blocks // 2)
    col = pl.BlockSpec((width, BLOCK), lambda i, c, s: (0, i))
    row_wide = pl.BlockSpec((BLOCK, wide), lambda i, c, s: (i, 0))
    small = pl.BlockSpec((HD // 2, BLOCK), lambda i, c, s: (0, i))
    const = lambda array: pl.BlockSpec(
        array.shape, lambda *_: (0,) * array.ndim, pipeline_mode=pl.Buffered(1)
    )
    any_spec = pl.BlockSpec(memory_space=pl.ANY)
    halves = [(rows_a, 128), (rows_a, 128), (rows_b, 128), (rows_b, 128)]
    out_shape = [
        jax.ShapeDtypeStruct((HQ * HD, rows), bf16),
        jax.ShapeDtypeStruct((KVH * HD, rows), bf16),
        jax.ShapeDtypeStruct((KVH, rows, HD), bf16),
        jax.ShapeDtypeStruct((blocks, HQ, rows, BLOCK), bf16),
        jax.ShapeDtypeStruct((rows, wide), bf16),
        jax.ShapeDtypeStruct((2, width, rows // 2), bf16),
        jax.ShapeDtypeStruct((width, rows // 2), bf16),
        jax.ShapeDtypeStruct((width, rows), f32),
        jax.ShapeDtypeStruct((HQ * HD, rows), bf16),
        jax.ShapeDtypeStruct((KVH, GROUPS, rows), f32),
    ] + [jax.ShapeDtypeStruct(shape, bf16) for shape in halves]
    return pl.pallas_call(
        layer_kernel,
        grid_spec=pltpu.PrefetchScalarGridSpec(
            num_scalar_prefetch=2,
            grid=(blocks,),
            in_specs=[
                own, oth, own, oth, const(gain_one), const(wqkv_t), const(w_out_t), const(gain_two),
                small, small, pl.BlockSpec(memory_space=pltpu.SMEM),
                const(w_out), any_spec, any_spec, any_spec,
            ],
            out_specs=[
                col,
                pl.BlockSpec((KVH * HD, BLOCK), lambda i, c, s: (0, i)),
                pl.BlockSpec((KVH, BLOCK, HD), lambda i, c, s: (0, i, 0)),
                any_spec,
                row_wide,
                *out_specs_halves(width, blocks // 2),
                col, col,
                pl.BlockSpec((KVH, GROUPS, BLOCK), lambda i, c, s: (0, 0, i)),
            ] + [any_spec] * 4,
            scratch_shapes=[
                pltpu.VMEM((KVH, rows, HD), bf16),
                pltpu.VMEM((blocks, KVH, HD + 16, BLOCK), bf16),
                pltpu.VMEM((blocks, HQ * HD, BLOCK), bf16),
                pltpu.VMEM((blocks, width, BLOCK), bf16),
                pltpu.VMEM((blocks, width, BLOCK), bf16),
                pltpu.VMEM((rows, cols), bf16),
                pltpu.VMEM((rows, 2 * cols), bf16),
                pltpu.VMEM((2 * cols, wide), bf16),
                pltpu.VMEM((cols, wide), bf16),
                pltpu.VMEM((rows, wide), bf16),
                pltpu.VMEM((width, 128), f32),
                pltpu.VMEM((HQ, 8, BLOCK), f32),
                pltpu.VMEM((HQ, rows, BLOCK), bf16),
                pltpu.VMEM(wg.shape, bf16),
                pltpu.VMEM(wu.shape, bf16),
                pltpu.VMEM(wdt.shape, bf16),
                pltpu.VMEM((4, rows_b, 128), bf16),
                pltpu.SemaphoreType.DMA((3,)),
                pltpu.SemaphoreType.DMA,
                pltpu.SemaphoreType.DMA((4,)),
            ],
        ),
        out_shape=out_shape,
        compiler_params=pltpu.CompilerParams(vmem_limit_bytes=VMEM),
        name="layer_forward",
        cost_estimate=cost(50),
    )(
        place, skip, tokens, other, cot, cot_other, gain_one, wqkv_t, w_out_t, gain_two, cos_t, sin_t, starts,
        w_out, wg, wu, wdt,
    )


def back_kernel(
    g, place_ref, soft_ref, qt_ref, kt_ref, vn_ref, dot_ref, delta_ref, cos_ref, sin_ref, n1_ref,
    dqkv_ref, keep_hbm, send_hbm,
    acc, ds_sc, pack_sc, pack_sem,
):
    step = pl.program_id(0)
    blocks = pl.num_programs(0)
    cosine, sine = cos_ref[...], sin_ref[...]

    @pl.when(step == 0)
    def _():
        acc[...] = jnp.zeros_like(acc)

    def attend(count):
        used = slice(0, count * BLOCK)
        here = slice((count - 1) * BLOCK, count * BLOCK)
        ups = [dot_ref[r * HD : (r + 1) * HD] for r in range(GROUPS)]
        soft_grads = [[dot(vn_ref[0, kb * BLOCK : (kb + 1) * BLOCK], up) for kb in range(count)] for up in ups]
        for r in range(GROUPS):
            rows = slice(r * HD, (r + 1) * HD)
            delta = delta_ref[0, r : r + 1]
            pair = jnp.concatenate([qt_ref[rows], ups[r]], 0).T
            left = lax.broadcasted_iota(jnp.int32, pair.shape, 1) < HD
            zero = jnp.zeros_like(pair)
            pads = jnp.concatenate([jnp.where(left, pair, zero), jnp.where(left, zero, pair)], 0)
            for kb in range(count):
                span = slice(kb * BLOCK, (kb + 1) * BLOCK)
                p = soft_ref[0, r, span]
                ds_sc[r, span, :BLOCK] = (p.astype(f32) * (soft_grads[r][kb] - delta)).astype(bf16)
                ds_sc[r, span, BLOCK:] = p
            acc[used] += dot(ds_sc[r, used], pads)
            dq = dot(kt_ref[:, used], ds_sc[r, used, :BLOCK])
            dqkv_ref[rows, here] = turn(dq * (HD**-0.5), cosine, sine, -1).astype(bf16)
        done = acc[here].T
        base = GROUPS * HD
        dqkv_ref[base : base + HD, here] = turn(done[:HD], cosine, sine, -1).astype(bf16)
        dqkv_ref[base + HD : base + 2 * HD, here] = done[HD:].astype(bf16)

    for count in range(1, 5):
        pl.when(step == 4 - count)(lambda count=count: attend(count))

    @pl.when(step == blocks - 1)
    def _():
        width = pack_sc.shape[1] * 128 * 2 // PER
        dw = dot(dqkv_ref[...], n1_ref[...])[:, :width].astype(bf16)
        span = pl.ds(g * pack_sc.shape[1], pack_sc.shape[1])
        copies = []
        for h in range(2):
            pack_thin(pack_sc.at[h], 0, h, dw)
            copies.append([pltpu.make_async_copy(pack_sc.at[h], t.at[span], pack_sem.at[h]) for t in (keep_hbm, send_hbm)])
            pl.when(place_ref[0] == h)(copies[h][0].start)
            pl.when(place_ref[0] != h)(copies[h][1].start)
        for keep, _ in copies:
            keep.wait()


def back(g, half_rows, width, place, soft, qt, kt, vn, dot_t, delta, cos_t, sin_t, n1, packed, after=()):
    blocks, _, rows, _ = soft.shape
    last = blocks - 1
    small = pl.BlockSpec((HD // 2, BLOCK), lambda i, c: (0, last - i))
    inputs = 10
    return pl.pallas_call(
        without(functools.partial(back_kernel, g), inputs, tuple(packed) + tuple(after)),
        grid_spec=pltpu.PrefetchScalarGridSpec(
            num_scalar_prefetch=1,
            grid=(blocks,),
            in_specs=[
                pl.BlockSpec((1, GROUPS, rows, BLOCK), lambda i, c: (last - i, g, 0, 0)),
                pl.BlockSpec((GROUPS * HD, BLOCK), lambda i, c: (g, last - i)),
                pl.BlockSpec((HD, rows), lambda i, c: (g, 0)),
                pl.BlockSpec((1, rows, HD), lambda i, c: (g, 0, 0)),
                pl.BlockSpec((GROUPS * HD, BLOCK), lambda i, c: (g, last - i)),
                pl.BlockSpec((1, GROUPS, BLOCK), lambda i, c: (g, 0, last - i)),
                small, small, full(n1.shape),
            ] + [ANY] * (len(packed) + len(after)),
            out_specs=[full((PER, rows)), ANY, ANY],
            scratch_shapes=[
                pltpu.VMEM((rows, 2 * HD), f32),
                pltpu.VMEM((GROUPS, rows, 2 * BLOCK), bf16),
                pltpu.VMEM((2, PER * width // 256, 128), bf16),
                pltpu.SemaphoreType.DMA((2,)),
            ],
        ),
        out_shape=[jax.ShapeDtypeStruct((PER, rows), bf16)] + [jax.ShapeDtypeStruct((half_rows, 128), bf16)] * 2,
        input_output_aliases={inputs + k: 1 + k for k in range(len(packed))},
        compiler_params=pltpu.CompilerParams(vmem_limit_bytes=VMEM),
        name="attention_backward",
        cost_estimate=cost(9),
    )(place, soft, qt, kt, vn, dot_t, delta, cos_t, sin_t, n1, *packed, *after)


def input_grad(place_ref, skip_ref, x_ref, cot_ref, gh_ref, parts, wqkv_ref, gain_one_ref):
    x = x_ref[...].reshape(gh_ref.shape).astype(f32)
    skipped = skip_ref[place_ref[0]] == 1
    inverse = lax.rsqrt(jnp.mean(x * x, 0, keepdims=True) + eps_norm)
    normed = x * inverse
    dqkv = jnp.concatenate([part[...] for part in parts], 0)
    c = dot(wqkv_ref[...], dqkv) * gain_one_ref[:, :1]
    gx = gh_ref[...] + inverse * (c - normed * jnp.mean(c * normed, 0, keepdims=True))
    return jnp.where(skipped, cot_ref[...].reshape(gh_ref.shape), gx.astype(bf16))


def away_kernel(
    place_ref, skip_ref, x_ref, cot_ref, gh_ref, d0_ref, d1_ref, d2_ref, wqkv_ref, gain_one_ref, grad_ref
):
    grad_ref[...] = input_grad(
        place_ref, skip_ref, x_ref, cot_ref, gh_ref, (d0_ref, d1_ref, d2_ref), wqkv_ref, gain_one_ref
    )


def own_kernel(
    place_ref, skip_ref, x_ref, cot_ref, gh_ref, d0_ref, d1_ref, d2_ref, wqkv_ref, gain_one_ref,
    grad_got, result_got, result_in, grad_hbm, result_hbm,
    block_sc, sem, got_sem,
):
    step = pl.program_id(0)
    steps = block_sc.shape[0]
    own, away = place_ref[0], 1 - place_ref[0]
    gots = [
        pltpu.make_async_copy(source, target.at[away], got_sem.at[k])
        for k, (source, target) in enumerate(((grad_got, grad_hbm), (result_got, result_hbm)))
    ]
    copies = [
        pltpu.make_async_copy(block_sc.at[k], grad_hbm.at[own, :, pl.ds(k * BLOCK, BLOCK)], sem.at[k]) for k in range(steps)
    ]

    @pl.when(step == 0)
    def _():
        for copy in gots:
            copy.start()

    gx = input_grad(place_ref, skip_ref, x_ref, cot_ref, gh_ref, (d0_ref, d1_ref, d2_ref), wqkv_ref, gain_one_ref)
    for k in range(steps):
        @pl.when(step == k)
        def _():
            block_sc[k] = gx
            copies[k].start()

    @pl.when(step == steps - 1)
    def _():
        for copy in copies + gots:
            copy.wait()


def last(mine, place, skip, x, cot, gh, parts, wqkv_n, gain_one, gots=(), after=()):
    width, rows = gh.shape
    near = rows // BLOCK // 2
    if mine:
        source = pl.BlockSpec((1, width, BLOCK), lambda i, c, s: (c[0], 0, i))
        at = lambda i, c, s: (0, near * c[0] + i)
        kernel, out_specs, aliases = own_kernel, [ANY, ANY], {12: 1}
        out_shape = [jax.ShapeDtypeStruct(x.shape, bf16)] * 2
        scratch = [pltpu.VMEM((near, width, BLOCK), bf16), pltpu.SemaphoreType.DMA((near,)), pltpu.SemaphoreType.DMA((2,))]
    else:
        source = pl.BlockSpec((width, BLOCK), lambda i, c, s: (0, i))
        at = lambda i, c, s: (0, near * (1 - c[0]) + i)
        kernel, out_specs, aliases = away_kernel, source, {}
        out_shape = jax.ShapeDtypeStruct(x.shape, bf16)
        scratch = []
    col = pl.BlockSpec((width, BLOCK), at)
    part = pl.BlockSpec((PER, BLOCK), at)
    return pl.pallas_call(
        without(kernel, 10 + len(gots), after),
        grid_spec=pltpu.PrefetchScalarGridSpec(
            num_scalar_prefetch=2,
            grid=(near,),
            in_specs=[source, source, col, part, part, part, full(wqkv_n.shape), full((width, 128))]
            + [full(got.shape) for got in gots[:2]] + [ANY] * (len(gots[2:]) + len(after)),
            out_specs=out_specs,
            scratch_shapes=scratch,
        ),
        out_shape=out_shape,
        input_output_aliases=aliases,
        compiler_params=pltpu.CompilerParams(vmem_limit_bytes=VMEM),
        name="input_backward",
        cost_estimate=cost(4),
    )(place, skip, x, cot, gh, *parts, wqkv_n, gain_one, *gots, *after)


def rotary_rows(rows):
    frequency = theta_base ** (-2.0 * np.arange(HD // 2, dtype=np.float64) / HD)
    angles = frequency[:, None] * np.arange(rows, dtype=np.float64)[None, :]
    return np.cos(angles).astype(np.float32), np.sin(angles).astype(np.float32)


def swap_core(array):
    return lax.ppermute(array, "narrow", [(0, 1), (1, 0)])


def axis_orders(bits, turn_index):
    if bits == 4:
        return (((0, 1, 2, 3), (1, 2, 3, 0)), ((1, 2, 0, 3), (2, 0, 1, 3)), ((0, 1, 2, 3), (1, 0, 2, 3)))[turn_index]
    base = tuple(range(bits))
    shift = bits // 2
    return base, base[shift:] + base[:shift]


class Summer:
    def __init__(self, core, chips, turn_index, exchanges):
        self.core = core
        self.chips = chips
        self.bits = chips.bit_length() - 1
        self.halvings = self.bits - exchanges
        self.orders = axis_orders(self.bits, turn_index)
        self.place = lax.axis_index("wide")
        self.stage = 0

    def bit(self, step):
        by_core = [(self.place >> order[step]) & 1 for order in self.orders]
        return jnp.where(self.core == 0, by_core[0], by_core[1])

    def swap(self, array, step):
        pairs = [
            (2 * chip + c, 2 * (chip ^ (1 << self.orders[c][step])) + c) for chip in range(self.chips) for c in range(2)
        ]
        return lax.ppermute(array, ("wide", "narrow"), pairs)

    def first(self, keep, send):
        self.keep, self.got = keep, swap_core(send)

    def advance(self, line):
        if line.last is not None:
            self.keep, self.got, _ = lax.optimization_barrier((self.keep, self.got, line.last))
        if self.stage < self.halvings:
            bit = self.bit(self.stage)
            half = self.keep.shape[0] // 2

            def part(which):
                a = lax.dynamic_slice_in_dim(self.keep, which * half, half, 0).astype(f32)
                b = lax.dynamic_slice_in_dim(self.got, which * half, half, 0).astype(f32)
                return (a + b).astype(bf16)

            line.last = part(1 - bit)
            self.keep, self.got = part(bit), self.swap(line.last, self.stage)
        elif self.stage <= self.bits:
            line.last = self.keep = (self.keep.astype(f32) + self.got.astype(f32)).astype(bf16)
            axis = self.stage if self.stage < self.bits else self.halvings - 1
            self.got = self.swap(self.keep, axis)
        else:
            step = self.halvings + self.bits - self.stage
            low = self.bit(step) == 0
            line.last = self.keep = jnp.where(
                low, jnp.concatenate([self.keep, self.got], 0), jnp.concatenate([self.got, self.keep], 0)
            )
            self.got = self.swap(self.keep, step - 1) if step else swap_core(self.keep)
        self.stage += 1

    @property
    def done(self):
        return self.stage > self.bits + self.halvings


class Line:
    last = None

    def after(self):
        return () if self.last is None else (self.last,)


def unpack_kernel(chain, place_ref, own_hbm, got_hbm, *refs):
    own, got, sem = refs[-3:]
    gate_ref, up_ref, down_ref = refs[-8:-5] if chain else refs[:3]
    step = pl.program_id(0)
    width = gate_ref.shape[0]
    copies = [
        pltpu.make_async_copy(source, target, sem.at[k]) for k, (source, target) in enumerate(((own_hbm, own), (got_hbm, got)))
    ]

    @pl.when(step == 0)
    def _():
        for copy in copies:
            copy.start()
        for copy in copies:
            copy.wait()

    def take(halves):
        for third in range(3):
            blocks = ((halves[0], 2), (halves[1], 2)) if third == 2 else ((halves[third], 0), (halves[third], 1))

            @pl.when(step == third)
            def _():
                for m, target in enumerate((gate_ref, up_ref, down_ref)):
                    for b, (source, place) in enumerate(blocks):
                        spot = (3 * m + place) * width
                        target[:, b * 128 : (b + 1) * 128] = source[spot : spot + width].astype(f32)

    pl.when(place_ref[0] == 0)(lambda: take((own, got)))
    pl.when(place_ref[0] != 0)(lambda: take((got, own)))

    if chain:
        w_out_ref, gain_ref = refs[-5:-3]

        def take_rest(first, second):
            spot = 9 * width
            unpack_thin(w_out_ref, first, second, spot)
            spot += width // 128 // 2 * width + width // 4
            rows = first[spot : spot + GAIN_ROWS].astype(f32)
            line = jnp.concatenate([rows[k : k + 1] for k in range(lanes_up(width) // 128)], 1)
            gain_ref[...] = line[:, :width].reshape(width)

        pl.when((step == 0) & (place_ref[0] == 0))(lambda: take_rest(own, got))
        pl.when((step == 0) & (place_ref[0] != 0))(lambda: take_rest(got, own))


def unpack(chain, place, buffers, width, inner, earlier):
    spec = pl.BlockSpec((width, BLOCK), lambda i, c: (0, 3 * chain + i))
    out_specs = [spec, spec, spec]
    out_shape = [jax.ShapeDtypeStruct((width, inner), f32)] * 3
    if chain:
        out_specs += [full((HQ * HD, width)), full((width,))]
        out_shape += [jax.ShapeDtypeStruct((HQ * HD, width), f32), jax.ShapeDtypeStruct((width,), f32)]
    return pl.pallas_call(
        functools.partial(unpack_kernel, chain),
        grid_spec=pltpu.PrefetchScalarGridSpec(
            num_scalar_prefetch=1,
            grid=(3,),
            in_specs=[pl.BlockSpec(memory_space=pltpu.HBM)] * 2 + [ANY] * len(earlier),
            out_specs=out_specs,
            scratch_shapes=[pltpu.VMEM(b.shape, bf16) for b in buffers] + [pltpu.SemaphoreType.DMA((2,))],
        ),
        out_shape=out_shape,
        input_output_aliases={3 + k: k for k in range(len(earlier))},
        compiler_params=pltpu.CompilerParams(vmem_limit_bytes=VMEM),
        name="unpack_mlp",
        cost_estimate=cost(4),
    )(place, *buffers, *earlier)


def unpack_last_kernel(place_ref, own_ref, got_ref, wqkv_ref, gain_one_ref, dq_ref, dkt_ref, dvt_ref, gain_ref, all_sc):
    q_cols = GROUPS * HD

    def take(first, second):
        for g in range(KVH):
            unpack_thin(all_sc.at[g * PER : (g + 1) * PER], first, second, g * PER * all_sc.shape[1] // 256)

    pl.when(place_ref[0] == 0)(lambda: take(own_ref, got_ref))
    pl.when(place_ref[0] != 0)(lambda: take(got_ref, own_ref))
    both = all_sc[...]
    dq = []
    for g in range(KVH):
        dq.append(both[g * PER : g * PER + q_cols])
        dkt_ref[g * HD : (g + 1) * HD] = both[g * PER + q_cols : g * PER + q_cols + HD]
        dvt_ref[g * HD : (g + 1) * HD] = both[g * PER + q_cols + HD : (g + 1) * PER]
    dq_ref[...] = jnp.concatenate(dq, 0).T
    gain = jnp.sum(both * wqkv_ref[...].astype(f32), 0, keepdims=True) / gain_one_ref[...]
    gain_ref[...] = gain.reshape(gain_ref.shape)


def unpack_last(place, own, got, wqkv_t, gain_one, after):
    width = wqkv_t.shape[1]
    shapes = [(width, HQ * HD), (KVH * HD, width), (KVH * HD, width), (width,)]
    return pl.pallas_call(
        without(unpack_last_kernel, 5, after),
        grid_spec=pltpu.PrefetchScalarGridSpec(
            num_scalar_prefetch=1,
            grid=(1,),
            in_specs=[full(own.shape)] * 2 + [full(wqkv_t.shape), full((1, width))] + [ANY] * len(after),
            out_specs=[full(shape) for shape in shapes],
            scratch_shapes=[pltpu.VMEM(wqkv_t.shape, f32)],
        ),
        out_shape=[jax.ShapeDtypeStruct(shape, f32) for shape in shapes],
        compiler_params=pltpu.CompilerParams(vmem_limit_bytes=VMEM),
        name="unpack_attention",
        cost_estimate=cost(3),
    )(place, own, got, wqkv_t, gain_one, *after)


def flip(array):
    return jnp.swapaxes(array, -1, -2)


def per_device(tokens, doc_starts, skip_flags, cotangent, attn_gain, wq, wk, wv, w_out, mlp_gain, wg, wu, wd):
    core = lax.axis_index("narrow")
    chips = lax.axis_size("wide")
    tokens, cotangent = flip(tokens), flip(cotangent)
    rows = 2 * tokens.shape[2]
    width = tokens.shape[1]
    inner = wg.shape[1]
    place = core.astype(jnp.int32).reshape(1)
    skip = skip_flags
    other = swap_core(lax.dynamic_index_in_dim(tokens, 1 - core, 0, keepdims=False))
    cot_other = swap_core(lax.dynamic_index_in_dim(cotangent, 1 - core, 0, keepdims=False))
    cos_t, sin_t = rotary_rows(rows)
    wdt = flip(wd)
    wqkv_t, wqkv_n, w_out_t, gain_one, gain_two, gain_line = prelude(wq, flip(wk), flip(wv), w_out, attn_gain, mlp_gain)
    unit = 16 * chips

    def half_rows(count):
        return -(-count // unit) * unit

    mlp_rows = 3 * width * inner // 4 // 128
    thin = width // 128 // 2
    out_rows = thin * HQ * HD + HQ * HD // 4 + GAIN_ROWS
    rest_rows = thin * KVH * PER + KVH * PER // 4

    (
        qt, kt, vn, soft, n1, res_own, res_away, gh, dot_t, delta, keep_a, send_a, keep_b, send_b,
    ) = layer(
        half_rows(mlp_rows), half_rows(mlp_rows + out_rows),
        place, skip, tokens, other, cotangent, cot_other, gain_one, wqkv_t, w_out_t, gain_two, cos_t, sin_t,
        doc_starts, w_out, wg, wu, wdt,
    )
    a_sum, b_sum, c_sum = (Summer(core, chips, k, exchanges) for k, exchanges in ((0, 0), (1, 0), (2, 2)))
    a_sum.first(keep_a, send_a)
    b_sum.first(keep_b, send_b)
    line = Line()
    parts, packed = [], ()
    for g in range(KVH):
        part, *packed = back(
            g, half_rows(rest_rows), width, place, soft, qt, kt, vn, dot_t, delta, cos_t, sin_t, n1, packed, line.after()
        )
        parts.append(part)
        line.last = part
        if g == KVH - 1:
            c_sum.first(*packed)
        a_sum.advance(line)
        b_sum.advance(line)
    grad_away = last(False, place, skip, other, cot_other, gh, parts, wqkv_n, gain_one, (), line.after())
    line.last = grad_away
    for chain in (c_sum, a_sum, b_sum):
        chain.advance(line)
    grad_got = swap_core(grad_away)
    for chain in (c_sum, a_sum, b_sum):
        chain.advance(line)
    line.last = grad_got
    result_got = swap_core(res_away)
    for chain in (c_sum, a_sum, b_sum, c_sum, a_sum, b_sum, c_sum, c_sum, a_sum, b_sum):
        chain.advance(line)
    c_sum.advance(line)
    grad_x, result = last(
        True, place, skip, tokens, cotangent, gh, parts, wqkv_n, gain_one, (grad_got, result_got, res_own), line.after()
    )
    line.last = grad_x
    a_sum.advance(line)
    for chain in (a_sum, c_sum):
        while not chain.done:
            chain.advance(line)
    dq, dkt, dvt, dgain_one = unpack_last(place, c_sum.keep, c_sum.got, wqkv_t, gain_line, line.after())
    line.last = dgain_one
    while not b_sum.done:
        b_sum.advance(line)
    first = unpack(0, place, (a_sum.keep, a_sum.got), width, inner, ())
    dwg, dwu, dwdt, dwo, dgain_two = unpack(1, place, (b_sum.keep, b_sum.got), width, inner, first)
    return (
        flip(result), flip(grad_x),
        dgain_one, dq, flip(dkt), flip(dvt), dwo, dgain_two, dwg, dwu, flip(dwdt),
    )


def solution(mesh):
    split = P("wide", "narrow", None)
    in_specs = (split, P("wide", None), P("wide"), split) + (P(),) * 9
    out_specs = (split, split) + (P(),) * 9
    return jax.shard_map(per_device, mesh=mesh, in_specs=in_specs, out_specs=out_specs, check_vma=False)
```

```python
import functools

import jax
import jax.numpy as jnp
import numpy as np
from jax import lax
from jax.experimental import pallas as pl
from jax.experimental.pallas import tpu as pltpu
from jax.sharding import PartitionSpec as P

HQ = 9
KVH = 3
HD = 64
GROUPS = HQ // KVH
PER = (GROUPS + 2) * HD
theta_base = 100000.0
eps_norm = 1e-05
masked_score = -1e30
BLOCK = 256
GAIN_ROWS = 16
VMEM = 60 * 2**20
f32 = jnp.float32
bf16 = jnp.bfloat16


def cost(microseconds):
    return pl.CostEstimate(flops=int(microseconds * 1.0e9), bytes_accessed=1024, transcendentals=0)


def dot(a, b, ca=1, cb=0):
    return lax.dot_general(a, b, (((ca,), (cb,)), ((), ())), preferred_element_type=f32)


def turn(rows, cosine, sine, sign):
    half = HD // 2
    first, second = rows[:half], rows[half:]
    if sign > 0:
        return jnp.concatenate([first * cosine - second * sine, second * cosine + first * sine], 0)
    return jnp.concatenate([first * cosine + second * sine, second * cosine - first * sine], 0)


def lanes_up(count):
    return -(-count // 128) * 128


ANY = pl.BlockSpec(memory_space=pl.ANY)


def without(kernel, inputs, after):
    return lambda *refs: kernel(*refs[:inputs], *refs[inputs + len(after) :])


def full(shape):
    return pl.BlockSpec(shape, lambda *_: (0,) * len(shape))


def widen(matrix):
    extra = lanes_up(matrix.shape[1]) - matrix.shape[1]
    return jnp.concatenate([matrix, jnp.zeros((matrix.shape[0], extra), matrix.dtype)], 1)


def pack_blocks(target, spot, matrix):
    for k in range(matrix.shape[1] // 128):
        target[spot : spot + matrix.shape[0]] = matrix[:, k * 128 : (k + 1) * 128]
        spot += matrix.shape[0]
    return spot


def pack_thin(target, spot, h, matrix):
    rows = matrix.shape[0]
    quarter = rows // 4
    base = matrix.shape[1] // 128
    for k in range(h * base // 2, (h + 1) * base // 2):
        target[spot : spot + rows] = matrix[:, k * 128 : (k + 1) * 128]
        spot += rows
    left = matrix[2 * h * quarter : (2 * h + 1) * quarter, base * 128 :]
    right = matrix[(2 * h + 1) * quarter : (2 * h + 2) * quarter, base * 128 :]
    target[spot : spot + quarter] = jnp.concatenate([left, right], 1)
    return spot + quarter


def unpack_thin(target, first, second, spot):
    rows, width = target.shape
    quarter = rows // 4
    base = width // 128
    for h, source in enumerate((first, second)):
        at = spot
        for k in range(h * base // 2, (h + 1) * base // 2):
            target[:, k * 128 : (k + 1) * 128] = source[at : at + rows].astype(f32)
            at += rows
        last = source[at : at + quarter].astype(f32)
        target[2 * h * quarter : (2 * h + 1) * quarter, base * 128 :] = last[:, : width - base * 128]
        target[(2 * h + 1) * quarter : (2 * h + 2) * quarter, base * 128 :] = last[:, width - base * 128 :]


def prelude_kernel(wq_ref, wkt_ref, wvt_ref, w_out_ref, gain_one_ref, gain_two_ref, t_ref, n_ref, out_t_ref, g1_ref, g2_ref, line_ref):
    q_cols = GROUPS * HD
    wqt = wq_ref[...].T
    for g in range(KVH):
        t_ref[g * PER : g * PER + q_cols] = wqt[g * q_cols : (g + 1) * q_cols]
        t_ref[g * PER + q_cols : g * PER + q_cols + HD] = wkt_ref[g * HD : (g + 1) * HD]
        t_ref[g * PER + q_cols + HD : (g + 1) * PER] = wvt_ref[g * HD : (g + 1) * HD]
    n_ref[...] = t_ref[...].T
    out_t_ref[...] = w_out_ref[...].T
    for source, target in ((gain_one_ref, g1_ref), (gain_two_ref, g2_ref)):
        gain = source[...].astype(f32).reshape(1, source.shape[0])
        target[...] = jnp.broadcast_to(gain, (128, source.shape[0])).T
    line_ref[...] = gain_one_ref[...].astype(f32).reshape(line_ref.shape)


def prelude(wq, wkt, wvt, w_out, gain_one, gain_two):
    width = wq.shape[0]
    return pl.pallas_call(
        prelude_kernel,
        out_shape=[
            jax.ShapeDtypeStruct((KVH * PER, width), bf16),
            jax.ShapeDtypeStruct((width, KVH * PER), bf16),
            jax.ShapeDtypeStruct((width, w_out.shape[0]), bf16),
            jax.ShapeDtypeStruct((width, 128), f32),
            jax.ShapeDtypeStruct((width, 128), f32),
            jax.ShapeDtypeStruct((1, width), f32),
        ],
        compiler_params=pltpu.CompilerParams(vmem_limit_bytes=VMEM),
        name="prelude",
        cost_estimate=cost(4),
    )(wq, wkt, wvt, w_out, gain_one, gain_two)


def layer_kernel(
    place_ref, skip_ref, own_ref, other_ref, cot_own_ref, cot_other_ref,
    gain_one_ref, wqkv_ref, w_out_t_ref, gain_two_ref, cos_ref, sin_ref, start_ref,
    w_out_ref, w_gate_hbm, w_up_hbm, w_down_hbm,
    qt_ref, kt_ref, vn_ref, soft_hbm, n1_ref,
    res_own_ref, res_away_ref, gh_ref, dot_ref, delta_ref, keep_a_hbm, send_a_hbm, keep_b_hbm, send_b_hbm,
    kn_all, vt_all, mixed_sc, n2t_sc, gt_sc, inner_sc, grads_sc, in_t_sc, down_sc, ga_sc, dgain_sc,
    scale_sc, soft_sc, w_gate_ref, w_up_ref, w_down_ref, pack_sc, weight_sem, soft_sem, pack_sem,
):
    step = pl.program_id(0)
    mine = (step >= 2).astype(jnp.int32) == place_ref[0]
    width = other_ref.shape[0]
    cols = w_gate_hbm.shape[1]

    weight_copies = [
        pltpu.make_async_copy(source, target, weight_sem.at[k])
        for k, (source, target) in enumerate(
            ((w_gate_hbm, w_gate_ref), (w_up_hbm, w_up_ref), (w_down_hbm, w_down_ref))
        )
    ]

    @pl.when(step == 0)
    def _():
        for copy in weight_copies:
            copy.start()
        dgain_sc[...] = jnp.zeros_like(dgain_sc)

    low = jnp.where(mine, own_ref[0], other_ref[...])
    x = low.astype(f32)
    cot = jnp.where(mine, cot_own_ref[0], cot_other_ref[...])
    g = jnp.where(skip_ref[place_ref[0]] == 1, jnp.zeros_like(cot), cot)
    gt_sc[step] = g
    inverse = lax.rsqrt(jnp.mean(x * x, 0, keepdims=True) + eps_norm)
    n1 = (x * inverse * gain_one_ref[:, :1]).astype(bf16)
    n1_ref[...] = widen(n1.T)
    qkv = dot(wqkv_ref[...], n1)
    cosine, sine = cos_ref[...], sin_ref[...]
    here = pl.ds(pl.multiple_of(step * BLOCK, BLOCK), BLOCK)
    for group in range(KVH):
        for r in range(GROUPS):
            head = group * GROUPS + r
            base = group * PER + r * HD
            rows = (turn(qkv[base : base + HD], cosine, sine, 1) * (HD**-0.5)).astype(bf16)
            qt_ref[head * HD : (head + 1) * HD] = rows
        base = group * PER + GROUPS * HD
        rows = turn(qkv[base : base + HD], cosine, sine, 1).astype(bf16)
        kt_ref[group * HD : (group + 1) * HD] = rows
        kn_all[group, here] = rows.T
        rows = qkv[base + HD : base + 2 * HD].astype(bf16)
        vt_all[step, group] = jnp.concatenate([rows, jnp.ones((16, BLOCK), bf16)], 0)
        vn_ref[group] = rows.T

    pos = step * BLOCK + lax.broadcasted_iota(jnp.int32, (1, BLOCK), 1)
    start_row = jnp.zeros((1, BLOCK), jnp.int32)
    for k in range(start_ref.shape[1]):
        first = start_ref[place_ref[0], k]
        start_row = jnp.where(pos >= first, first, start_row)

    def soft_copy(count):
        used = pl.ds(0, count * BLOCK)
        return pltpu.make_async_copy(soft_sc.at[:, used], soft_hbm.at[count - 1, :, used], soft_sem)

    def attend(count):
        t = lax.broadcasted_iota(jnp.int32, (BLOCK, BLOCK), 0)
        s_pos = lax.broadcasted_iota(jnp.int32, (BLOCK, BLOCK), 1)
        if count > 1:
            soft_copy(count - 1).wait()

        def one_group(group, carry):
            def scores_of(r):
                rows = pl.ds(pl.multiple_of((group * GROUPS + r) * HD, HD), HD)
                q = qt_ref[rows]
                scores = []
                for kb in range(count):
                    s = dot(kn_all[group, kb * BLOCK : (kb + 1) * BLOCK], q)
                    ok = t + kb * BLOCK >= start_row
                    if kb == count - 1:
                        ok = ok & (t <= s_pos)
                    scores.append(jnp.where(ok, s, masked_score))
                return scores

            def finish(r, scores):
                head = group * GROUPS + r
                rows = pl.ds(pl.multiple_of(head * HD, HD), HD)
                peak = scores[0].max(0, keepdims=True)
                for s in scores[1:]:
                    peak = jnp.maximum(peak, s.max(0, keepdims=True))
                out = None
                for kb in range(count):
                    p = jnp.exp(scores[kb] - peak).astype(bf16)
                    soft_sc[head, kb * BLOCK : (kb + 1) * BLOCK] = p
                    term = dot(vt_all[kb, group], p)
                    out = term if out is None else out + term
                scale = 1.0 / out[HD : HD + 1]
                scale_sc[head] = jnp.broadcast_to(scale, scale_sc.shape[1:])
                mixed_sc[step, rows] = (out[:HD] * scale).astype(bf16)

            every = [scores_of(r) for r in range(GROUPS)]
            for r in range(GROUPS):
                finish(r, every[r])
            return carry

        lax.fori_loop(0, KVH, one_group, 0)
        soft_copy(count).start()

    for count in range(1, 5):
        pl.when(step == count - 1)(lambda count=count: attend(count))

    @pl.when(step == 0)
    def _():
        for copy in weight_copies:
            copy.wait()
        for k, ref in enumerate((w_gate_ref, w_up_ref)):
            in_t_sc[k * cols : (k + 1) * cols] = widen(ref[...].T)
        down_sc[...] = widen(w_down_ref[...].T)

    mixed = mixed_sc[step]
    hidden = x + dot(w_out_t_ref[...], mixed)
    inverse = lax.rsqrt(jnp.mean(hidden * hidden, 0, keepdims=True) + eps_norm)
    normed = hidden * inverse
    n2t = (normed * gain_two_ref[:, :1]).astype(bf16)
    n2t_sc[step] = n2t
    n2 = n2t.T
    gn = g.T

    def chunk(k, carry):
        work = []
        for c in range(3):
            at = pl.ds(pl.multiple_of((3 * k + c) * BLOCK, BLOCK), BLOCK)
            at_up = pl.ds(pl.multiple_of(cols + (3 * k + c) * BLOCK, BLOCK), BLOCK)
            work.append((at, at_up, dot(n2, w_gate_ref[:, at]), dot(n2, w_up_ref[:, at]), dot(gn, w_down_ref[:, at])))
        for at, at_up, gate, up, grad_inner in work:
            sig = jax.nn.sigmoid(gate)
            act = gate * sig
            inner_sc[here, at] = (act * up).astype(bf16)
            grads_sc[here, at] = (grad_inner * up * (sig + act * (1.0 - sig))).astype(bf16)
            grads_sc[here, at_up] = (grad_inner * act).astype(bf16)
        return carry

    lax.fori_loop(0, cols // BLOCK // 3, chunk, 0)
    result = hidden + dot(inner_sc[here], down_sc[...]).T[:width]
    result = jnp.where(skip_ref[place_ref[0]] == 1, low, result.astype(bf16))

    @pl.when(mine)
    def _():
        res_own_ref[0] = result

    @pl.when(jnp.logical_not(mine))
    def _():
        res_away_ref[...] = result

    gn2 = dot(grads_sc[here], in_t_sc[...]).T[:width]
    c = gn2 * gain_two_ref[:, :1]
    dgain_sc[:, :1] += jnp.sum(gn2 * normed, 1, keepdims=True)
    gh = g.astype(f32) + inverse * (c - normed * jnp.mean(c * normed, 0, keepdims=True))
    gh_ref[...] = gh
    ga = gh.astype(bf16)
    ga_sc[here] = widen(ga.T)
    back_t = dot(w_out_ref[...], ga)
    for head in range(HQ):
        rows = (back_t[head * HD : (head + 1) * HD] * scale_sc[head, 0:1]).astype(bf16)
        dot_ref[head * HD : (head + 1) * HD] = rows
        delta_ref[head // GROUPS, head % GROUPS : head % GROUPS + 1] = jnp.sum(
            rows.astype(f32) * mixed[head * HD : (head + 1) * HD].astype(f32), 0, keepdims=True
        )

    @pl.when(step == pl.num_programs(0) - 1)
    def _():
        blocks = mixed_sc.shape[0]
        whole = lambda ref: jnp.concatenate([ref[k] for k in range(blocks)], 1)
        n2t_all, gt_all = whole(n2t_sc), whole(gt_sc)
        dw_out = dot(whole(mixed_sc), ga_sc[...])[:, :width].astype(bf16)
        line = dgain_sc[...].T[0:1]
        line = jnp.concatenate([line, jnp.zeros((1, lanes_up(width) - width), f32)], 1)
        lines = [line[:, k * 128 : (k + 1) * 128] for k in range(line.shape[1] // 128)]
        lines.append(jnp.zeros((GAIN_ROWS - len(lines), 128), f32))
        gain_rows = jnp.concatenate(lines, 0).astype(bf16)
        thin = 9 * width
        for h in range(2):
            target = pack_sc.at[2 + h]
            spot = pack_thin(target, thin, h, dw_out)
            target[spot : spot + GAIN_ROWS] = gain_rows

        def one_chunk(k, carry):
            at = pl.ds(pl.multiple_of(k * BLOCK, BLOCK), BLOCK)
            at_up = pl.ds(pl.multiple_of(cols + k * BLOCK, BLOCK), BLOCK)
            chain = jnp.where(k >= 3, 1, 0)
            third = k - 3 * chain
            for m, (left, right) in enumerate(
                ((n2t_all, grads_sc[:, at]), (n2t_all, grads_sc[:, at_up]), (gt_all, inner_sc[:, at]))
            ):
                both = dot(left, right).astype(bf16)
                for b in range(2):
                    half = jnp.where(third == 2, b, third)
                    spot = (3 * m + jnp.where(third == 2, 2, b)) * width
                    pack_sc[2 * chain + half, pl.ds(pl.multiple_of(spot, 16), width)] = both[:, b * 128 : (b + 1) * 128]
            for q in range(4):
                keep, send = pack_copies[q]
                pl.when((k == 3 * (q // 2) + 2) & (place_ref[0] == q % 2))(keep.start)
                pl.when((k == 3 * (q // 2) + 2) & (place_ref[0] != q % 2))(send.start)
            return carry

        pack_copies = []
        for q in range(4):
            targets = (keep_a_hbm, send_a_hbm) if q < 2 else (keep_b_hbm, send_b_hbm)
            source = pack_sc.at[q, pl.ds(0, targets[0].shape[0])]
            pack_copies.append([pltpu.make_async_copy(source, target, pack_sem.at[q]) for target in targets])
        lax.fori_loop(0, 6, one_chunk, 0)
        for keep, _ in pack_copies:
            keep.wait()
        soft_copy(blocks).wait()


def own_specs(width, near):
    own = pl.BlockSpec((1, width, BLOCK), lambda i, c, s: (c[0], 0, jnp.where(i >= near, i - near, i)))
    oth = pl.BlockSpec((width, BLOCK), lambda i, c, s: (0, jnp.where(i >= near, i - near, i)))
    return own, oth


def out_specs_halves(width, near):
    mine = pl.BlockSpec((1, width, BLOCK), lambda i, c, s: (c[0], 0, jnp.clip(i - near * c[0], 0, near - 1)))
    away = pl.BlockSpec((width, BLOCK), lambda i, c, s: (0, jnp.clip(i - near * (1 - c[0]), 0, near - 1)))
    return mine, away


def layer(
    rows_a, rows_b, place, skip, tokens, other, cot, cot_other, gain_one, wqkv_t, w_out_t, gain_two, cos_t, sin_t,
    starts, w_out, wg, wu, wdt,
):
    rows = 2 * tokens.shape[2]
    width = tokens.shape[1]
    cols = wg.shape[1]
    wide = lanes_up(width)
    blocks = rows // BLOCK
    own, oth = own_specs(width, blocks // 2)
    col = pl.BlockSpec((width, BLOCK), lambda i, c, s: (0, i))
    row_wide = pl.BlockSpec((BLOCK, wide), lambda i, c, s: (i, 0))
    small = pl.BlockSpec((HD // 2, BLOCK), lambda i, c, s: (0, i))
    const = lambda array: pl.BlockSpec(
        array.shape, lambda *_: (0,) * array.ndim, pipeline_mode=pl.Buffered(1)
    )
    any_spec = pl.BlockSpec(memory_space=pl.ANY)
    halves = [(rows_a, 128), (rows_a, 128), (rows_b, 128), (rows_b, 128)]
    out_shape = [
        jax.ShapeDtypeStruct((HQ * HD, rows), bf16),
        jax.ShapeDtypeStruct((KVH * HD, rows), bf16),
        jax.ShapeDtypeStruct((KVH, rows, HD), bf16),
        jax.ShapeDtypeStruct((blocks, HQ, rows, BLOCK), bf16),
        jax.ShapeDtypeStruct((rows, wide), bf16),
        jax.ShapeDtypeStruct((2, width, rows // 2), bf16),
        jax.ShapeDtypeStruct((width, rows // 2), bf16),
        jax.ShapeDtypeStruct((width, rows), f32),
        jax.ShapeDtypeStruct((HQ * HD, rows), bf16),
        jax.ShapeDtypeStruct((KVH, GROUPS, rows), f32),
    ] + [jax.ShapeDtypeStruct(shape, bf16) for shape in halves]
    return pl.pallas_call(
        layer_kernel,
        grid_spec=pltpu.PrefetchScalarGridSpec(
            num_scalar_prefetch=2,
            grid=(blocks,),
            in_specs=[
                own, oth, own, oth, const(gain_one), const(wqkv_t), const(w_out_t), const(gain_two),
                small, small, pl.BlockSpec(memory_space=pltpu.SMEM),
                const(w_out), any_spec, any_spec, any_spec,
            ],
            out_specs=[
                col,
                pl.BlockSpec((KVH * HD, BLOCK), lambda i, c, s: (0, i)),
                pl.BlockSpec((KVH, BLOCK, HD), lambda i, c, s: (0, i, 0)),
                any_spec,
                row_wide,
                *out_specs_halves(width, blocks // 2),
                col, col,
                pl.BlockSpec((KVH, GROUPS, BLOCK), lambda i, c, s: (0, 0, i)),
            ] + [any_spec] * 4,
            scratch_shapes=[
                pltpu.VMEM((KVH, rows, HD), bf16),
                pltpu.VMEM((blocks, KVH, HD + 16, BLOCK), bf16),
                pltpu.VMEM((blocks, HQ * HD, BLOCK), bf16),
                pltpu.VMEM((blocks, width, BLOCK), bf16),
                pltpu.VMEM((blocks, width, BLOCK), bf16),
                pltpu.VMEM((rows, cols), bf16),
                pltpu.VMEM((rows, 2 * cols), bf16),
                pltpu.VMEM((2 * cols, wide), bf16),
                pltpu.VMEM((cols, wide), bf16),
                pltpu.VMEM((rows, wide), bf16),
                pltpu.VMEM((width, 128), f32),
                pltpu.VMEM((HQ, 8, BLOCK), f32),
                pltpu.VMEM((HQ, rows, BLOCK), bf16),
                pltpu.VMEM(wg.shape, bf16),
                pltpu.VMEM(wu.shape, bf16),
                pltpu.VMEM(wdt.shape, bf16),
                pltpu.VMEM((4, rows_b, 128), bf16),
                pltpu.SemaphoreType.DMA((3,)),
                pltpu.SemaphoreType.DMA,
                pltpu.SemaphoreType.DMA((4,)),
            ],
        ),
        out_shape=out_shape,
        compiler_params=pltpu.CompilerParams(vmem_limit_bytes=VMEM),
        name="layer_forward",
        cost_estimate=cost(50),
    )(
        place, skip, tokens, other, cot, cot_other, gain_one, wqkv_t, w_out_t, gain_two, cos_t, sin_t, starts,
        w_out, wg, wu, wdt,
    )


def back_kernel(
    g, place_ref, soft_ref, qt_ref, kt_ref, vn_ref, dot_ref, delta_ref, cos_ref, sin_ref, n1_ref,
    dqkv_ref, keep_hbm, send_hbm,
    acc, ds_sc, pack_sc, pack_sem,
):
    step = pl.program_id(0)
    blocks = pl.num_programs(0)
    cosine, sine = cos_ref[...], sin_ref[...]

    @pl.when(step == 0)
    def _():
        acc[...] = jnp.zeros_like(acc)

    def attend(count):
        used = slice(0, count * BLOCK)
        here = slice((count - 1) * BLOCK, count * BLOCK)
        ups = [dot_ref[r * HD : (r + 1) * HD] for r in range(GROUPS)]
        soft_grads = [[dot(vn_ref[0, kb * BLOCK : (kb + 1) * BLOCK], up) for kb in range(count)] for up in ups]
        for r in range(GROUPS):
            rows = slice(r * HD, (r + 1) * HD)
            delta = delta_ref[0, r : r + 1]
            pair = jnp.concatenate([qt_ref[rows], ups[r]], 0).T
            left = lax.broadcasted_iota(jnp.int32, pair.shape, 1) < HD
            zero = jnp.zeros_like(pair)
            pads = jnp.concatenate([jnp.where(left, pair, zero), jnp.where(left, zero, pair)], 0)
            for kb in range(count):
                span = slice(kb * BLOCK, (kb + 1) * BLOCK)
                p = soft_ref[0, r, span]
                ds_sc[r, span, :BLOCK] = (p.astype(f32) * (soft_grads[r][kb] - delta)).astype(bf16)
                ds_sc[r, span, BLOCK:] = p
            acc[used] += dot(ds_sc[r, used], pads)
            dq = dot(kt_ref[:, used], ds_sc[r, used, :BLOCK])
            dqkv_ref[rows, here] = turn(dq * (HD**-0.5), cosine, sine, -1).astype(bf16)
        done = acc[here].T
        base = GROUPS * HD
        dqkv_ref[base : base + HD, here] = turn(done[:HD], cosine, sine, -1).astype(bf16)
        dqkv_ref[base + HD : base + 2 * HD, here] = done[HD:].astype(bf16)

    for count in range(1, 5):
        pl.when(step == 4 - count)(lambda count=count: attend(count))

    @pl.when(step == blocks - 1)
    def _():
        width = pack_sc.shape[1] * 128 * 2 // PER
        dw = dot(dqkv_ref[...], n1_ref[...])[:, :width].astype(bf16)
        span = pl.ds(g * pack_sc.shape[1], pack_sc.shape[1])
        copies = []
        for h in range(2):
            pack_thin(pack_sc.at[h], 0, h, dw)
            copies.append([pltpu.make_async_copy(pack_sc.at[h], t.at[span], pack_sem.at[h]) for t in (keep_hbm, send_hbm)])
            pl.when(place_ref[0] == h)(copies[h][0].start)
            pl.when(place_ref[0] != h)(copies[h][1].start)
        for keep, _ in copies:
            keep.wait()


def back(g, half_rows, width, place, soft, qt, kt, vn, dot_t, delta, cos_t, sin_t, n1, packed, after=()):
    blocks, _, rows, _ = soft.shape
    last = blocks - 1
    small = pl.BlockSpec((HD // 2, BLOCK), lambda i, c: (0, last - i))
    inputs = 10
    return pl.pallas_call(
        without(functools.partial(back_kernel, g), inputs, tuple(packed) + tuple(after)),
        grid_spec=pltpu.PrefetchScalarGridSpec(
            num_scalar_prefetch=1,
            grid=(blocks,),
            in_specs=[
                pl.BlockSpec((1, GROUPS, rows, BLOCK), lambda i, c: (last - i, g, 0, 0)),
                pl.BlockSpec((GROUPS * HD, BLOCK), lambda i, c: (g, last - i)),
                pl.BlockSpec((HD, rows), lambda i, c: (g, 0)),
                pl.BlockSpec((1, rows, HD), lambda i, c: (g, 0, 0)),
                pl.BlockSpec((GROUPS * HD, BLOCK), lambda i, c: (g, last - i)),
                pl.BlockSpec((1, GROUPS, BLOCK), lambda i, c: (g, 0, last - i)),
                small, small, full(n1.shape),
            ] + [ANY] * (len(packed) + len(after)),
            out_specs=[full((PER, rows)), ANY, ANY],
            scratch_shapes=[
                pltpu.VMEM((rows, 2 * HD), f32),
                pltpu.VMEM((GROUPS, rows, 2 * BLOCK), bf16),
                pltpu.VMEM((2, PER * width // 256, 128), bf16),
                pltpu.SemaphoreType.DMA((2,)),
            ],
        ),
        out_shape=[jax.ShapeDtypeStruct((PER, rows), bf16)] + [jax.ShapeDtypeStruct((half_rows, 128), bf16)] * 2,
        input_output_aliases={inputs + k: 1 + k for k in range(len(packed))},
        compiler_params=pltpu.CompilerParams(vmem_limit_bytes=VMEM),
        name="attention_backward",
        cost_estimate=cost(9),
    )(place, soft, qt, kt, vn, dot_t, delta, cos_t, sin_t, n1, *packed, *after)


def input_grad(place_ref, skip_ref, x_ref, cot_ref, gh_ref, parts, wqkv_ref, gain_one_ref):
    x = x_ref[...].reshape(gh_ref.shape).astype(f32)
    skipped = skip_ref[place_ref[0]] == 1
    inverse = lax.rsqrt(jnp.mean(x * x, 0, keepdims=True) + eps_norm)
    normed = x * inverse
    dqkv = jnp.concatenate([part[...] for part in parts], 0)
    c = dot(wqkv_ref[...], dqkv) * gain_one_ref[:, :1]
    gx = gh_ref[...] + inverse * (c - normed * jnp.mean(c * normed, 0, keepdims=True))
    return jnp.where(skipped, cot_ref[...].reshape(gh_ref.shape), gx.astype(bf16))


def away_kernel(
    place_ref, skip_ref, x_ref, cot_ref, gh_ref, d0_ref, d1_ref, d2_ref, wqkv_ref, gain_one_ref, grad_ref
):
    grad_ref[...] = input_grad(
        place_ref, skip_ref, x_ref, cot_ref, gh_ref, (d0_ref, d1_ref, d2_ref), wqkv_ref, gain_one_ref
    )


def own_kernel(
    place_ref, skip_ref, x_ref, cot_ref, gh_ref, d0_ref, d1_ref, d2_ref, wqkv_ref, gain_one_ref,
    grad_got, result_got, result_in, grad_hbm, result_hbm,
    block_sc, sem, got_sem,
):
    step = pl.program_id(0)
    steps = block_sc.shape[0]
    own, away = place_ref[0], 1 - place_ref[0]
    gots = [
        pltpu.make_async_copy(source, target.at[away], got_sem.at[k])
        for k, (source, target) in enumerate(((grad_got, grad_hbm), (result_got, result_hbm)))
    ]
    copies = [
        pltpu.make_async_copy(block_sc.at[k], grad_hbm.at[own, :, pl.ds(k * BLOCK, BLOCK)], sem.at[k]) for k in range(steps)
    ]

    @pl.when(step == 0)
    def _():
        for copy in gots:
            copy.start()

    gx = input_grad(place_ref, skip_ref, x_ref, cot_ref, gh_ref, (d0_ref, d1_ref, d2_ref), wqkv_ref, gain_one_ref)
    for k in range(steps):
        @pl.when(step == k)
        def _():
            block_sc[k] = gx
            copies[k].start()

    @pl.when(step == steps - 1)
    def _():
        for copy in copies + gots:
            copy.wait()


def last(mine, place, skip, x, cot, gh, parts, wqkv_n, gain_one, gots=(), after=()):
    width, rows = gh.shape
    near = rows // BLOCK // 2
    if mine:
        source = pl.BlockSpec((1, width, BLOCK), lambda i, c, s: (c[0], 0, i))
        at = lambda i, c, s: (0, near * c[0] + i)
        kernel, out_specs, aliases = own_kernel, [ANY, ANY], {12: 1}
        out_shape = [jax.ShapeDtypeStruct(x.shape, bf16)] * 2
        scratch = [pltpu.VMEM((near, width, BLOCK), bf16), pltpu.SemaphoreType.DMA((near,)), pltpu.SemaphoreType.DMA((2,))]
    else:
        source = pl.BlockSpec((width, BLOCK), lambda i, c, s: (0, i))
        at = lambda i, c, s: (0, near * (1 - c[0]) + i)
        kernel, out_specs, aliases = away_kernel, source, {}
        out_shape = jax.ShapeDtypeStruct(x.shape, bf16)
        scratch = []
    col = pl.BlockSpec((width, BLOCK), at)
    part = pl.BlockSpec((PER, BLOCK), at)
    return pl.pallas_call(
        without(kernel, 10 + len(gots), after),
        grid_spec=pltpu.PrefetchScalarGridSpec(
            num_scalar_prefetch=2,
            grid=(near,),
            in_specs=[source, source, col, part, part, part, full(wqkv_n.shape), full((width, 128))]
            + [full(got.shape) for got in gots[:2]] + [ANY] * (len(gots[2:]) + len(after)),
            out_specs=out_specs,
            scratch_shapes=scratch,
        ),
        out_shape=out_shape,
        input_output_aliases=aliases,
        compiler_params=pltpu.CompilerParams(vmem_limit_bytes=VMEM),
        name="input_backward",
        cost_estimate=cost(4),
    )(place, skip, x, cot, gh, *parts, wqkv_n, gain_one, *gots, *after)


def rotary_rows(rows):
    frequency = theta_base ** (-2.0 * np.arange(HD // 2, dtype=np.float64) / HD)
    angles = frequency[:, None] * np.arange(rows, dtype=np.float64)[None, :]
    return np.cos(angles).astype(np.float32), np.sin(angles).astype(np.float32)


def swap_core(array):
    return lax.ppermute(array, "narrow", [(0, 1), (1, 0)])


def axis_orders(bits, turn_index):
    if bits == 4:
        return (((0, 1, 2, 3), (1, 2, 3, 0)), ((1, 2, 0, 3), (2, 0, 1, 3)), ((0, 1, 2, 3), (1, 0, 2, 3)))[turn_index]
    base = tuple(range(bits))
    shift = bits // 2
    return base, base[shift:] + base[:shift]


class Summer:
    def __init__(self, core, chips, turn_index, exchanges):
        self.core = core
        self.chips = chips
        self.bits = chips.bit_length() - 1
        self.halvings = self.bits - exchanges
        self.orders = axis_orders(self.bits, turn_index)
        self.place = lax.axis_index("wide")
        self.stage = 0

    def bit(self, step):
        by_core = [(self.place >> order[step]) & 1 for order in self.orders]
        return jnp.where(self.core == 0, by_core[0], by_core[1])

    def swap(self, array, step):
        pairs = [
            (2 * chip + c, 2 * (chip ^ (1 << self.orders[c][step])) + c) for chip in range(self.chips) for c in range(2)
        ]
        return lax.ppermute(array, ("wide", "narrow"), pairs)

    def first(self, keep, send):
        self.keep, self.got = keep, swap_core(send)

    def advance(self, line):
        if line.last is not None:
            self.keep, self.got, _ = lax.optimization_barrier((self.keep, self.got, line.last))
        if self.stage < self.halvings:
            bit = self.bit(self.stage)
            half = self.keep.shape[0] // 2

            def part(which):
                a = lax.dynamic_slice_in_dim(self.keep, which * half, half, 0).astype(f32)
                b = lax.dynamic_slice_in_dim(self.got, which * half, half, 0).astype(f32)
                return (a + b).astype(bf16)

            line.last = part(1 - bit)
            self.keep, self.got = part(bit), self.swap(line.last, self.stage)
        elif self.stage <= self.bits:
            line.last = self.keep = (self.keep.astype(f32) + self.got.astype(f32)).astype(bf16)
            axis = self.stage if self.stage < self.bits else self.halvings - 1
            self.got = self.swap(self.keep, axis)
        else:
            step = self.halvings + self.bits - self.stage
            low = self.bit(step) == 0
            line.last = self.keep = jnp.where(
                low, jnp.concatenate([self.keep, self.got], 0), jnp.concatenate([self.got, self.keep], 0)
            )
            self.got = self.swap(self.keep, step - 1) if step else swap_core(self.keep)
        self.stage += 1

    @property
    def done(self):
        return self.stage > self.bits + self.halvings


class Line:
    last = None

    def after(self):
        return () if self.last is None else (self.last,)


def unpack_kernel(chain, place_ref, own_hbm, got_hbm, *refs):
    own, got, sem = refs[-3:]
    gate_ref, up_ref, down_ref = refs[-8:-5] if chain else refs[:3]
    step = pl.program_id(0)
    width = gate_ref.shape[0]
    copies = [
        pltpu.make_async_copy(source, target, sem.at[k]) for k, (source, target) in enumerate(((own_hbm, own), (got_hbm, got)))
    ]

    @pl.when(step == 0)
    def _():
        for copy in copies:
            copy.start()

    for k in range(2):
        pl.when((step == 0) & (place_ref[0] == k))(copies[k].wait)
        pl.when((step == 1) & (place_ref[0] != k))(copies[k].wait)

    def take(halves):
        for third in range(3):
            blocks = ((halves[0], 2), (halves[1], 2)) if third == 2 else ((halves[third], 0), (halves[third], 1))

            @pl.when(step == third)
            def _():
                for m, target in enumerate((gate_ref, up_ref, down_ref)):
                    for b, (source, place) in enumerate(blocks):
                        spot = (3 * m + place) * width
                        target[:, b * 128 : (b + 1) * 128] = source[spot : spot + width].astype(f32)

    pl.when(place_ref[0] == 0)(lambda: take((own, got)))
    pl.when(place_ref[0] != 0)(lambda: take((got, own)))

    if chain:
        w_out_ref, gain_ref = refs[-5:-3]

        def take_rest(first, second):
            spot = 9 * width
            unpack_thin(w_out_ref, first, second, spot)
            spot += width // 128 // 2 * width + width // 4
            rows = first[spot : spot + GAIN_ROWS].astype(f32)
            line = jnp.concatenate([rows[k : k + 1] for k in range(lanes_up(width) // 128)], 1)
            gain_ref[...] = line[:, :width].reshape(width)

        pl.when((step == 2) & (place_ref[0] == 0))(lambda: take_rest(own, got))
        pl.when((step == 2) & (place_ref[0] != 0))(lambda: take_rest(got, own))


def unpack(chain, place, buffers, width, inner, earlier):
    spec = pl.BlockSpec((width, BLOCK), lambda i, c: (0, 3 * chain + i))
    out_specs = [spec, spec, spec]
    out_shape = [jax.ShapeDtypeStruct((width, inner), f32)] * 3
    if chain:
        out_specs += [full((HQ * HD, width)), full((width,))]
        out_shape += [jax.ShapeDtypeStruct((HQ * HD, width), f32), jax.ShapeDtypeStruct((width,), f32)]
    return pl.pallas_call(
        functools.partial(unpack_kernel, chain),
        grid_spec=pltpu.PrefetchScalarGridSpec(
            num_scalar_prefetch=1,
            grid=(3,),
            in_specs=[ANY, pl.BlockSpec(memory_space=pltpu.HBM)] + [ANY] * len(earlier),
            out_specs=out_specs,
            scratch_shapes=[pltpu.VMEM(b.shape, bf16) for b in buffers] + [pltpu.SemaphoreType.DMA((2,))],
        ),
        out_shape=out_shape,
        input_output_aliases={3 + k: k for k in range(len(earlier))},
        compiler_params=pltpu.CompilerParams(vmem_limit_bytes=VMEM),
        name="unpack_mlp",
        cost_estimate=cost(4),
    )(place, *buffers, *earlier)


def unpack_last_kernel(place_ref, own_ref, got_ref, wqkv_ref, gain_one_ref, dq_ref, dkt_ref, dvt_ref, gain_ref, all_sc):
    q_cols = GROUPS * HD

    def take(first, second):
        for g in range(KVH):
            unpack_thin(all_sc.at[g * PER : (g + 1) * PER], first, second, g * PER * all_sc.shape[1] // 256)

    pl.when(place_ref[0] == 0)(lambda: take(own_ref, got_ref))
    pl.when(place_ref[0] != 0)(lambda: take(got_ref, own_ref))
    both = all_sc[...]
    dq = []
    for g in range(KVH):
        dq.append(both[g * PER : g * PER + q_cols])
        dkt_ref[g * HD : (g + 1) * HD] = both[g * PER + q_cols : g * PER + q_cols + HD]
        dvt_ref[g * HD : (g + 1) * HD] = both[g * PER + q_cols + HD : (g + 1) * PER]
    dq_ref[...] = jnp.concatenate(dq, 0).T
    gain = jnp.sum(both * wqkv_ref[...].astype(f32), 0, keepdims=True) / gain_one_ref[...]
    gain_ref[...] = gain.reshape(gain_ref.shape)


def unpack_last(place, own, got, wqkv_t, gain_one, after):
    width = wqkv_t.shape[1]
    shapes = [(width, HQ * HD), (KVH * HD, width), (KVH * HD, width), (width,)]
    return pl.pallas_call(
        without(unpack_last_kernel, 5, after),
        grid_spec=pltpu.PrefetchScalarGridSpec(
            num_scalar_prefetch=1,
            grid=(1,),
            in_specs=[full(own.shape)] * 2 + [full(wqkv_t.shape), full((1, width))] + [ANY] * len(after),
            out_specs=[full(shape) for shape in shapes],
            scratch_shapes=[pltpu.VMEM(wqkv_t.shape, f32)],
        ),
        out_shape=[jax.ShapeDtypeStruct(shape, f32) for shape in shapes],
        compiler_params=pltpu.CompilerParams(vmem_limit_bytes=VMEM),
        name="unpack_attention",
        cost_estimate=cost(3),
    )(place, own, got, wqkv_t, gain_one, *after)


def flip(array):
    return jnp.swapaxes(array, -1, -2)


def per_device(tokens, doc_starts, skip_flags, cotangent, attn_gain, wq, wk, wv, w_out, mlp_gain, wg, wu, wd):
    core = lax.axis_index("narrow")
    chips = lax.axis_size("wide")
    tokens, cotangent = flip(tokens), flip(cotangent)
    rows = 2 * tokens.shape[2]
    width = tokens.shape[1]
    inner = wg.shape[1]
    place = core.astype(jnp.int32).reshape(1)
    skip = skip_flags
    other = swap_core(lax.dynamic_index_in_dim(tokens, 1 - core, 0, keepdims=False))
    cot_other = swap_core(lax.dynamic_index_in_dim(cotangent, 1 - core, 0, keepdims=False))
    cos_t, sin_t = rotary_rows(rows)
    wdt = flip(wd)
    wqkv_t, wqkv_n, w_out_t, gain_one, gain_two, gain_line = prelude(wq, flip(wk), flip(wv), w_out, attn_gain, mlp_gain)
    unit = 16 * chips

    def half_rows(count):
        return -(-count // unit) * unit

    mlp_rows = 3 * width * inner // 4 // 128
    thin = width // 128 // 2
    out_rows = thin * HQ * HD + HQ * HD // 4 + GAIN_ROWS
    rest_rows = thin * KVH * PER + KVH * PER // 4

    (
        qt, kt, vn, soft, n1, res_own, res_away, gh, dot_t, delta, keep_a, send_a, keep_b, send_b,
    ) = layer(
        half_rows(mlp_rows), half_rows(mlp_rows + out_rows),
        place, skip, tokens, other, cotangent, cot_other, gain_one, wqkv_t, w_out_t, gain_two, cos_t, sin_t,
        doc_starts, w_out, wg, wu, wdt,
    )
    a_sum, b_sum, c_sum = (Summer(core, chips, k, exchanges) for k, exchanges in ((0, 0), (1, 0), (2, 2)))
    a_sum.first(keep_a, send_a)
    b_sum.first(keep_b, send_b)
    result_got = swap_core(res_away)
    line = Line()
    parts, packed = [], ()
    for g in range(KVH):
        part, *packed = back(
            g, half_rows(rest_rows), width, place, soft, qt, kt, vn, dot_t, delta, cos_t, sin_t, n1, packed, line.after()
        )
        parts.append(part)
        line.last = part
        if g == KVH - 1:
            c_sum.first(*packed)
        a_sum.advance(line)
        b_sum.advance(line)
    grad_away = last(False, place, skip, other, cot_other, gh, parts, wqkv_n, gain_one, (), line.after())
    line.last = grad_away
    for chain in (c_sum, a_sum, b_sum):
        chain.advance(line)
    grad_got = swap_core(grad_away)
    for chain in (c_sum, a_sum, b_sum):
        chain.advance(line)
    for chain in (c_sum, a_sum, b_sum, c_sum, a_sum, b_sum, c_sum, c_sum, a_sum, b_sum):
        chain.advance(line)
    c_sum.advance(line)
    grad_x, result = last(
        True, place, skip, tokens, cotangent, gh, parts, wqkv_n, gain_one, (grad_got, result_got, res_own), line.after()
    )
    line.last = grad_x
    a_sum.advance(line)
    for chain in (a_sum, c_sum):
        while not chain.done:
            chain.advance(line)
    dq, dkt, dvt, dgain_one = unpack_last(place, c_sum.keep, c_sum.got, wqkv_t, gain_line, line.after())
    line.last = dgain_one
    while not b_sum.done:
        b_sum.advance(line)
    first = unpack(0, place, (a_sum.keep, a_sum.got), width, inner, ())
    dwg, dwu, dwdt, dwo, dgain_two = unpack(1, place, (b_sum.keep, b_sum.got), width, inner, first)
    return (
        flip(result), flip(grad_x),
        dgain_one, dq, flip(dkt), flip(dvt), dwo, dgain_two, dwg, dwu, flip(dwdt),
    )


def solution(mesh):
    split = P("wide", "narrow", None)
    in_specs = (split, P("wide", None), P("wide"), split) + (P(),) * 9
    out_specs = (split, split) + (P(),) * 9
    return jax.shard_map(per_device, mesh=mesh, in_specs=in_specs, out_specs=out_specs, check_vma=False)
```

```python
import functools

import jax
import jax.numpy as jnp
import numpy as np
from jax import lax
from jax.experimental import pallas as pl
from jax.experimental.pallas import tpu as pltpu
from jax.sharding import PartitionSpec as P

HQ = 9
KVH = 3
HD = 64
GROUPS = HQ // KVH
PER = (GROUPS + 2) * HD
theta_base = 100000.0
eps_norm = 1e-05
masked_score = -1e30
BLOCK = 256
GAIN_ROWS = 16
VMEM = 60 * 2**20
f32 = jnp.float32
bf16 = jnp.bfloat16


def cost(microseconds):
    return pl.CostEstimate(flops=int(microseconds * 1.0e9), bytes_accessed=1024, transcendentals=0)


def dot(a, b, ca=1, cb=0):
    return lax.dot_general(a, b, (((ca,), (cb,)), ((), ())), preferred_element_type=f32)


def turn(rows, cosine, sine, sign):
    half = HD // 2
    first, second = rows[:half], rows[half:]
    if sign > 0:
        return jnp.concatenate([first * cosine - second * sine, second * cosine + first * sine], 0)
    return jnp.concatenate([first * cosine + second * sine, second * cosine - first * sine], 0)


def lanes_up(count):
    return -(-count // 128) * 128


ANY = pl.BlockSpec(memory_space=pl.ANY)


def without(kernel, inputs, after):
    return lambda *refs: kernel(*refs[:inputs], *refs[inputs + len(after) :])


def full(shape):
    return pl.BlockSpec(shape, lambda *_: (0,) * len(shape))


def widen(matrix):
    extra = lanes_up(matrix.shape[1]) - matrix.shape[1]
    return jnp.concatenate([matrix, jnp.zeros((matrix.shape[0], extra), matrix.dtype)], 1)


def pack_blocks(target, spot, matrix):
    for k in range(matrix.shape[1] // 128):
        target[spot : spot + matrix.shape[0]] = matrix[:, k * 128 : (k + 1) * 128]
        spot += matrix.shape[0]
    return spot


def pack_thin(target, spot, h, matrix):
    rows = matrix.shape[0]
    quarter = rows // 4
    base = matrix.shape[1] // 128
    for k in range(h * base // 2, (h + 1) * base // 2):
        target[spot : spot + rows] = matrix[:, k * 128 : (k + 1) * 128]
        spot += rows
    left = matrix[2 * h * quarter : (2 * h + 1) * quarter, base * 128 :]
    right = matrix[(2 * h + 1) * quarter : (2 * h + 2) * quarter, base * 128 :]
    target[spot : spot + quarter] = jnp.concatenate([left, right], 1)
    return spot + quarter


def unpack_thin(target, first, second, spot):
    rows, width = target.shape
    quarter = rows // 4
    base = width // 128
    for h, source in enumerate((first, second)):
        at = spot
        for k in range(h * base // 2, (h + 1) * base // 2):
            target[:, k * 128 : (k + 1) * 128] = source[at : at + rows].astype(f32)
            at += rows
        last = source[at : at + quarter].astype(f32)
        target[2 * h * quarter : (2 * h + 1) * quarter, base * 128 :] = last[:, : width - base * 128]
        target[(2 * h + 1) * quarter : (2 * h + 2) * quarter, base * 128 :] = last[:, width - base * 128 :]


def prelude_kernel(wq_ref, wkt_ref, wvt_ref, w_out_ref, gain_one_ref, gain_two_ref, t_ref, n_ref, out_t_ref, g1_ref, g2_ref, line_ref):
    q_cols = GROUPS * HD
    wqt = wq_ref[...].T
    for g in range(KVH):
        t_ref[g * PER : g * PER + q_cols] = wqt[g * q_cols : (g + 1) * q_cols]
        t_ref[g * PER + q_cols : g * PER + q_cols + HD] = wkt_ref[g * HD : (g + 1) * HD]
        t_ref[g * PER + q_cols + HD : (g + 1) * PER] = wvt_ref[g * HD : (g + 1) * HD]
    n_ref[...] = t_ref[...].T
    out_t_ref[...] = w_out_ref[...].T
    for source, target in ((gain_one_ref, g1_ref), (gain_two_ref, g2_ref)):
        gain = source[...].astype(f32).reshape(1, source.shape[0])
        target[...] = jnp.broadcast_to(gain, (128, source.shape[0])).T
    line_ref[...] = gain_one_ref[...].astype(f32).reshape(line_ref.shape)


def prelude(wq, wkt, wvt, w_out, gain_one, gain_two):
    width = wq.shape[0]
    return pl.pallas_call(
        prelude_kernel,
        out_shape=[
            jax.ShapeDtypeStruct((KVH * PER, width), bf16),
            jax.ShapeDtypeStruct((width, KVH * PER), bf16),
            jax.ShapeDtypeStruct((width, w_out.shape[0]), bf16),
            jax.ShapeDtypeStruct((width, 128), f32),
            jax.ShapeDtypeStruct((width, 128), f32),
            jax.ShapeDtypeStruct((1, width), f32),
        ],
        compiler_params=pltpu.CompilerParams(vmem_limit_bytes=VMEM),
        name="prelude",
        cost_estimate=cost(4),
    )(wq, wkt, wvt, w_out, gain_one, gain_two)


def layer_kernel(
    place_ref, skip_ref, own_ref, other_ref, cot_own_ref, cot_other_ref,
    gain_one_ref, wqkv_ref, w_out_t_ref, gain_two_ref, cos_ref, sin_ref, start_ref,
    w_out_ref, w_gate_hbm, w_up_hbm, w_down_hbm,
    qt_ref, kt_ref, vn_ref, soft_hbm, n1_ref,
    res_own_ref, res_away_ref, gh_ref, dot_ref, delta_ref, keep_a_hbm, send_a_hbm, keep_b_hbm, send_b_hbm,
    kn_all, vt_all, mixed_sc, n2t_sc, gt_sc, inner_sc, grads_sc, in_t_sc, down_sc, ga_sc, dgain_sc,
    scale_sc, soft_sc, w_gate_ref, w_up_ref, w_down_ref, pack_sc, weight_sem, soft_sem, pack_sem,
):
    step = pl.program_id(0)
    mine = (step >= 2).astype(jnp.int32) == place_ref[0]
    width = other_ref.shape[0]
    cols = w_gate_hbm.shape[1]

    weight_copies = [
        pltpu.make_async_copy(source, target, weight_sem.at[k])
        for k, (source, target) in enumerate(
            ((w_gate_hbm, w_gate_ref), (w_up_hbm, w_up_ref), (w_down_hbm, w_down_ref))
        )
    ]

    @pl.when(step == 0)
    def _():
        for copy in weight_copies:
            copy.start()
        dgain_sc[...] = jnp.zeros_like(dgain_sc)

    low = jnp.where(mine, own_ref[0], other_ref[...])
    x = low.astype(f32)
    cot = jnp.where(mine, cot_own_ref[0], cot_other_ref[...])
    g = jnp.where(skip_ref[place_ref[0]] == 1, jnp.zeros_like(cot), cot)
    gt_sc[step] = g
    inverse = lax.rsqrt(jnp.mean(x * x, 0, keepdims=True) + eps_norm)
    n1 = (x * inverse * gain_one_ref[:, :1]).astype(bf16)
    n1_ref[...] = widen(n1.T)
    qkv = dot(wqkv_ref[...], n1)
    cosine, sine = cos_ref[...], sin_ref[...]
    here = pl.ds(pl.multiple_of(step * BLOCK, BLOCK), BLOCK)
    for group in range(KVH):
        for r in range(GROUPS):
            head = group * GROUPS + r
            base = group * PER + r * HD
            rows = (turn(qkv[base : base + HD], cosine, sine, 1) * (HD**-0.5)).astype(bf16)
            qt_ref[head * HD : (head + 1) * HD] = rows
        base = group * PER + GROUPS * HD
        rows = turn(qkv[base : base + HD], cosine, sine, 1).astype(bf16)
        kt_ref[group * HD : (group + 1) * HD] = rows
        kn_all[group, here] = rows.T
        rows = qkv[base + HD : base + 2 * HD].astype(bf16)
        vt_all[step, group] = jnp.concatenate([rows, jnp.ones((16, BLOCK), bf16)], 0)
        vn_ref[group] = rows.T

    pos = step * BLOCK + lax.broadcasted_iota(jnp.int32, (1, BLOCK), 1)
    start_row = jnp.zeros((1, BLOCK), jnp.int32)
    for k in range(start_ref.shape[1]):
        first = start_ref[place_ref[0], k]
        start_row = jnp.where(pos >= first, first, start_row)

    def soft_copy(count):
        used = pl.ds(0, count * BLOCK)
        return pltpu.make_async_copy(soft_sc.at[:, used], soft_hbm.at[count - 1, :, used], soft_sem)

    def attend(count):
        t = lax.broadcasted_iota(jnp.int32, (BLOCK, BLOCK), 0)
        s_pos = lax.broadcasted_iota(jnp.int32, (BLOCK, BLOCK), 1)
        if count > 1:
            soft_copy(count - 1).wait()

        def one_group(group, carry):
            def scores_of(r):
                rows = pl.ds(pl.multiple_of((group * GROUPS + r) * HD, HD), HD)
                q = qt_ref[rows]
                scores = []
                for kb in range(count):
                    s = dot(kn_all[group, kb * BLOCK : (kb + 1) * BLOCK], q)
                    ok = t + kb * BLOCK >= start_row
                    if kb == count - 1:
                        ok = ok & (t <= s_pos)
                    scores.append(jnp.where(ok, s, masked_score))
                return scores

            def finish(r, scores):
                head = group * GROUPS + r
                rows = pl.ds(pl.multiple_of(head * HD, HD), HD)
                peak = scores[0].max(0, keepdims=True)
                for s in scores[1:]:
                    peak = jnp.maximum(peak, s.max(0, keepdims=True))
                out = None
                for kb in range(count):
                    p = jnp.exp(scores[kb] - peak).astype(bf16)
                    soft_sc[head, kb * BLOCK : (kb + 1) * BLOCK] = p
                    term = dot(vt_all[kb, group], p)
                    out = term if out is None else out + term
                scale = 1.0 / out[HD : HD + 1]
                scale_sc[head] = jnp.broadcast_to(scale, scale_sc.shape[1:])
                mixed_sc[step, rows] = (out[:HD] * scale).astype(bf16)

            every = [scores_of(r) for r in range(GROUPS)]
            for r in range(GROUPS):
                finish(r, every[r])
            return carry

        lax.fori_loop(0, KVH, one_group, 0)
        soft_copy(count).start()

    for count in range(1, 5):
        pl.when(step == count - 1)(lambda count=count: attend(count))

    @pl.when(step == 0)
    def _():
        for copy in weight_copies:
            copy.wait()
        for k, ref in enumerate((w_gate_ref, w_up_ref)):
            in_t_sc[k * cols : (k + 1) * cols] = widen(ref[...].T)
        down_sc[...] = widen(w_down_ref[...].T)

    mixed = mixed_sc[step]
    hidden = x + dot(w_out_t_ref[...], mixed)
    inverse = lax.rsqrt(jnp.mean(hidden * hidden, 0, keepdims=True) + eps_norm)
    normed = hidden * inverse
    n2t = (normed * gain_two_ref[:, :1]).astype(bf16)
    n2t_sc[step] = n2t
    n2 = n2t.T
    gn = g.T

    def chunk(k, carry):
        work = []
        for c in range(3):
            at = pl.ds(pl.multiple_of((3 * k + c) * BLOCK, BLOCK), BLOCK)
            at_up = pl.ds(pl.multiple_of(cols + (3 * k + c) * BLOCK, BLOCK), BLOCK)
            work.append((at, at_up, dot(n2, w_gate_ref[:, at]), dot(n2, w_up_ref[:, at]), dot(gn, w_down_ref[:, at])))
        for at, at_up, gate, up, grad_inner in work:
            sig = jax.nn.sigmoid(gate)
            act = gate * sig
            inner_sc[here, at] = (act * up).astype(bf16)
            grads_sc[here, at] = (grad_inner * up * (sig + act * (1.0 - sig))).astype(bf16)
            grads_sc[here, at_up] = (grad_inner * act).astype(bf16)
        return carry

    lax.fori_loop(0, cols // BLOCK // 3, chunk, 0)
    result = hidden + dot(inner_sc[here], down_sc[...]).T[:width]
    result = jnp.where(skip_ref[place_ref[0]] == 1, low, result.astype(bf16))

    @pl.when(mine)
    def _():
        res_own_ref[0] = result

    @pl.when(jnp.logical_not(mine))
    def _():
        res_away_ref[...] = result

    gn2 = dot(grads_sc[here], in_t_sc[...]).T[:width]
    c = gn2 * gain_two_ref[:, :1]
    dgain_sc[:, :1] += jnp.sum(gn2 * normed, 1, keepdims=True)
    gh = g.astype(f32) + inverse * (c - normed * jnp.mean(c * normed, 0, keepdims=True))
    gh_ref[...] = gh
    ga = gh.astype(bf16)
    ga_sc[here] = widen(ga.T)
    back_t = dot(w_out_ref[...], ga)
    for head in range(HQ):
        rows = (back_t[head * HD : (head + 1) * HD] * scale_sc[head, 0:1]).astype(bf16)
        dot_ref[head * HD : (head + 1) * HD] = rows
        delta_ref[head // GROUPS, head % GROUPS : head % GROUPS + 1] = jnp.sum(
            rows.astype(f32) * mixed[head * HD : (head + 1) * HD].astype(f32), 0, keepdims=True
        )

    @pl.when(step == pl.num_programs(0) - 1)
    def _():
        blocks = mixed_sc.shape[0]
        whole = lambda ref: jnp.concatenate([ref[k] for k in range(blocks)], 1)
        n2t_all, gt_all = whole(n2t_sc), whole(gt_sc)
        dw_out = dot(whole(mixed_sc), ga_sc[...])[:, :width].astype(bf16)
        line = dgain_sc[...].T[0:1]
        line = jnp.concatenate([line, jnp.zeros((1, lanes_up(width) - width), f32)], 1)
        lines = [line[:, k * 128 : (k + 1) * 128] for k in range(line.shape[1] // 128)]
        lines.append(jnp.zeros((GAIN_ROWS - len(lines), 128), f32))
        gain_rows = jnp.concatenate(lines, 0).astype(bf16)
        thin = 9 * width
        for h in range(2):
            target = pack_sc.at[2 + h]
            spot = pack_thin(target, thin, h, dw_out)
            target[spot : spot + GAIN_ROWS] = gain_rows

        def one_chunk(k, carry):
            at = pl.ds(pl.multiple_of(k * BLOCK, BLOCK), BLOCK)
            at_up = pl.ds(pl.multiple_of(cols + k * BLOCK, BLOCK), BLOCK)
            chain = jnp.where(k >= 3, 1, 0)
            third = k - 3 * chain
            for m, (left, right) in enumerate(
                ((n2t_all, grads_sc[:, at]), (n2t_all, grads_sc[:, at_up]), (gt_all, inner_sc[:, at]))
            ):
                both = dot(left, right).astype(bf16)
                for b in range(2):
                    half = jnp.where(third == 2, b, third)
                    spot = (3 * m + jnp.where(third == 2, 2, b)) * width
                    pack_sc[2 * chain + half, pl.ds(pl.multiple_of(spot, 16), width)] = both[:, b * 128 : (b + 1) * 128]
            for q in range(4):
                keep, send = pack_copies[q]
                pl.when((k == 3 * (q // 2) + 2) & (place_ref[0] == q % 2))(keep.start)
                pl.when((k == 3 * (q // 2) + 2) & (place_ref[0] != q % 2))(send.start)
            return carry

        pack_copies = []
        for q in range(4):
            targets = (keep_a_hbm, send_a_hbm) if q < 2 else (keep_b_hbm, send_b_hbm)
            source = pack_sc.at[q, pl.ds(0, targets[0].shape[0])]
            pack_copies.append([pltpu.make_async_copy(source, target, pack_sem.at[q]) for target in targets])
        lax.fori_loop(0, 6, one_chunk, 0)
        for keep, _ in pack_copies:
            keep.wait()
        soft_copy(blocks).wait()


def own_specs(width, near):
    own = pl.BlockSpec((1, width, BLOCK), lambda i, c, s: (c[0], 0, jnp.where(i >= near, i - near, i)))
    oth = pl.BlockSpec((width, BLOCK), lambda i, c, s: (0, jnp.where(i >= near, i - near, i)))
    return own, oth


def out_specs_halves(width, near):
    mine = pl.BlockSpec((1, width, BLOCK), lambda i, c, s: (c[0], 0, jnp.clip(i - near * c[0], 0, near - 1)))
    away = pl.BlockSpec((width, BLOCK), lambda i, c, s: (0, jnp.clip(i - near * (1 - c[0]), 0, near - 1)))
    return mine, away


def layer(
    rows_a, rows_b, place, skip, tokens, other, cot, cot_other, gain_one, wqkv_t, w_out_t, gain_two, cos_t, sin_t,
    starts, w_out, wg, wu, wdt,
):
    rows = 2 * tokens.shape[2]
    width = tokens.shape[1]
    cols = wg.shape[1]
    wide = lanes_up(width)
    blocks = rows // BLOCK
    own, oth = own_specs(width, blocks // 2)
    col = pl.BlockSpec((width, BLOCK), lambda i, c, s: (0, i))
    row_wide = pl.BlockSpec((BLOCK, wide), lambda i, c, s: (i, 0))
    small = pl.BlockSpec((HD // 2, BLOCK), lambda i, c, s: (0, i))
    const = lambda array: pl.BlockSpec(
        array.shape, lambda *_: (0,) * array.ndim, pipeline_mode=pl.Buffered(1)
    )
    any_spec = pl.BlockSpec(memory_space=pl.ANY)
    halves = [(rows_a, 128), (rows_a, 128), (rows_b, 128), (rows_b, 128)]
    out_shape = [
        jax.ShapeDtypeStruct((HQ * HD, rows), bf16),
        jax.ShapeDtypeStruct((KVH * HD, rows), bf16),
        jax.ShapeDtypeStruct((KVH, rows, HD), bf16),
        jax.ShapeDtypeStruct((blocks, HQ, rows, BLOCK), bf16),
        jax.ShapeDtypeStruct((rows, wide), bf16),
        jax.ShapeDtypeStruct((2, width, rows // 2), bf16),
        jax.ShapeDtypeStruct((width, rows // 2), bf16),
        jax.ShapeDtypeStruct((width, rows), f32),
        jax.ShapeDtypeStruct((HQ * HD, rows), bf16),
        jax.ShapeDtypeStruct((KVH, GROUPS, rows), f32),
    ] + [jax.ShapeDtypeStruct(shape, bf16) for shape in halves]
    return pl.pallas_call(
        layer_kernel,
        grid_spec=pltpu.PrefetchScalarGridSpec(
            num_scalar_prefetch=2,
            grid=(blocks,),
            in_specs=[
                own, oth, own, oth, const(gain_one), const(wqkv_t), const(w_out_t), const(gain_two),
                small, small, pl.BlockSpec(memory_space=pltpu.SMEM),
                const(w_out), any_spec, any_spec, any_spec,
            ],
            out_specs=[
                col,
                pl.BlockSpec((KVH * HD, BLOCK), lambda i, c, s: (0, i)),
                pl.BlockSpec((KVH, BLOCK, HD), lambda i, c, s: (0, i, 0)),
                any_spec,
                row_wide,
                *out_specs_halves(width, blocks // 2),
                col, col,
                pl.BlockSpec((KVH, GROUPS, BLOCK), lambda i, c, s: (0, 0, i)),
            ] + [any_spec] * 4,
            scratch_shapes=[
                pltpu.VMEM((KVH, rows, HD), bf16),
                pltpu.VMEM((blocks, KVH, HD + 16, BLOCK), bf16),
                pltpu.VMEM((blocks, HQ * HD, BLOCK), bf16),
                pltpu.VMEM((blocks, width, BLOCK), bf16),
                pltpu.VMEM((blocks, width, BLOCK), bf16),
                pltpu.VMEM((rows, cols), bf16),
                pltpu.VMEM((rows, 2 * cols), bf16),
                pltpu.VMEM((2 * cols, wide), bf16),
                pltpu.VMEM((cols, wide), bf16),
                pltpu.VMEM((rows, wide), bf16),
                pltpu.VMEM((width, 128), f32),
                pltpu.VMEM((HQ, 8, BLOCK), f32),
                pltpu.VMEM((HQ, rows, BLOCK), bf16),
                pltpu.VMEM(wg.shape, bf16),
                pltpu.VMEM(wu.shape, bf16),
                pltpu.VMEM(wdt.shape, bf16),
                pltpu.VMEM((4, rows_b, 128), bf16),
                pltpu.SemaphoreType.DMA((3,)),
                pltpu.SemaphoreType.DMA,
                pltpu.SemaphoreType.DMA((4,)),
            ],
        ),
        out_shape=out_shape,
        compiler_params=pltpu.CompilerParams(vmem_limit_bytes=VMEM),
        name="layer_forward",
        cost_estimate=cost(50),
    )(
        place, skip, tokens, other, cot, cot_other, gain_one, wqkv_t, w_out_t, gain_two, cos_t, sin_t, starts,
        w_out, wg, wu, wdt,
    )


def back_kernel(
    g, place_ref, soft_ref, qt_ref, kt_ref, vn_ref, dot_ref, delta_ref, cos_ref, sin_ref, n1_ref,
    dqkv_ref, keep_hbm, send_hbm,
    acc, ds_sc, pack_sc, pack_sem,
):
    step = pl.program_id(0)
    blocks = pl.num_programs(0)
    cosine, sine = cos_ref[...], sin_ref[...]

    @pl.when(step == 0)
    def _():
        acc[...] = jnp.zeros_like(acc)

    def attend(count):
        used = slice(0, count * BLOCK)
        here = slice((count - 1) * BLOCK, count * BLOCK)
        ups = [dot_ref[r * HD : (r + 1) * HD] for r in range(GROUPS)]
        soft_grads = [[dot(vn_ref[0, kb * BLOCK : (kb + 1) * BLOCK], up) for kb in range(count)] for up in ups]
        for r in range(GROUPS):
            rows = slice(r * HD, (r + 1) * HD)
            delta = delta_ref[0, r : r + 1]
            pair = jnp.concatenate([qt_ref[rows], ups[r]], 0).T
            left = lax.broadcasted_iota(jnp.int32, pair.shape, 1) < HD
            zero = jnp.zeros_like(pair)
            pads = jnp.concatenate([jnp.where(left, pair, zero), jnp.where(left, zero, pair)], 0)
            for kb in range(count):
                span = slice(kb * BLOCK, (kb + 1) * BLOCK)
                p = soft_ref[0, r, span]
                ds_sc[r, span, :BLOCK] = (p.astype(f32) * (soft_grads[r][kb] - delta)).astype(bf16)
                ds_sc[r, span, BLOCK:] = p
            acc[used] += dot(ds_sc[r, used], pads)
            dq = dot(kt_ref[:, used], ds_sc[r, used, :BLOCK])
            dqkv_ref[rows, here] = turn(dq * (HD**-0.5), cosine, sine, -1).astype(bf16)
        done = acc[here].T
        base = GROUPS * HD
        dqkv_ref[base : base + HD, here] = turn(done[:HD], cosine, sine, -1).astype(bf16)
        dqkv_ref[base + HD : base + 2 * HD, here] = done[HD:].astype(bf16)

    for count in range(1, 5):
        pl.when(step == 4 - count)(lambda count=count: attend(count))

    @pl.when(step == blocks - 1)
    def _():
        width = pack_sc.shape[1] * 128 * 2 // PER
        dw = dot(dqkv_ref[...], n1_ref[...])[:, :width].astype(bf16)
        span = pl.ds(g * pack_sc.shape[1], pack_sc.shape[1])
        copies = []
        for h in range(2):
            pack_thin(pack_sc.at[h], 0, h, dw)
            copies.append([pltpu.make_async_copy(pack_sc.at[h], t.at[span], pack_sem.at[h]) for t in (keep_hbm, send_hbm)])
            pl.when(place_ref[0] == h)(copies[h][0].start)
            pl.when(place_ref[0] != h)(copies[h][1].start)
        for keep, _ in copies:
            keep.wait()


def back(g, half_rows, width, place, soft, qt, kt, vn, dot_t, delta, cos_t, sin_t, n1, packed, after=()):
    blocks, _, rows, _ = soft.shape
    last = blocks - 1
    small = pl.BlockSpec((HD // 2, BLOCK), lambda i, c: (0, last - i))
    inputs = 10
    return pl.pallas_call(
        without(functools.partial(back_kernel, g), inputs, tuple(packed) + tuple(after)),
        grid_spec=pltpu.PrefetchScalarGridSpec(
            num_scalar_prefetch=1,
            grid=(blocks,),
            in_specs=[
                pl.BlockSpec((1, GROUPS, rows, BLOCK), lambda i, c: (last - i, g, 0, 0)),
                pl.BlockSpec((GROUPS * HD, BLOCK), lambda i, c: (g, last - i)),
                pl.BlockSpec((HD, rows), lambda i, c: (g, 0)),
                pl.BlockSpec((1, rows, HD), lambda i, c: (g, 0, 0)),
                pl.BlockSpec((GROUPS * HD, BLOCK), lambda i, c: (g, last - i)),
                pl.BlockSpec((1, GROUPS, BLOCK), lambda i, c: (g, 0, last - i)),
                small, small, full(n1.shape),
            ] + [ANY] * (len(packed) + len(after)),
            out_specs=[full((PER, rows)), ANY, ANY],
            scratch_shapes=[
                pltpu.VMEM((rows, 2 * HD), f32),
                pltpu.VMEM((GROUPS, rows, 2 * BLOCK), bf16),
                pltpu.VMEM((2, PER * width // 256, 128), bf16),
                pltpu.SemaphoreType.DMA((2,)),
            ],
        ),
        out_shape=[jax.ShapeDtypeStruct((PER, rows), bf16)] + [jax.ShapeDtypeStruct((half_rows, 128), bf16)] * 2,
        input_output_aliases={inputs + k: 1 + k for k in range(len(packed))},
        compiler_params=pltpu.CompilerParams(vmem_limit_bytes=VMEM),
        name="attention_backward",
        cost_estimate=cost(9),
    )(place, soft, qt, kt, vn, dot_t, delta, cos_t, sin_t, n1, *packed, *after)


def input_grad(place_ref, skip_ref, x_ref, cot_ref, gh_ref, parts, wqkv_ref, gain_one_ref):
    x = x_ref[...].reshape(gh_ref.shape).astype(f32)
    skipped = skip_ref[place_ref[0]] == 1
    inverse = lax.rsqrt(jnp.mean(x * x, 0, keepdims=True) + eps_norm)
    normed = x * inverse
    dqkv = jnp.concatenate([part[...] for part in parts], 0)
    c = dot(wqkv_ref[...], dqkv) * gain_one_ref[:, :1]
    gx = gh_ref[...] + inverse * (c - normed * jnp.mean(c * normed, 0, keepdims=True))
    return jnp.where(skipped, cot_ref[...].reshape(gh_ref.shape), gx.astype(bf16))


def away_kernel(
    place_ref, skip_ref, x_ref, cot_ref, gh_ref, d0_ref, d1_ref, d2_ref, wqkv_ref, gain_one_ref, grad_ref
):
    grad_ref[...] = input_grad(
        place_ref, skip_ref, x_ref, cot_ref, gh_ref, (d0_ref, d1_ref, d2_ref), wqkv_ref, gain_one_ref
    )


def own_kernel(
    place_ref, skip_ref, x_ref, cot_ref, gh_ref, d0_ref, d1_ref, d2_ref, wqkv_ref, gain_one_ref,
    grad_got, result_got, result_in, grad_hbm, result_hbm,
    block_sc, sem, got_sem,
):
    step = pl.program_id(0)
    steps = block_sc.shape[0]
    own, away = place_ref[0], 1 - place_ref[0]
    gots = [
        pltpu.make_async_copy(source, target.at[away], got_sem.at[k])
        for k, (source, target) in enumerate(((grad_got, grad_hbm), (result_got, result_hbm)))
    ]
    copies = [
        pltpu.make_async_copy(block_sc.at[k], grad_hbm.at[own, :, pl.ds(k * BLOCK, BLOCK)], sem.at[k]) for k in range(steps)
    ]

    @pl.when(step == 0)
    def _():
        for copy in gots:
            copy.start()

    gx = input_grad(place_ref, skip_ref, x_ref, cot_ref, gh_ref, (d0_ref, d1_ref, d2_ref), wqkv_ref, gain_one_ref)
    for k in range(steps):
        @pl.when(step == k)
        def _():
            block_sc[k] = gx
            copies[k].start()

    @pl.when(step == steps - 1)
    def _():
        for copy in copies + gots:
            copy.wait()


def last(mine, place, skip, x, cot, gh, parts, wqkv_n, gain_one, gots=(), after=()):
    width, rows = gh.shape
    near = rows // BLOCK // 2
    if mine:
        source = pl.BlockSpec((1, width, BLOCK), lambda i, c, s: (c[0], 0, i))
        at = lambda i, c, s: (0, near * c[0] + i)
        kernel, out_specs, aliases = own_kernel, [ANY, ANY], {12: 1}
        out_shape = [jax.ShapeDtypeStruct(x.shape, bf16)] * 2
        scratch = [pltpu.VMEM((near, width, BLOCK), bf16), pltpu.SemaphoreType.DMA((near,)), pltpu.SemaphoreType.DMA((2,))]
    else:
        source = pl.BlockSpec((width, BLOCK), lambda i, c, s: (0, i))
        at = lambda i, c, s: (0, near * (1 - c[0]) + i)
        kernel, out_specs, aliases = away_kernel, source, {}
        out_shape = jax.ShapeDtypeStruct(x.shape, bf16)
        scratch = []
    col = pl.BlockSpec((width, BLOCK), at)
    part = pl.BlockSpec((PER, BLOCK), at)
    return pl.pallas_call(
        without(kernel, 10 + len(gots), after),
        grid_spec=pltpu.PrefetchScalarGridSpec(
            num_scalar_prefetch=2,
            grid=(near,),
            in_specs=[source, source, col, part, part, part, full(wqkv_n.shape), full((width, 128))]
            + [full(got.shape) for got in gots[:2]] + [ANY] * (len(gots[2:]) + len(after)),
            out_specs=out_specs,
            scratch_shapes=scratch,
        ),
        out_shape=out_shape,
        input_output_aliases=aliases,
        compiler_params=pltpu.CompilerParams(vmem_limit_bytes=VMEM),
        name="input_backward",
        cost_estimate=cost(4),
    )(place, skip, x, cot, gh, *parts, wqkv_n, gain_one, *gots, *after)


def rotary_rows(rows):
    frequency = theta_base ** (-2.0 * np.arange(HD // 2, dtype=np.float64) / HD)
    angles = frequency[:, None] * np.arange(rows, dtype=np.float64)[None, :]
    return np.cos(angles).astype(np.float32), np.sin(angles).astype(np.float32)


def swap_core(array):
    return lax.ppermute(array, "narrow", [(0, 1), (1, 0)])


def axis_orders(bits, turn_index):
    if bits == 4:
        return (((0, 1, 2, 3), (1, 2, 3, 0)), ((1, 2, 0, 3), (2, 0, 1, 3)), ((0, 1, 2, 3), (1, 0, 2, 3)))[turn_index]
    base = tuple(range(bits))
    shift = bits // 2
    return base, base[shift:] + base[:shift]


class Summer:
    def __init__(self, core, chips, turn_index, exchanges):
        self.core = core
        self.chips = chips
        self.bits = chips.bit_length() - 1
        self.halvings = self.bits - exchanges
        self.orders = axis_orders(self.bits, turn_index)
        self.place = lax.axis_index("wide")
        self.stage = 0

    def bit(self, step):
        by_core = [(self.place >> order[step]) & 1 for order in self.orders]
        return jnp.where(self.core == 0, by_core[0], by_core[1])

    def swap(self, array, step):
        pairs = [
            (2 * chip + c, 2 * (chip ^ (1 << self.orders[c][step])) + c) for chip in range(self.chips) for c in range(2)
        ]
        return lax.ppermute(array, ("wide", "narrow"), pairs)

    def first(self, keep, send):
        self.keep, self.got = keep, swap_core(send)

    def advance(self, line):
        if line.last is not None:
            self.keep, self.got, _ = lax.optimization_barrier((self.keep, self.got, line.last))
        if self.stage < self.halvings:
            bit = self.bit(self.stage)
            half = self.keep.shape[0] // 2

            def part(which):
                a = lax.dynamic_slice_in_dim(self.keep, which * half, half, 0).astype(f32)
                b = lax.dynamic_slice_in_dim(self.got, which * half, half, 0).astype(f32)
                return (a + b).astype(bf16)

            line.last = part(1 - bit)
            self.keep, self.got = part(bit), self.swap(line.last, self.stage)
        elif self.stage <= self.bits:
            line.last = self.keep = (self.keep.astype(f32) + self.got.astype(f32)).astype(bf16)
            axis = self.stage if self.stage < self.bits else self.halvings - 1
            self.got = self.swap(self.keep, axis)
        else:
            step = self.halvings + self.bits - self.stage
            low = self.bit(step) == 0
            line.last = self.keep = jnp.where(
                low, jnp.concatenate([self.keep, self.got], 0), jnp.concatenate([self.got, self.keep], 0)
            )
            self.got = self.swap(self.keep, step - 1) if step else swap_core(self.keep)
        self.stage += 1

    @property
    def done(self):
        return self.stage > self.bits + self.halvings


class Line:
    last = None

    def after(self):
        return () if self.last is None else (self.last,)


def unpack_kernel(chain, place_ref, own_hbm, got_hbm, *refs):
    own, got, sem = refs[-3:]
    gate_ref, up_ref, down_ref = refs[-8:-5] if chain else refs[:3]
    step = pl.program_id(0)
    width = gate_ref.shape[0]
    copies = [
        pltpu.make_async_copy(source, target, sem.at[k]) for k, (source, target) in enumerate(((own_hbm, own), (got_hbm, got)))
    ]

    @pl.when(step == 0)
    def _():
        for copy in copies:
            copy.start()

    for k in range(2):
        pl.when((step == 0) & (place_ref[0] == k))(copies[k].wait)
        pl.when((step == 1) & (place_ref[0] != k))(copies[k].wait)

    def take(halves):
        for third in range(3):
            blocks = ((halves[0], 2), (halves[1], 2)) if third == 2 else ((halves[third], 0), (halves[third], 1))

            @pl.when(step == third)
            def _():
                for m, target in enumerate((gate_ref, up_ref, down_ref)):
                    for b, (source, place) in enumerate(blocks):
                        spot = (3 * m + place) * width
                        target[:, b * 128 : (b + 1) * 128] = source[spot : spot + width].astype(f32)

    pl.when(place_ref[0] == 0)(lambda: take((own, got)))
    pl.when(place_ref[0] != 0)(lambda: take((got, own)))

    if chain:
        w_out_ref, gain_ref = refs[-5:-3]

        def take_rest(first, second):
            spot = 9 * width
            unpack_thin(w_out_ref, first, second, spot)
            spot += width // 128 // 2 * width + width // 4
            rows = first[spot : spot + GAIN_ROWS].astype(f32)
            line = jnp.concatenate([rows[k : k + 1] for k in range(lanes_up(width) // 128)], 1)
            gain_ref[...] = line[:, :width].reshape(width)

        pl.when((step == 2) & (place_ref[0] == 0))(lambda: take_rest(own, got))
        pl.when((step == 2) & (place_ref[0] != 0))(lambda: take_rest(got, own))


def unpack(chain, place, buffers, width, inner, earlier):
    spec = pl.BlockSpec((width, BLOCK), lambda i, c: (0, 3 * chain + i))
    out_specs = [spec, spec, spec]
    out_shape = [jax.ShapeDtypeStruct((width, inner), f32)] * 3
    if chain:
        out_specs += [full((HQ * HD, width)), full((width,))]
        out_shape += [jax.ShapeDtypeStruct((HQ * HD, width), f32), jax.ShapeDtypeStruct((width,), f32)]
    return pl.pallas_call(
        functools.partial(unpack_kernel, chain),
        grid_spec=pltpu.PrefetchScalarGridSpec(
            num_scalar_prefetch=1,
            grid=(3,),
            in_specs=[ANY, pl.BlockSpec(memory_space=pltpu.HBM)] + [ANY] * len(earlier),
            out_specs=out_specs,
            scratch_shapes=[pltpu.VMEM(b.shape, bf16) for b in buffers] + [pltpu.SemaphoreType.DMA((2,))],
        ),
        out_shape=out_shape,
        input_output_aliases={3 + k: k for k in range(len(earlier))},
        compiler_params=pltpu.CompilerParams(vmem_limit_bytes=VMEM),
        name="unpack_mlp",
        cost_estimate=cost(4),
    )(place, *buffers, *earlier)


def unpack_last_kernel(place_ref, own_ref, got_ref, wqkv_ref, gain_one_ref, dq_ref, dkt_ref, dvt_ref, gain_ref, all_sc):
    q_cols = GROUPS * HD

    def take(first, second):
        for g in range(KVH):
            unpack_thin(all_sc.at[g * PER : (g + 1) * PER], first, second, g * PER * all_sc.shape[1] // 256)

    pl.when(place_ref[0] == 0)(lambda: take(own_ref, got_ref))
    pl.when(place_ref[0] != 0)(lambda: take(got_ref, own_ref))
    both = all_sc[...]
    dq = []
    for g in range(KVH):
        dq.append(both[g * PER : g * PER + q_cols])
        dkt_ref[g * HD : (g + 1) * HD] = both[g * PER + q_cols : g * PER + q_cols + HD]
        dvt_ref[g * HD : (g + 1) * HD] = both[g * PER + q_cols + HD : (g + 1) * PER]
    dq_ref[...] = jnp.concatenate(dq, 0).T
    gain = jnp.sum(both * wqkv_ref[...].astype(f32), 0, keepdims=True) / gain_one_ref[...]
    gain_ref[...] = gain.reshape(gain_ref.shape)


def unpack_last(place, own, got, wqkv_t, gain_one, after):
    width = wqkv_t.shape[1]
    shapes = [(width, HQ * HD), (KVH * HD, width), (KVH * HD, width), (width,)]
    return pl.pallas_call(
        without(unpack_last_kernel, 5, after),
        grid_spec=pltpu.PrefetchScalarGridSpec(
            num_scalar_prefetch=1,
            grid=(1,),
            in_specs=[full(own.shape)] * 2 + [full(wqkv_t.shape), full((1, width))] + [ANY] * len(after),
            out_specs=[full(shape) for shape in shapes],
            scratch_shapes=[pltpu.VMEM(wqkv_t.shape, f32)],
        ),
        out_shape=[jax.ShapeDtypeStruct(shape, f32) for shape in shapes],
        compiler_params=pltpu.CompilerParams(vmem_limit_bytes=VMEM),
        name="unpack_attention",
        cost_estimate=cost(3),
    )(place, own, got, wqkv_t, gain_one, *after)


def flip(array):
    return jnp.swapaxes(array, -1, -2)


def per_device(tokens, doc_starts, skip_flags, cotangent, attn_gain, wq, wk, wv, w_out, mlp_gain, wg, wu, wd):
    core = lax.axis_index("narrow")
    chips = lax.axis_size("wide")
    tokens, cotangent = flip(tokens), flip(cotangent)
    rows = 2 * tokens.shape[2]
    width = tokens.shape[1]
    inner = wg.shape[1]
    place = core.astype(jnp.int32).reshape(1)
    skip = skip_flags
    other = swap_core(lax.dynamic_index_in_dim(tokens, 1 - core, 0, keepdims=False))
    cot_other = swap_core(lax.dynamic_index_in_dim(cotangent, 1 - core, 0, keepdims=False))
    cos_t, sin_t = rotary_rows(rows)
    wdt = flip(wd)
    wqkv_t, wqkv_n, w_out_t, gain_one, gain_two, gain_line = prelude(wq, flip(wk), flip(wv), w_out, attn_gain, mlp_gain)
    unit = 16 * chips

    def half_rows(count):
        return -(-count // unit) * unit

    mlp_rows = 3 * width * inner // 4 // 128
    thin = width // 128 // 2
    out_rows = thin * HQ * HD + HQ * HD // 4 + GAIN_ROWS
    rest_rows = thin * KVH * PER + KVH * PER // 4

    (
        qt, kt, vn, soft, n1, res_own, res_away, gh, dot_t, delta, keep_a, send_a, keep_b, send_b,
    ) = layer(
        half_rows(mlp_rows), half_rows(mlp_rows + out_rows),
        place, skip, tokens, other, cotangent, cot_other, gain_one, wqkv_t, w_out_t, gain_two, cos_t, sin_t,
        doc_starts, w_out, wg, wu, wdt,
    )
    a_sum, b_sum, c_sum = (Summer(core, chips, k, exchanges) for k, exchanges in ((0, 0), (1, 0), (2, 2)))
    a_sum.first(keep_a, send_a)
    b_sum.first(keep_b, send_b)
    result_got = swap_core(res_away)
    line = Line()
    parts, packed = [], ()
    for g in range(KVH):
        part, *packed = back(
            g, half_rows(rest_rows), width, place, soft, qt, kt, vn, dot_t, delta, cos_t, sin_t, n1, packed, line.after()
        )
        parts.append(part)
        line.last = part
        if g == KVH - 1:
            c_sum.first(*packed)
        a_sum.advance(line)
        b_sum.advance(line)
    grad_away = last(False, place, skip, other, cot_other, gh, parts, wqkv_n, gain_one, (), line.after())
    line.last = grad_away
    for chain in (c_sum, a_sum, b_sum):
        chain.advance(line)
    grad_got = swap_core(grad_away)
    for chain in (c_sum, a_sum, b_sum):
        chain.advance(line)
    for chain in (c_sum, a_sum, b_sum, c_sum, a_sum, b_sum, c_sum, c_sum, a_sum, b_sum):
        chain.advance(line)
    c_sum.advance(line)
    grad_x, result = last(
        True, place, skip, tokens, cotangent, gh, parts, wqkv_n, gain_one, (grad_got, result_got, res_own), line.after()
    )
    line.last = grad_x
    for chain in (c_sum, a_sum):
        while not chain.done:
            chain.advance(line)
    dq, dkt, dvt, dgain_one = unpack_last(place, c_sum.keep, c_sum.got, wqkv_t, gain_line, line.after())
    line.last = dgain_one
    while not b_sum.done:
        b_sum.advance(line)
    first = unpack(0, place, (a_sum.keep, a_sum.got), width, inner, ())
    dwg, dwu, dwdt, dwo, dgain_two = unpack(1, place, (b_sum.keep, b_sum.got), width, inner, first)
    return (
        flip(result), flip(grad_x),
        dgain_one, dq, flip(dkt), flip(dvt), dwo, dgain_two, dwg, dwu, flip(dwdt),
    )


def solution(mesh):
    split = P("wide", "narrow", None)
    in_specs = (split, P("wide", None), P("wide"), split) + (P(),) * 9
    out_specs = (split, split) + (P(),) * 9
    return jax.shard_map(per_device, mesh=mesh, in_specs=in_specs, out_specs=out_specs, check_vma=False)
```
